128 devices in a mesh: dp: 8 (over y, x_hi), tensor: 16 (over z, x_lo, core).
Axes of the slice: x: 4 (x_hi: 2, x_lo: 2; x = x_hi * 2 + x_lo), y: 4, z: 4, core: 2. Of those that a mesh axis runs over, the one named last changes fastest.
Arguments:
- grad: bfloat16 [4096, 4096], P(('dp', 'tensor')), may hold values from -6 to 6
- left_basis: float32 [4096, 4096], P('dp', 'tensor'), may hold values from -0.09375 to 0.09375
- right_basis: float32 [4096, 4096], P('dp', 'tensor'), may hold values from -0.09375 to 0.09375
- first_moment: float32 [4096, 4096], P('dp', 'tensor'), may hold values from -3 to 3
- second_moment: float32 [4096, 4096], P('dp', 'tensor'), may hold values from 0.1 to 10
Outputs:
- update: float32 [4096, 4096], P(('dp', 'tensor'))
- new_first: float32 [4096, 4096], P('dp', 'tensor')
- new_second: float32 [4096, 4096], P('dp', 'tensor')
The draws below stay inside these ranges and needn't reach their ends.
All inputs are finite; a program needn't handle non-finite values.
Results may differ from the reference program's by a relative error of at most 0.0003.
Values may be sent and summed in bfloat16 or wider, within the bound.
A program may use at most 128 MiB of HBM per device.

```python
import math
import jax
import jax.numpy as jnp
from jax import lax

BS = 4096
STEP = 10


def level_of(own_key, extent, pieces, least, top_value):
    def one(dim, shards_of):
        steps = jax.random.uniform(jax.random.fold_in(jax.random.fold_in(own_key, 6), dim), (shards_of,), jnp.float32, least / len(pieces), top_value / len(pieces))
        return jnp.repeat(jnp.exp(steps), extent[dim] // shards_of).reshape((-1,) + (1,) * (len(extent) - dim - 1))

    gain = one(*pieces[0])
    for cut in pieces[1:]:
        gain = gain * one(*cut)
    return gain


def bell_draw(own_key, shape, width, most, split=(), dtype=jnp.bfloat16):
    factor_of = level_of(own_key, shape, split, -0.22, 0.18) if split else 1.0
    values = jax.random.normal(own_key, shape, jnp.float32) * width * factor_of
    return jnp.minimum(jnp.maximum(values, -most), most).astype(dtype)


def setup_inputs(seed: int = 0) -> dict:
    key_list = jax.random.split(jax.random.key(seed), 6)
    return {
        "grad": bell_draw(key_list[0], (BS, BS), 1.0, 6.0, ((0, 128),)),
        "left_basis": bell_draw(key_list[1], (BS, BS), BS ** -0.5, 0.09375, ((0, 8), (1, 16)), jnp.float32),
        "right_basis": bell_draw(key_list[2], (BS, BS), BS ** -0.5, 0.09375, ((0, 8), (1, 16)), jnp.float32),
        "first_moment": bell_draw(key_list[3], (BS, BS), 0.5, 3.0, ((0, 8), (1, 16)), jnp.float32),
        "second_moment": jnp.clip(jnp.exp(math.log(10.0) - 4.6051702 * jax.random.uniform(key_list[4], (BS, BS), jnp.float32) ** level_of(key_list[4], (BS, BS), ((0, 8), (1, 16)), -0.2, 0.2)), 0.1, 10.0),
    }


def reference(grad, left_basis, right_basis, first_moment, second_moment):
    highest = lax.Precision.HIGHEST
    widened = grad.astype(jnp.float32)
    half_turned = jnp.dot(left_basis.T, widened, precision=highest, preferred_element_type=jnp.float32)
    rotated = jnp.dot(half_turned, right_basis, precision=highest, preferred_element_type=jnp.float32)
    new_first = 0.9 * first_moment + 0.1 * rotated
    new_second = 0.95 * second_moment + 0.05 * rotated * rotated
    first_fix = 1.0 - 0.9 ** STEP
    second_fix = 1.0 - 0.95 ** STEP
    direction = new_first / first_fix / (jnp.sqrt(new_second / second_fix) + 1e-08)
    half_back = jnp.dot(direction, right_basis.T, precision=highest, preferred_element_type=jnp.float32)
    update = jnp.dot(left_basis, half_back, precision=highest, preferred_element_type=jnp.float32)
    return (update, new_first, new_second)
```

```python
import functools

import jax
import jax.numpy as jnp
from jax import lax
from jax.experimental import pallas as pl
from jax.experimental.pallas import tpu as pltpu
from jax.sharding import PartitionSpec as P

STEP = 10
F32 = jnp.float32
BF16 = jnp.bfloat16
MESH = pl.DeviceIdType.MESH

SPAN = 250.0
BASE = 124.0
BOUND = 0.09375


def encode(x, inverse):
    t = jnp.maximum(jnp.abs(x) * inverse, 1e-30)
    y = jnp.exp2((t * lax.rsqrt(t)) * SPAN - BASE)
    return jnp.where(x < 0, -y, y).astype(BF16)


def decode(code, scale):
    y = code.astype(F32)
    t = (jnp.log2(jnp.abs(y)) + BASE) * (1.0 / SPAN)
    v = t * t * scale
    return jnp.where(y < 0, -v, v)


def pack(get, message, rows, blocks):
    most = None
    for b in range(blocks):
        a = jnp.abs(get(b))
        most = a if most is None else jnp.maximum(most, a)
    most = jnp.max(jnp.max(most, axis=0, keepdims=True), axis=1, keepdims=True)
    scale16 = (jnp.broadcast_to(most, (16, 128)) * 1.01 + 1e-30).astype(BF16)
    message[pl.ds(blocks * rows, 16), :] = scale16
    inverse = 1.0 / scale16.astype(F32)[0:1, :]
    for b in range(blocks):
        message[pl.ds(b * rows, rows), :] = encode(get(b), inverse)


def unpack(message, b, rows, blocks):
    scale = message[pl.ds(blocks * rows, 16), :].astype(F32)[0:1, :]
    return decode(message[pl.ds(b * rows, rows), :], scale)


def halves(x):
    hi = x.astype(BF16)
    return hi, (x - hi.astype(F32)).astype(BF16)


def dot(a, b):
    return lax.dot_general(a, b, (((1,), (0,)), ((), ())), preferred_element_type=F32)


def dot_t(a, b):
    return lax.dot_general(a, b, (((1,), (1,)), ((), ())), preferred_element_type=F32)


def kernel(
    grad, left, right, first, second, update, new_first, new_second,
    left_out, left_in, lt, lf, grad_out, grad_in, right_out, right_in, right_hi, right_lo,
    h_out, h_in, h_gather_out, h_gather_in, h_block, h_parts,
    rot_out, rot_in, d_out, d_in, d_parts, y_block, y_out, y_in, y_gather_out, y_gather_in, y_hi, y_lo,
    u_block, u_out, u_in, u_last_out, u_last_in,
    ss, rs,
):
    dp = lax.axis_index("dp")
    tensor = lax.axis_index("tensor")
    y, xh = dp // 2, dp % 2
    z, xl, core = tensor // 4, (tensor // 2) % 2, tensor % 2
    x = xh * 2 + xl
    other = 1 - core

    def device(px, py, pz, pc):
        return (py * 2 + px // 2, pz * 4 + (px % 2) * 2 + pc)

    def turn(a, o):
        return (a + o) % 4

    sems = {}
    total = [0, 0]

    def bank(name, sends, receives):
        sems[name] = tuple(total)
        total[0] += sends
        total[1] += receives

    for name, sends, receives in (
        ("l1", 4, 4), ("lg", 4, 4), ("lc", 4, 4), ("g1", 8, 8), ("g2", 4, 4),
        ("r1", 4, 4), ("rg", 4, 4), ("rc", 4, 4), ("h1", 8, 8), ("h2", 4, 4),
        ("p", 16, 16), ("d", 16, 16), ("y1", 4, 4), ("y2", 8, 8), ("u1", 4, 4), ("u2", 8, 8),
    ):
        bank(name, sends, receives)

    pending = []

    def remote(name, i, j, src, dst, target):
        return pltpu.make_async_remote_copy(
            src_ref=src, dst_ref=dst, send_sem=ss.at[sems[name][0] + i], recv_sem=rs.at[sems[name][1] + j],
            device_id=device(*target), device_id_type=MESH,
        )

    def send(name, i, j, src, dst, target):
        copy = remote(name, i, j, src, dst, target)
        copy.start()
        pending.append(copy.wait_send)

    def send_unless(own, name, i, j, src, dst, target):
        here = pltpu.make_async_copy(src, dst, rs.at[sems[name][1] + j])
        there = remote(name, i, j, src, dst, target)
        pl.when(own)(here.start)
        pl.when(jnp.logical_not(own))(there.start)
        pending.append(lambda: pl.when(jnp.logical_not(own))(there.wait_send))

    def arrive(name, j, dst):
        pltpu.make_async_copy(dst, dst, rs.at[sems[name][1] + j]).wait()

    barrier = pltpu.get_barrier_semaphore()
    peers = [(x, turn(y, a), turn(z, b), core) for a in range(4) for b in range(4) if a or b]
    peers += [(turn(x, o), y, z, c) for o in range(4) for c in (core, other) if o or c is other]
    peers += [(x, y, turn(z, o), other) for o in (1, 2, 3)]
    for peer in peers:
        pl.semaphore_signal(barrier, inc=1, device_id=device(*peer), device_id_type=MESH)

    for b in range(4):
        left_out[b] = encode(left[pl.ds(b * 128, 128), :].T, 1.0 / BOUND)
    for px in range(4):
        for pc in range(2):
            for b in range(4):
                grad_out[px, pc, :, pl.ds(b * 128, 128)] = grad[:, pl.ds(pc * 2048 + b * 512 + px * 128, 128)]

    pl.semaphore_wait(barrier, len(peers))

    for o in (2, 1, 3, 0):
        to = turn(z, o)
        args = ("l1", o, y, left_out.at[to], left_in.at[x, core, y], (x, z, to, core))
        if o:
            send(*args)
        else:
            send_unless(y == z, *args)

    own_rows = pl.ds(pl.multiple_of(y * 256 + x * 64 + core * 32, 32), 32)
    for o in (2, 1, 3, 0):
        for oc, pc in ((1, other), (0, core)):
            if o or oc:
                px = turn(x, o)
                send("g1", o * 2 + oc, o * 2 + oc, grad_out.at[px, pc], grad_in.at[own_rows], (px, y, z, pc))
    grad_in[own_rows] = grad_out[x, core]

    for q in range(4):
        for b in range(2):
            right_out[q, pl.ds(b * 128, 128), :] = encode(
                right[pl.ds(q * 128, 128), pl.ds(b * 128, 128)], 1.0 / BOUND
            )
    for o in (2, 1, 3):
        px = turn(x, o)
        send("r1", o, o, right_out.at[px], right_in.at[y, core, x], (px, y, z, core))
    right_in[y, core, x] = right_out[x]

    for i in range(4):
        arrive("l1", i, left_in.at[x, core, i])
    for o in (2, 1, 3):
        piece = left_in.at[x, core]
        send("lg", o, o, piece, piece, (turn(x, o), y, z, core))
    send("lc", 0, 0, left_in.at[x, core], left_in.at[x, core], (x, y, z, other))

    for o in range(4):
        for oc, pc in ((1, other), (0, core)):
            if o or oc:
                px = turn(x, 4 - o)
                rows = pl.ds(pl.multiple_of(y * 256 + px * 64 + pc * 32, 32), 32)
                arrive("g1", o * 2 + oc, grad_in.at[rows])
    own_rows = pl.ds(pl.multiple_of(y * 256, 256), 256)
    for o in (2, 1, 3):
        send("g2", o, o, grad_in.at[own_rows], grad_in.at[own_rows], (x, turn(y, o), z, core))

    for o in (1, 2, 3):
        arrive("r1", o, right_in.at[y, core, turn(x, 4 - o)])
    for o in (2, 1, 3):
        piece = right_in.at[y, core]
        send("rg", o, o, piece, piece, (x, turn(y, o), z, core))
    send("rc", 0, 0, right_in.at[y, core], right_in.at[y, core], (x, y, z, other))

    def left_piece(px, pc):
        def one(ry, carry):
            for h in range(2):
                v = decode(left_in[px, pc, ry, pl.ds(h * 128, 128), :], BOUND)
                hi, lo = halves(v)
                chunk = (px % 2) * 4 + pc * 2 + h
                at = pl.ds(pl.multiple_of(ry * 256 + (px // 2) * 128, 128), 128)
                lt[chunk, pl.ds(0, 128), at] = hi
                lt[chunk, pl.ds(128, 128), at] = lo
            return carry

        lax.fori_loop(0, 4, one, 0)

    left_piece(x, core)
    for o in (1, 3, 2):
        px = turn(x, 4 - o)
        arrive("lg", o, left_in.at[px, core])
        send("lc", o, o, left_in.at[px, core], left_in.at[px, core], (x, y, z, other))
        left_piece(px, core)
    for o in (0, 1, 3, 2):
        px = turn(x, 4 - o)
        arrive("lc", o, left_in.at[px, other])
        left_piece(px, other)

    for o in (1, 2, 3):
        rows = pl.ds(pl.multiple_of(turn(y, 4 - o) * 256, 256), 256)
        arrive("g2", o, grad_in.at[rows])

    def turned(pz, pc, message):
        both = dot(lt[pc * 4 + pz], grad_in[...])
        h_block[:, pl.ds(0, 512)] = both[0:128] + both[128:256]
        pack(lambda b: h_block[:, pl.ds(b * 128, 128)], message, 128, 4)

    for o in (2, 1, 3):
        for oc, pc in ((1, other), (0, core)):
            pz = turn(z, o)
            turned(pz, pc, h_out.at[o * 2 + oc])
            send("h1", o * 2 + oc, o * 2 + oc, h_out.at[o * 2 + oc], h_in.at[z, core], (x, y, pz, pc))
    turned(z, other, h_out.at[1])
    send("h1", 1, 1, h_out.at[1], h_in.at[z, core], (x, y, z, other))
    turned(z, core, h_in.at[z, core])

    def right_piece(py, pc):
        def one(px, carry):
            for b in range(2):
                v = decode(right_in[py, pc, px, pl.ds(b * 128, 128), :], BOUND)
                hi, lo = halves(v)
                rows = pl.ds(pl.multiple_of(py * 256 + (px // 2) * 128, 128), 128)
                at = pl.ds(pl.multiple_of((px % 2) * 512 + pc * 256 + b * 128, 128), 128)
                right_hi[rows, at] = hi
                right_lo[rows, at] = lo
            return carry

        lax.fori_loop(0, 4, one, 0)

    right_piece(y, core)
    for o in (1, 3, 2):
        py = turn(y, 4 - o)
        arrive("rg", o, right_in.at[py, core])
        send("rc", o, o, right_in.at[py, core], right_in.at[py, core], (x, y, z, other))
        right_piece(py, core)
    for o in (0, 1, 3, 2):
        py = turn(y, 4 - o)
        arrive("rc", o, right_in.at[py, other])
        right_piece(py, other)

    for o in range(4):
        for oc, pc in ((1, other), (0, core)):
            if o or oc:
                arrive("h1", o * 2 + oc, h_in.at[turn(z, 4 - o), pc])

    def h_sum(i, carry):
        pc, b = i // 4, i % 4
        v = None
        for pz in range(4):
            message = h_in.at[pz, pc]
            scale = message[pl.ds(512, 16), :].astype(F32)[0:1, :]
            term = decode(message[pl.ds(pl.multiple_of(b * 128, 128), 128), :], scale)
            v = term if v is None else v + term
        h_block[:, pl.ds(pl.multiple_of(i * 128, 128), 128)] = v
        return carry

    lax.fori_loop(0, 8, h_sum, 0)
    pack(lambda b: h_block[:, pl.ds(b * 128, 128)], h_gather_out, 128, 8)
    for o in (2, 1, 3):
        send("h2", o, o, h_gather_out, h_gather_in.at[z], (x, y, turn(z, o), core))

    order = (0, 1, 3, 2)

    def rotate(o):
        pz = turn(z, o)
        if o == 0:
            for b in range(8):
                hi, lo = halves(h_block[:, pl.ds(b * 128, 128)])
                h_parts[pl.ds(0, 128), pl.ds(b * 128, 128)] = hi
                h_parts[pl.ds(128, 128), pl.ds(b * 128, 128)] = lo
        else:
            arrive("h2", 4 - o, h_gather_in.at[pz])
            for b in range(8):
                hi, lo = halves(unpack(h_gather_in.at[pz], b, 128, 8))
                h_parts[pl.ds(0, 128), pl.ds(b * 128, 128)] = hi
                h_parts[pl.ds(128, 128), pl.ds(b * 128, 128)] = lo
        for i in (1, 2, 3, 0):
            jd = turn(xl * 2 + core, i)
            at = pl.ds(pl.multiple_of(jd * 256, 256), 256)
            both = dot(h_parts[...], right_hi[:, at])
            rot = both[0:128] + both[128:256] + dot(h_parts[pl.ds(0, 128), :], right_lo[:, at])
            pack(lambda b, rot=rot: rot[:, b * 128 : (b + 1) * 128], rot_out.at[o, i], 128, 2)
            target = (core * 2 + jd // 2, y, z, jd % 2)
            args = ("p", o * 4 + i, o * 4 + x, rot_out.at[o, i], rot_in.at[o, x], target)
            if i:
                send(*args)
            else:
                send_unless(xh == core, *args)

    def moments(o):
        for px in range(4):
            arrive("p", o * 4 + px, rot_in.at[o, px])
        rows = pl.ds(pl.multiple_of(turn(z, o) * 128, 128), 128)
        direction = []
        for b in range(2):
            rot = None
            for px in range(4):
                term = unpack(rot_in.at[o, px], b, 128, 2)
                rot = term if rot is None else rot + term
            at = pl.ds(b * 128, 128)
            moved_first = 0.9 * first[rows, at] + 0.1 * rot
            moved_second = 0.95 * second[rows, at] + 0.05 * rot * rot
            new_first[rows, at] = moved_first
            new_second[rows, at] = moved_second
            direction.append(
                moved_first / (1.0 - 0.9**STEP) / (jnp.sqrt(moved_second / (1.0 - 0.95**STEP)) + 1e-08)
            )
        pack(lambda b: direction[b], d_out.at[o], 128, 2)
        for i in (2, 1, 3, 0):
            args = ("d", o * 4 + i, o * 4 + xl * 2 + core, d_out.at[o], d_in.at[o, xl * 2 + core], (turn(x, i), y, z, xh))
            if i:
                send(*args)
            else:
                send_unless(xh == core, *args)

    def back(o):
        for j in range(4):
            arrive("d", o * 4 + j, d_in.at[o, j])
            for b in range(2):
                hi, lo = halves(unpack(d_in.at[o, j], b, 128, 2))
                at = pl.ds(j * 256 + b * 128, 128)
                d_parts[pl.ds(0, 128), at] = hi
                d_parts[pl.ds(128, 128), at] = lo

        def tile(i, carry):
            at = pl.ds(pl.multiple_of(i * 256, 256), 256)
            both = dot_t(d_parts[...], right_hi[at, :])
            v = both[0:128] + both[128:256] + dot_t(d_parts[pl.ds(0, 128), :], right_lo[at, :])
            y_block[:, at] = v
            return carry

        lax.fori_loop(0, 4, tile, 0)
        pz = turn(z, o)
        message = y_out.at[o] if o else y_in.at[z]
        pack(lambda b: y_block[:, pl.ds(b * 128, 128)], message, 128, 8)
        if o:
            send("y1", o, o, message, y_in.at[z], (x, y, pz, core))

    rotate(order[0])
    rotate(order[1])
    moments(order[0])
    rotate(order[2])
    moments(order[1])
    back(order[0])
    rotate(order[3])
    moments(order[2])
    back(order[1])
    moments(order[3])
    back(order[2])
    back(order[3])

    def flip(i, carry):
        chunk, s = i // 8, i % 8
        at = pl.ds(pl.multiple_of(s * 128, 128), 128)
        to = pl.ds(pl.multiple_of(chunk * 128, 128), 128)
        for part in range(2):
            v = lt[chunk, pl.ds(part * 128, 128), at].astype(F32).T.astype(BF16)
            lf[s // 2, pl.ds(pl.multiple_of(part * 256 + (s % 2) * 128, 128), 128), to] = v
        return carry

    lax.fori_loop(0, 64, flip, 0)

    for o in (1, 2, 3):
        arrive("y1", o, y_in.at[turn(z, 4 - o)])

    def y_sum(b, carry):
        v = None
        for pz in range(4):
            message = y_in.at[pz]
            scale = message[pl.ds(1024, 16), :].astype(F32)[0:1, :]
            term = decode(message[pl.ds(pl.multiple_of(b * 128, 128), 128), :], scale)
            v = term if v is None else v + term
        y_block[:, pl.ds(pl.multiple_of(b * 128, 128), 128)] = v
        return carry

    lax.fori_loop(0, 8, y_sum, 0)
    for half in range(2):
        pack(lambda b, half=half: y_block[:, pl.ds(half * 512 + b * 128, 128)], y_gather_out.at[half], 128, 4)
    for o in (2, 1, 3, 0):
        for oc, pc in ((1, other), (0, core)):
            if o or oc:
                send("y2", o * 2 + oc, o * 2 + oc, y_gather_out.at[pc], y_gather_in.at[core, z], (x, y, turn(z, o), pc))
    y_gather_in[core, z] = y_gather_out[core]

    def y_piece(pc, pz):
        rows = pl.ds(pl.multiple_of(pc * 512 + pz * 128, 128), 128)
        for b in range(4):
            hi, lo = halves(unpack(y_gather_in.at[pc, pz], b, 128, 4))
            y_hi[rows, pl.ds(b * 128, 128)] = hi
            y_lo[rows, pl.ds(b * 128, 128)] = lo

    y_piece(core, z)
    for o in (0, 1, 3, 2):
        for oc, pc in ((1, other), (0, core)):
            if o or oc:
                pz = turn(z, 4 - o)
                arrive("y2", o * 2 + oc, y_gather_in.at[pc, pz])
                y_piece(pc, pz)

    def raised(py, message):
        both = dot(lf[py], y_hi[...])
        u_block[...] = both[0:256] + both[256:512]
        u_block[...] += dot(lf[py, pl.ds(0, 256), :], y_lo[...])
        pack(lambda b: u_block[:, pl.ds(b * 128, 128)], message, 256, 4)

    for o in (2, 1, 3):
        py = turn(y, o)
        raised(py, u_out.at[o])
        send("u1", o, o, u_out.at[o], u_in.at[y], (x, py, z, core))
    raised(y, u_in.at[y])
    for o in (1, 2, 3):
        arrive("u1", o, u_in.at[turn(y, 4 - o)])

    def u_sum(b, carry):
        v = None
        for py in range(4):
            message = u_in.at[py]
            scale = message[pl.ds(1024, 16), :].astype(F32)[0:1, :]
            term = decode(message[pl.ds(pl.multiple_of(b * 256, 256), 256), :], scale)
            v = term if v is None else v + term
        u_block[:, pl.ds(pl.multiple_of(b * 128, 128), 128)] = v
        return carry

    lax.fori_loop(0, 4, u_sum, 0)
    for px in range(4):
        for pc in range(2):
            rows = pl.ds(px * 64 + pc * 32, 32)
            pack(lambda b, rows=rows: u_block[rows, pl.ds(b * 128, 128)], u_last_out.at[px, pc], 32, 4)
    for o in (2, 1, 3, 0):
        for oc, pc in ((1, other), (0, core)):
            if o or oc:
                px = turn(x, o)
                send("u2", o * 2 + oc, o * 2 + oc, u_last_out.at[px, pc], u_last_in.at[x, core], (px, y, z, pc))
    u_last_in[x, core] = u_last_out[x, core]
    for o in range(4):
        for oc, pc in ((1, other), (0, core)):
            if o or oc:
                arrive("u2", o * 2 + oc, u_last_in.at[turn(x, 4 - o), pc])
    for px in range(4):
        for pc in range(2):
            for b in range(4):
                update[:, pl.ds(pc * 2048 + b * 512 + px * 128, 128)] = unpack(u_last_in.at[px, pc], b, 32, 4)

    for wait in pending:
        wait()


def body(grad, left_basis, right_basis, first_moment, second_moment):
    vm = pltpu.VMEM
    scratch = [
        vm((4, 256, 128), BF16),
        vm((4, 2, 4, 256, 128), BF16),
        vm((8, 256, 1024), BF16),
        vm((4, 512, 1024), BF16),
        vm((4, 2, 32, 512), BF16),
        vm((1024, 512), BF16),
        vm((4, 256, 128), BF16),
        vm((4, 2, 4, 256, 128), BF16),
        vm((1024, 1024), BF16),
        vm((1024, 1024), BF16),
        vm((8, 528, 128), BF16),
        vm((4, 2, 528, 128), BF16),
        vm((1040, 128), BF16),
        vm((4, 1040, 128), BF16),
        vm((128, 1024), F32),
        vm((256, 1024), BF16),
        vm((4, 4, 272, 128), BF16),
        vm((4, 4, 272, 128), BF16),
        vm((4, 272, 128), BF16),
        vm((4, 4, 272, 128), BF16),
        vm((256, 1024), BF16),
        vm((128, 1024), F32),
        vm((4, 1040, 128), BF16),
        vm((4, 1040, 128), BF16),
        vm((2, 528, 128), BF16),
        vm((2, 4, 528, 128), BF16),
        vm((1024, 512), BF16),
        vm((1024, 512), BF16),
        vm((256, 512), F32),
        vm((4, 1040, 128), BF16),
        vm((4, 1040, 128), BF16),
        vm((4, 2, 144, 128), BF16),
        vm((4, 2, 144, 128), BF16),
        pltpu.SemaphoreType.DMA((104,)),
        pltpu.SemaphoreType.DMA((104,)),
    ]
    whole = pl.BlockSpec(memory_space=pltpu.VMEM)
    return pl.pallas_call(
        kernel,
        out_shape=(
            jax.ShapeDtypeStruct((32, 4096), F32),
            jax.ShapeDtypeStruct((512, 256), F32),
            jax.ShapeDtypeStruct((512, 256), F32),
        ),
        in_specs=[whole] * 5,
        out_specs=(whole,) * 3,
        scratch_shapes=scratch,
        compiler_params=pltpu.CompilerParams(
            collective_id=0, has_side_effects=True, vmem_limit_bytes=56 * 2**20
        ),
    )(grad, left_basis, right_basis, first_moment, second_moment)


def solution(mesh):
    placed = (
        P(("dp", "tensor"), None),
        P("dp", "tensor"),
        P("dp", "tensor"),
        P("dp", "tensor"),
        P("dp", "tensor"),
    )
    return jax.shard_map(
        body,
        mesh=mesh,
        in_specs=placed,
        out_specs=(P(("dp", "tensor"), None), P("dp", "tensor"), P("dp", "tensor")),
        check_vma=False,
    )
```

```python
import jax
import jax.numpy as jnp
from jax import lax
from jax.experimental import pallas as pl
from jax.experimental.pallas import tpu as pltpu
from jax.sharding import PartitionSpec as P

STEP = 10
F32 = jnp.float32
BF16 = jnp.bfloat16
MESH = pl.DeviceIdType.MESH

SPAN = 250.0
BASE = 124.0
BOUND = 0.09375


def encode(x, inverse):
    t = jnp.maximum(jnp.abs(x) * inverse, 1e-30)
    y = jnp.exp2((t * lax.rsqrt(t)) * SPAN - BASE)
    return jnp.where(x < 0, -y, y).astype(BF16)


def decode(code, scale):
    y = code.astype(F32)
    t = (jnp.log2(jnp.abs(y)) + BASE) * (1.0 / SPAN)
    v = t * t * scale
    return jnp.where(y < 0, -v, v)


def pack(get, message, rows, blocks):
    most = None
    for b in range(blocks):
        a = jnp.abs(get(b))
        most = a if most is None else jnp.maximum(most, a)
    most = jnp.max(jnp.max(most, axis=0, keepdims=True), axis=1, keepdims=True)
    scale16 = (jnp.broadcast_to(most, (16, 128)) * 1.01 + 1e-30).astype(BF16)
    message[pl.ds(blocks * rows, 16), :] = scale16
    inverse = 1.0 / scale16.astype(F32)[0:1, :]
    for b in range(blocks):
        message[pl.ds(b * rows, rows), :] = encode(get(b), inverse)


def unpack(message, b, rows, blocks):
    scale = message[pl.ds(blocks * rows, 16), :].astype(F32)[0:1, :]
    return decode(message[pl.ds(b * rows, rows), :], scale)


def halves(x):
    hi = x.astype(BF16)
    return hi, (x - hi.astype(F32)).astype(BF16)


def dot(a, b):
    return lax.dot_general(a, b, (((1,), (0,)), ((), ())), preferred_element_type=F32)


def dot_t(a, b):
    return lax.dot_general(a, b, (((1,), (1,)), ((), ())), preferred_element_type=F32)


NC = 2
RC = 128 // NC


def kernel(
    grad, left, right, first, second, update, new_first, new_second,
    left_out, left_mid, left_in, lt, lf, grad_out, grad_in, right_out, right_in, right_hi, right_lo,
    h_out, h_in, h_gather, h_part, h_block, h_parts, rot_out, rot_in, d_block, d_out, d_in, d_parts,
    y_block, y_sum, y_out, y_in, y_gather_out, y_gather, y_hi, y_lo, u_acc, u_out, u_in, u_last_out, u_last_in,
    ss, rs,
):
    dp = lax.axis_index("dp")
    tensor = lax.axis_index("tensor")
    y, xh = dp // 2, dp % 2
    z, xl, core = tensor // 4, (tensor // 2) % 2, tensor % 2
    x = xh * 2 + xl
    other = 1 - core

    def device(px, py, pz, pc):
        return (py * 2 + px // 2, pz * 4 + (px % 2) * 2 + pc)

    def turn(a, o):
        return (a + o) % 4

    first_sem = {}
    total = 0
    for name, count in SEMAPHORES:
        first_sem[name] = total
        total += count

    pending = []

    def remote(name, i, j, src, dst, target):
        return pltpu.make_async_remote_copy(
            src_ref=src, dst_ref=dst, send_sem=ss.at[first_sem[name] + i], recv_sem=rs.at[first_sem[name] + j],
            device_id=device(*target), device_id_type=MESH,
        )

    def send(name, i, src, dst, target, j=None):
        copy = remote(name, i, i if j is None else j, src, dst, target)
        copy.start()
        pending.append(copy.wait_send)

    def send_unless(own, name, i, src, dst, target, j):
        here = pltpu.make_async_copy(src, dst, rs.at[first_sem[name] + j])
        there = remote(name, i, j, src, dst, target)
        pl.when(own)(here.start)
        pl.when(jnp.logical_not(own))(there.start)
        pending.append(lambda: pl.when(jnp.logical_not(own))(there.wait_send))

    def arrive(name, j, dst):
        pltpu.make_async_copy(dst, dst, rs.at[first_sem[name] + j]).wait()

    def both_cores(o):
        return [(oc, pc) for oc, pc in ((1, other), (0, core)) if o or oc]

    barrier = pltpu.get_barrier_semaphore()
    peers = [(turn(x, o), y, z, pc) for o in range(4) for _, pc in both_cores(o)]
    peers += [(x, y, turn(z, o), pc) for o in (1, 2, 3) for _, pc in both_cores(o)]
    peers += [(x, turn(y, o), z, core) for o in (1, 2, 3)]
    for peer in peers:
        pl.semaphore_signal(barrier, inc=1, device_id=device(*peer), device_id_type=MESH)

    for b in range(4):
        code = encode(left[pl.ds(b * 128, 128), :].T, 1.0 / BOUND)
        for a in range(NC):
            for h in range(2):
                left_out[a, b, pl.ds(h * RC, RC), :] = code[h * 128 + a * RC : h * 128 + (a + 1) * RC]
    for px in range(4):
        for pc in range(2):
            for b in range(4):
                grad_out[px, pc, :, pl.ds(b * 128, 128)] = grad[:, pl.ds(pc * 2048 + b * 512 + px * 128, 128)]

    pl.semaphore_wait(barrier, len(peers))

    for a in range(NC):
        for o in (2, 1, 3):
            send("lz", a * 4 + o, left_out.at[a, turn(z, o)], left_mid.at[a, z], (x, y, turn(z, o), core))
        left_mid[a, z] = left_out[a, z]
    own_rows = pl.ds(pl.multiple_of(y * 256 + x * 64 + core * 32, 32), 32)
    for o in (2, 1, 3, 0):
        for oc, pc in both_cores(o):
            px = turn(x, o)
            send("g1", o * 2 + oc, grad_out.at[px, pc], grad_in.at[own_rows], (px, y, z, pc))
    grad_in[own_rows] = grad_out[x, core]
    for q in range(4):
        for b in range(2):
            right_out[q, pl.ds(b * 128, 128), :] = encode(
                right[pl.ds(q * 128, 128), pl.ds(b * 128, 128)], 1.0 / BOUND
            )
    for o in (2, 1, 3):
        px = turn(x, o)
        send("r1", o, right_out.at[px], right_in.at[y, core, x], (px, y, z, core))
    right_in[y, core, x] = right_out[x]

    for a in range(NC):
        for o in (1, 2, 3):
            arrive("lz", a * 4 + o, left_mid.at[a, turn(z, 4 - o)])
        for o in (2, 1, 3):
            to = turn(y, o)
            send("ly", a * 4 + o, left_mid.at[a, to], left_in.at[a, x, core, y], (x, to, z, core))
        left_in[a, x, core, y] = left_mid[a, y]

    def left_spread(a):
        for o in (1, 2, 3):
            arrive("ly", a * 4 + o, left_in.at[a, x, core, turn(y, 4 - o)])
        piece = left_in.at[a, x, core]
        for o in (2, 1, 3):
            send("lg", a * 4 + o, piece, piece, (turn(x, o), y, z, core))
        send("lc", a * 4, piece, piece, (x, y, z, other))

    def left_piece(a, px, pc):
        def one(ry, carry):
            hi, lo = halves(decode(left_in[a, px, pc, ry], BOUND))
            at = pl.ds(pl.multiple_of(ry * 256 + (px // 2) * 128, 128), 128)
            for h in range(2):
                rows = (pc * 2 + h) * RC
                lt[a, px % 2, pl.ds(pl.multiple_of(rows, RC), RC), at] = hi[h * RC : (h + 1) * RC]
                lt[a, px % 2, pl.ds(pl.multiple_of(4 * RC + rows, RC), RC), at] = lo[h * RC : (h + 1) * RC]
            return carry

        lax.fori_loop(0, 4, one, 0)

    def left_forward(a):
        for o in (1, 3, 2):
            piece = left_in.at[a, turn(x, 4 - o), core]
            arrive("lg", a * 4 + o, piece)
            send("lc", a * 4 + o, piece, piece, (x, y, z, other))

    def left_take(a):
        for o in (0, 1, 3, 2):
            left_piece(a, turn(x, 4 - o), core)
        for o in (0, 1, 3, 2):
            px = turn(x, 4 - o)
            arrive("lc", a * 4 + o, left_in.at[a, px, other])
            left_piece(a, px, other)

    left_spread(0)
    for o in range(4):
        for oc, pc in both_cores(o):
            rows = pl.ds(pl.multiple_of(y * 256 + turn(x, 4 - o) * 64 + pc * 32, 32), 32)
            arrive("g1", o * 2 + oc, grad_in.at[rows])
    own_rows = pl.ds(pl.multiple_of(y * 256, 256), 256)
    for o in (2, 1, 3):
        send("g2", o, grad_in.at[own_rows], grad_in.at[own_rows], (x, turn(y, o), z, core))
    left_forward(0)
    left_spread(1)
    left_take(0)
    for o in (1, 2, 3):
        rows = pl.ds(pl.multiple_of(turn(y, 4 - o) * 256, 256), 256)
        arrive("g2", o, grad_in.at[rows])
    for o in (1, 2, 3):
        arrive("r1", o, right_in.at[y, core, turn(x, 4 - o)])
    piece = right_in.at[y, core]
    for o in (2, 1, 3):
        send("rg", o, piece, piece, (x, turn(y, o), z, core))
    send("rc", 0, piece, piece, (x, y, z, other))

    def turned(a):
        for oc, pc in ((1, other), (0, core)):
            both = dot(lt[a, pc], grad_in[...])
            h_block[...] = both[0 : 4 * RC] + both[4 * RC : 8 * RC]
            for o in (2, 1, 3, 0):
                pz = turn(z, o)
                rows = pl.ds(pl.multiple_of(pz * RC, RC), RC)
                message = h_out.at[a, o, oc] if o or oc else h_in.at[a, z, core]
                pack(lambda b, rows=rows: h_block[rows, pl.ds(b * 128, 128)], message, RC, 4)
                if o or oc:
                    send("h1", (a * 4 + o) * 2 + oc, message, h_in.at[a, z, core], (x, y, pz, pc))

    def turned_sum(a):
        for o in range(4):
            for oc, pc in both_cores(o):
                arrive("h1", (a * 4 + o) * 2 + oc, h_in.at[a, turn(z, 4 - o), pc])

        def one(b, carry):
            for pc in range(2):
                v = None
                for pz in range(4):
                    message = h_in.at[a, pz, pc]
                    scale = message[pl.ds(4 * RC, 16), :].astype(F32)[0:1, :]
                    term = decode(message[pl.ds(pl.multiple_of(b * RC, RC), RC), :], scale)
                    v = term if v is None else v + term
                h_part[:, pl.ds(pl.multiple_of(pc * 512 + b * 128, 128), 128)] = v
            return carry

        lax.fori_loop(0, 4, one, 0)
        message = h_gather.at[a, z]
        pack(lambda b: h_part[:, pl.ds(b * 128, 128)], message, RC, 8)
        for o in (2, 1, 3):
            send("h2", a * 4 + o, message, message, (x, y, turn(z, o), core))

    def rotate(a):
        for o in (1, 2, 3):
            arrive("h2", a * 4 + o, h_gather.at[a, turn(z, 4 - o)])

        def one(pz, carry):
            for b in range(8):
                hi, lo = halves(unpack(h_gather.at[a, pz], b, RC, 8))
                h_parts[pl.ds(pl.multiple_of(pz * RC, RC), RC), pl.ds(b * 128, 128)] = hi
                h_parts[pl.ds(pl.multiple_of((4 + pz) * RC, RC), RC), pl.ds(b * 128, 128)] = lo
            return carry

        lax.fori_loop(0, 4, one, 0)
        for i in (1, 2, 3, 0):
            jd = turn(xl * 2 + core, i)
            at = pl.ds(pl.multiple_of(jd * 256, 256), 256)
            both = dot(h_parts[...], right_hi[:, at])
            rot = both[0 : 4 * RC] + both[4 * RC : 8 * RC] + dot(h_parts[pl.ds(0, 4 * RC), :], right_lo[:, at])
            pack(lambda b, rot=rot: rot[:, b * 128 : (b + 1) * 128], rot_out.at[a, i], 4 * RC, 2)
            target = (core * 2 + jd // 2, y, z, jd % 2)
            args = ("p", a * 4 + i, rot_out.at[a, i], rot_in.at[a, x], target, a * 4 + x)
            if i:
                send(*args)
            else:
                send_unless(xh == core, *args)

    def moments(a):
        for px in range(4):
            arrive("p", a * 4 + px, rot_in.at[a, px])

        def one(pz, carry):
            rows = pl.ds(pl.multiple_of(pz * 128 + a * RC, RC), RC)
            part = pl.ds(pl.multiple_of(pz * RC, RC), RC)
            for b in range(2):
                rot = None
                for px in range(4):
                    message = rot_in.at[a, px]
                    scale = message[pl.ds(8 * RC, 16), :].astype(F32)[0:1, :]
                    term = decode(message[pl.ds(pl.multiple_of((b * 4 + pz) * RC, RC), RC), :], scale)
                    rot = term if rot is None else rot + term
                at = pl.ds(b * 128, 128)
                moved_first = 0.9 * first[rows, at] + 0.1 * rot
                moved_second = 0.95 * second[rows, at] + 0.05 * rot * rot
                new_first[rows, at] = moved_first
                new_second[rows, at] = moved_second
                d_block[part, at] = (
                    moved_first / (1.0 - 0.9**STEP) / (jnp.sqrt(moved_second / (1.0 - 0.95**STEP)) + 1e-08)
                )
            return carry

        lax.fori_loop(0, 4, one, 0)
        pack(lambda b: d_block[:, pl.ds(b * 128, 128)], d_out.at[a], 4 * RC, 2)
        slot = xl * 2 + core
        for i in (2, 1, 3, 0):
            args = ("d", a * 4 + i, d_out.at[a], d_in.at[a, slot], (turn(x, i), y, z, xh), a * 4 + slot)
            if i:
                send(*args)
            else:
                send_unless(xh == core, *args)

    def back(a):
        for j in range(4):
            arrive("d", a * 4 + j, d_in.at[a, j])
            for b in range(2):
                hi, lo = halves(unpack(d_in.at[a, j], b, 4 * RC, 2))
                at = pl.ds(j * 256 + b * 128, 128)
                d_parts[pl.ds(0, 4 * RC), at] = hi
                d_parts[pl.ds(4 * RC, 4 * RC), at] = lo

        def tile(i, carry):
            at = pl.ds(pl.multiple_of(i * 256, 256), 256)
            both = dot_t(d_parts[...], right_hi[at, :])
            low = dot_t(d_parts[pl.ds(0, 4 * RC), :], right_lo[at, :])
            y_block[:, at] = both[0 : 4 * RC] + both[4 * RC : 8 * RC] + low
            return carry

        lax.fori_loop(0, 4, tile, 0)
        for o in (2, 1, 3, 0):
            pz = turn(z, o)
            rows = pl.ds(pl.multiple_of(pz * RC, RC), RC)
            message = y_out.at[a, o] if o else y_in.at[a, z]
            pack(lambda b, rows=rows: y_block[rows, pl.ds(b * 128, 128)], message, RC, 8)
            if o:
                send("y1", a * 4 + o, message, y_in.at[a, z], (x, y, pz, core))

    def back_sum(a):
        for o in (1, 2, 3):
            arrive("y1", a * 4 + o, y_in.at[a, turn(z, 4 - o)])

        def one(b, carry):
            v = None
            for pz in range(4):
                message = y_in.at[a, pz]
                scale = message[pl.ds(8 * RC, 16), :].astype(F32)[0:1, :]
                term = decode(message[pl.ds(pl.multiple_of(b * RC, RC), RC), :], scale)
                v = term if v is None else v + term
            y_sum[:, pl.ds(pl.multiple_of(b * 128, 128), 128)] = v
            return carry

        lax.fori_loop(0, 8, one, 0)
        for oc, pc in ((1, other), (0, core)):
            message = y_gather_out.at[a] if oc else y_gather.at[a, core, z]
            pack(
                lambda b, pc=pc: y_sum[:, pl.ds(pl.multiple_of(pc * 512 + b * 128, 128), 128)], message, RC, 4
            )
            for o in (2, 1, 3, 0):
                if o or oc:
                    send("y2", (a * 4 + o) * 2 + oc, message, y_gather.at[a, core, z], (x, y, turn(z, o), pc))

    def flip(a):
        def one(i, carry):
            pc, s = i // 8, i % 8
            at = pl.ds(pl.multiple_of(s * 128, 128), 128)
            for part in range(2):
                for sub in range(4 * RC // 128):
                    rows = pl.ds(part * 4 * RC + sub * 128, 128)
                    v = lt[a, pc, rows, at].astype(F32).T.astype(BF16)
                    to = pl.ds(pl.multiple_of(part * 256 + (s % 2) * 128, 128), 128)
                    lf[a, s // 2, to, pl.ds(pl.multiple_of(pc * 4 * RC + sub * 128, 128), 128)] = v
            return carry

        lax.fori_loop(0, 16, one, 0)

    def raised_take(a):
        for o in range(4):
            for oc, pc in both_cores(o):
                arrive("y2", (a * 4 + o) * 2 + oc, y_gather.at[a, pc, turn(z, 4 - o)])

        def one(i, carry):
            rows = pl.ds(pl.multiple_of(i * RC, RC), RC)
            for b in range(4):
                hi, lo = halves(unpack(y_gather.at[a, i // 4, i % 4], b, RC, 4))
                y_hi[rows, pl.ds(b * 128, 128)] = hi
                y_lo[rows, pl.ds(b * 128, 128)] = lo
            return carry

        lax.fori_loop(0, 8, one, 0)

    def raised(a, py):
        both = dot(lf[a, py], y_hi[...])
        v = both[0:256] + both[256:512] + dot(lf[a, py, pl.ds(0, 256), :], y_lo[...])
        u_acc[py] = u_acc[py] + v if a else v

    turned(0)
    for a in range(1, NC):
        left_forward(a)
        if a + 1 < NC:
            left_spread(a + 1)
        left_take(a)
        turned(a)
    flip(0)
    turned_sum(0)

    def right_piece(py, pc):
        def one(px, carry):
            for b in range(2):
                hi, lo = halves(decode(right_in[py, pc, px, pl.ds(b * 128, 128), :], BOUND))
                rows = pl.ds(pl.multiple_of(py * 256 + (px // 2) * 128, 128), 128)
                at = pl.ds(pl.multiple_of((px % 2) * 512 + pc * 256 + b * 128, 128), 128)
                right_hi[rows, at] = hi
                right_lo[rows, at] = lo
            return carry

        lax.fori_loop(0, 4, one, 0)

    for o in (1, 3, 2):
        piece = right_in.at[turn(y, 4 - o), core]
        arrive("rg", o, piece)
        send("rc", o, piece, piece, (x, y, z, other))
    for o in (0, 1, 3, 2):
        right_piece(turn(y, 4 - o), core)
    for o in (0, 1, 3, 2):
        py = turn(y, 4 - o)
        arrive("rc", o, right_in.at[py, other])
        right_piece(py, other)

    for a in range(1, NC):
        turned_sum(a)
    for a in range(NC):
        rotate(a)
        if a + 1 < NC:
            flip(a + 1)
    for a in range(NC):
        moments(a)
    for a in range(NC):
        back(a)
    for a in range(NC):
        back_sum(a)
    for a in range(NC - 1):
        raised_take(a)

        def one(py, carry, a=a):
            raised(a, py)
            return carry

        lax.fori_loop(0, 4, one, 0)

    raised_take(NC - 1)
    for o in (2, 1, 3, 0):
        py = turn(y, o)
        raised(NC - 1, py)
        message = u_out.at[o] if o else u_in.at[y]
        pack(lambda b, py=py: u_acc[py, :, pl.ds(b * 128, 128)], message, 256, 4)
        if o:
            send("u1", o, message, u_in.at[y], (x, py, z, core))
    for o in (1, 2, 3):
        arrive("u1", o, u_in.at[turn(y, 4 - o)])

    def raised_sum(b, carry):
        v = None
        for py in range(4):
            message = u_in.at[py]
            scale = message[pl.ds(1024, 16), :].astype(F32)[0:1, :]
            term = decode(message[pl.ds(pl.multiple_of(b * 256, 256), 256), :], scale)
            v = term if v is None else v + term
        u_acc[0, :, pl.ds(pl.multiple_of(b * 128, 128), 128)] = v
        return carry

    lax.fori_loop(0, 4, raised_sum, 0)
    for px in range(4):
        for pc in range(2):
            rows = pl.ds(px * 64 + pc * 32, 32)
            pack(lambda b, rows=rows: u_acc[0, rows, pl.ds(b * 128, 128)], u_last_out.at[px, pc], 32, 4)
    for o in (2, 1, 3, 0):
        for oc, pc in both_cores(o):
            px = turn(x, o)
            send("u2", o * 2 + oc, u_last_out.at[px, pc], u_last_in.at[x, core], (px, y, z, pc))
    u_last_in[x, core] = u_last_out[x, core]
    for o in range(4):
        for oc, pc in both_cores(o):
            arrive("u2", o * 2 + oc, u_last_in.at[turn(x, 4 - o), pc])
    for px in range(4):
        for pc in range(2):
            for b in range(4):
                update[:, pl.ds(pc * 2048 + b * 512 + px * 128, 128)] = unpack(u_last_in.at[px, pc], b, 32, 4)

    for wait in pending:
        wait()


SEMAPHORES = (
    ("lz", 4 * NC), ("ly", 4 * NC), ("lg", 4 * NC), ("lc", 4 * NC), ("g1", 8), ("g2", 4),
    ("r1", 4), ("rg", 4), ("rc", 4), ("h1", 8 * NC), ("h2", 4 * NC), ("p", 4 * NC), ("d", 4 * NC),
    ("y1", 4 * NC), ("y2", 8 * NC), ("u1", 4), ("u2", 8),
)


def body(grad, left_basis, right_basis, first_moment, second_moment):
    vm = pltpu.VMEM
    count = sum(n for _, n in SEMAPHORES)
    scratch = [
        vm((NC, 4, 2 * RC, 128), BF16),
        vm((NC, 4, 2 * RC, 128), BF16),
        vm((NC, 4, 2, 4, 2 * RC, 128), BF16),
        vm((NC, 2, 8 * RC, 1024), BF16),
        vm((NC, 4, 512, 8 * RC), BF16),
        vm((4, 2, 32, 512), BF16),
        vm((1024, 512), BF16),
        vm((4, 256, 128), BF16),
        vm((4, 2, 4, 256, 128), BF16),
        vm((1024, 1024), BF16),
        vm((1024, 1024), BF16),
        vm((NC, 4, 2, 4 * RC + 16, 128), BF16),
        vm((NC, 4, 2, 4 * RC + 16, 128), BF16),
        vm((NC, 4, 8 * RC + 16, 128), BF16),
        vm((RC, 1024), F32),
        vm((4 * RC, 512), F32),
        vm((8 * RC, 1024), BF16),
        vm((NC, 4, 8 * RC + 16, 128), BF16),
        vm((NC, 4, 8 * RC + 16, 128), BF16),
        vm((4 * RC, 256), F32),
        vm((NC, 8 * RC + 16, 128), BF16),
        vm((NC, 4, 8 * RC + 16, 128), BF16),
        vm((8 * RC, 1024), BF16),
        vm((4 * RC, 1024), F32),
        vm((RC, 1024), F32),
        vm((NC, 4, 8 * RC + 16, 128), BF16),
        vm((NC, 4, 8 * RC + 16, 128), BF16),
        vm((NC, 4 * RC + 16, 128), BF16),
        vm((NC, 2, 4, 4 * RC + 16, 128), BF16),
        vm((8 * RC, 512), BF16),
        vm((8 * RC, 512), BF16),
        vm((4, 256, 512), F32),
        vm((4, 1040, 128), BF16),
        vm((4, 1040, 128), BF16),
        vm((4, 2, 144, 128), BF16),
        vm((4, 2, 144, 128), BF16),
        pltpu.SemaphoreType.DMA((count,)),
        pltpu.SemaphoreType.DMA((count,)),
    ]
    whole = pl.BlockSpec(memory_space=pltpu.VMEM)
    return pl.pallas_call(
        kernel,
        out_shape=(
            jax.ShapeDtypeStruct((32, 4096), F32),
            jax.ShapeDtypeStruct((512, 256), F32),
            jax.ShapeDtypeStruct((512, 256), F32),
        ),
        in_specs=[whole] * 5,
        out_specs=(whole,) * 3,
        scratch_shapes=scratch,
        compiler_params=pltpu.CompilerParams(
            collective_id=0, has_side_effects=True, vmem_limit_bytes=56 * 2**20
        ),
    )(grad, left_basis, right_basis, first_moment, second_moment)


def solution(mesh):
    placed = (
        P(("dp", "tensor"), None),
        P("dp", "tensor"),
        P("dp", "tensor"),
        P("dp", "tensor"),
        P("dp", "tensor"),
    )
    return jax.shard_map(
        body,
        mesh=mesh,
        in_specs=placed,
        out_specs=(P(("dp", "tensor"), None), P("dp", "tensor"), P("dp", "tensor")),
        check_vma=False,
    )
```

```python
import jax
import jax.numpy as jnp
from jax import lax
from jax.experimental import pallas as pl
from jax.experimental.pallas import tpu as pltpu
from jax.sharding import PartitionSpec as P

STEP = 10
F32 = jnp.float32
BF16 = jnp.bfloat16
MESH = pl.DeviceIdType.MESH

SPAN = 250.0
BASE = 124.0
BOUND = 0.09375


def encode(x, inverse):
    t = jnp.maximum(jnp.abs(x) * inverse, 1e-30)
    y = jnp.exp2((t * lax.rsqrt(t)) * SPAN - BASE)
    return jnp.where(x < 0, -y, y).astype(BF16)


def decode(code, scale):
    y = code.astype(F32)
    t = (jnp.log2(jnp.abs(y)) + BASE) * (1.0 / SPAN)
    v = t * t * scale
    return jnp.where(y < 0, -v, v)


def pack(get, message, rows, blocks):
    most = None
    for b in range(blocks):
        a = jnp.abs(get(b))
        most = a if most is None else jnp.maximum(most, a)
    most = jnp.max(jnp.max(most, axis=0, keepdims=True), axis=1, keepdims=True)
    scale16 = (jnp.broadcast_to(most, (16, 128)) * 1.01 + 1e-30).astype(BF16)
    message[pl.ds(blocks * rows, 16), :] = scale16
    inverse = 1.0 / scale16.astype(F32)[0:1, :]
    for b in range(blocks):
        message[pl.ds(b * rows, rows), :] = encode(get(b), inverse)


def unpack(message, b, rows, blocks):
    scale = message[pl.ds(blocks * rows, 16), :].astype(F32)[0:1, :]
    return decode(message[pl.ds(b * rows, rows), :], scale)


def halves(x):
    hi = x.astype(BF16)
    return hi, (x - hi.astype(F32)).astype(BF16)


def dot(a, b):
    return lax.dot_general(a, b, (((1,), (0,)), ((), ())), preferred_element_type=F32)


def dot_t(a, b):
    return lax.dot_general(a, b, (((1,), (1,)), ((), ())), preferred_element_type=F32)


NC = 4
RC = 128 // NC
OFF = 1
TIE = -1
CC = 2
CB = 4 // CC


def kernel(
    grad, left, right, first_hbm, second_hbm, u_last_in, first_out, second_out,
    left_out, left_mid, left_in, lt, lf, grad_out, grad_in, right_out, right_in, right_hi, right_lo,
    h_out, h_in, h_gather, h_part, h_block, h_parts, rot_block, rot_out, rot_in, d_block, d_out, d_in, d_parts,
    y_block, y_sum, y_out, y_in, y_gather_out, y_gather, y_hi, y_lo, u_acc, u_sum, u_out, u_in, u_last_out,
    first, second, new_first, new_second, ss, rs, ls,
):
    dp = lax.axis_index("dp")
    tensor = lax.axis_index("tensor")
    y, xh = dp // 2, dp % 2
    z, xl, core = tensor // 4, (tensor // 2) % 2, tensor % 2
    x = xh * 2 + xl
    other = 1 - core

    def device(px, py, pz, pc):
        return (py * 2 + px // 2, pz * 4 + (px % 2) * 2 + pc)

    def turn(a, o):
        return (a + o) % 4

    first_sem = {}
    total = 0
    for name, count in SEMAPHORES:
        first_sem[name] = total
        total += count

    pending = []

    def remote(name, i, j, src, dst, target):
        return pltpu.make_async_remote_copy(
            src_ref=src, dst_ref=dst, send_sem=ss.at[first_sem[name] + i], recv_sem=rs.at[first_sem[name] + j],
            device_id=device(*target), device_id_type=MESH,
        )

    def send(name, i, src, dst, target, j=None):
        copy = remote(name, i, i if j is None else j, src, dst, target)
        copy.start()
        pending.append(copy.wait_send)

    def send_unless(own, name, i, src, dst, target, j):
        here = pltpu.make_async_copy(src, dst, rs.at[first_sem[name] + j])
        there = remote(name, i, j, src, dst, target)
        pl.when(own)(here.start)
        pl.when(jnp.logical_not(own))(there.start)
        pending.append(lambda: pl.when(jnp.logical_not(own))(there.wait_send))

    def arrive(name, j, dst):
        pltpu.make_async_copy(dst, dst, rs.at[first_sem[name] + j]).wait()

    def both_cores(o):
        return [(oc, pc) for oc, pc in ((1, other), (0, core)) if o or oc]

    loads = [pltpu.make_async_copy(first_hbm, first, ls.at[0]), pltpu.make_async_copy(second_hbm, second, ls.at[1])]
    for load in loads:
        load.start()

    barrier = pltpu.get_barrier_semaphore()
    peers = [(turn(x, o), y, z, pc) for o in range(4) for _, pc in both_cores(o)]
    peers += [(x, y, turn(z, o), pc) for o in (1, 2, 3) for _, pc in both_cores(o)]
    peers += [(x, turn(y, o), z, core) for o in (1, 2, 3)]
    for peer in peers:
        pl.semaphore_signal(barrier, inc=1, device_id=device(*peer), device_id_type=MESH)

    for b in range(4):
        code = encode(left[pl.ds(b * 128, 128), :].T, 1.0 / BOUND)
        for a in range(NC):
            for h in range(2):
                left_out[a, b, pl.ds(h * RC, RC), :] = code[h * 128 + a * RC : h * 128 + (a + 1) * RC]
    for px in range(4):
        for pc in range(2):
            for b in range(4):
                grad_out[px, pc, :, pl.ds(b * 128, 128)] = grad[:, pl.ds(pc * 2048 + b * 512 + px * 128, 128)]

    pl.semaphore_wait(barrier, len(peers))

    for a in range(NC):
        for o in (2, 1, 3):
            send("lz", a * 4 + o, left_out.at[a, turn(z, o)], left_mid.at[a, z], (x, y, turn(z, o), core))
        left_mid[a, z] = left_out[a, z]
    own_rows = pl.ds(pl.multiple_of(y * 256 + x * 64 + core * 32, 32), 32)
    for o in (2, 1, 3, 0):
        for oc, pc in both_cores(o):
            px = turn(x, o)
            send("g1", o * 2 + oc, grad_out.at[px, pc], grad_in.at[own_rows], (px, y, z, pc))
    grad_in[own_rows] = grad_out[x, core]
    for q in range(4):
        for b in range(2):
            right_out[q, pl.ds(b * 128, 128), :] = encode(
                right[pl.ds(q * 128, 128), pl.ds(b * 128, 128)], 1.0 / BOUND
            )
    for o in (2, 1, 3):
        px = turn(x, o)
        send("r1", o, right_out.at[px], right_in.at[y, core, x], (px, y, z, core))
    right_in[y, core, x] = right_out[x]

    def left_turn(a):
        for o in (1, 2, 3):
            arrive("lz", a * 4 + o, left_mid.at[a, turn(z, 4 - o)])
        for o in (2, 1, 3):
            to = turn(y, o)
            send("ly", a * 4 + o, left_mid.at[a, to], left_in.at[a, x, core, y], (x, to, z, core))
        left_in[a, x, core, y] = left_mid[a, y]

    def left_spread(a):
        for o in (1, 2, 3):
            arrive("ly", a * 4 + o, left_in.at[a, x, core, turn(y, 4 - o)])
        piece = left_in.at[a, x, core]
        for o in (2, 1, 3):
            send("lg", a * 4 + o, piece, piece, (turn(x, o), y, z, core))
        send("lc", a * 4, piece, piece, (x, y, z, other))

    def left_piece(a, px, pc):
        def one(ry, carry):
            hi, lo = halves(decode(left_in[a, px, pc, ry], BOUND))
            at = pl.ds(pl.multiple_of(ry * 256 + (px // 2) * 128, 128), 128)
            for h in range(2):
                rows = (pc * 2 + h) * RC
                lt[a, px % 2, pl.ds(pl.multiple_of(rows, RC), RC), at] = hi[h * RC : (h + 1) * RC]
                lt[a, px % 2, pl.ds(pl.multiple_of(4 * RC + rows, RC), RC), at] = lo[h * RC : (h + 1) * RC]
            return carry

        lax.fori_loop(0, 4, one, 0)

    def left_forward(a):
        for o in (1, 3, 2):
            piece = left_in.at[a, turn(x, 4 - o), core]
            arrive("lg", a * 4 + o, piece)
            send("lc", a * 4 + o, piece, piece, (x, y, z, other))

    def left_take(a):
        for o in (0, 1, 3, 2):
            left_piece(a, turn(x, 4 - o), core)
        for o in (0, 1, 3, 2):
            px = turn(x, 4 - o)
            arrive("lc", a * 4 + o, left_in.at[a, px, other])
            left_piece(a, px, other)

    for a in range(NC):
        left_turn(a)
    for o in range(4):
        for oc, pc in both_cores(o):
            rows = pl.ds(pl.multiple_of(y * 256 + turn(x, 4 - o) * 64 + pc * 32, 32), 32)
            arrive("g1", o * 2 + oc, grad_in.at[rows])
    own_rows = pl.ds(pl.multiple_of(y * 256, 256), 256)
    for o in (2, 1, 3):
        send("g2", o, grad_in.at[own_rows], grad_in.at[own_rows], (x, turn(y, o), z, core))
    left_spread(0)
    left_spread(1)
    left_forward(0)
    left_take(0)

    def basis_send():
        for o in (1, 2, 3):
            rows = pl.ds(pl.multiple_of(turn(y, 4 - o) * 256, 256), 256)
            arrive("g2", o, grad_in.at[rows])
        for o in (1, 2, 3):
            arrive("r1", o, right_in.at[y, core, turn(x, 4 - o)])
        piece = right_in.at[y, core]
        for o in (2, 1, 3):
            send("rg", o, piece, piece, (x, turn(y, o), z, core))
        send("rc", 0, piece, piece, (x, y, z, other))

    basis_send()

    def turned(a):
        for oc, pc in ((1, other), (0, core)):
            both = dot(lt[a, pc], grad_in[...])
            h_block[...] = both[0 : 4 * RC] + both[4 * RC : 8 * RC]
            for o in (2, 1, 3, 0):
                pz = turn(z, o)
                rows = pl.ds(pl.multiple_of(pz * RC, RC), RC)
                message = h_out.at[a, o, oc] if o or oc else h_in.at[a, z, core]
                pack(lambda b, rows=rows: h_block[rows, pl.ds(b * 128, 128)], message, RC, 4)
                if o or oc:
                    send("h1", (a * 4 + o) * 2 + oc, message, h_in.at[a, z, core], (x, y, pz, pc))

    def turned_sum(a):
        for o in range(4):
            for oc, pc in both_cores(o):
                arrive("h1", (a * 4 + o) * 2 + oc, h_in.at[a, turn(z, 4 - o), pc])

        def one(b, carry):
            for pc in range(2):
                v = None
                for pz in range(4):
                    message = h_in.at[a, pz, pc]
                    scale = message[pl.ds(4 * RC, 16), :].astype(F32)[0:1, :]
                    term = decode(message[pl.ds(pl.multiple_of(b * RC, RC), RC), :], scale)
                    v = term if v is None else v + term
                h_part[:, pl.ds(pl.multiple_of(pc * 512 + b * 128, 128), 128)] = v
            return carry

        lax.fori_loop(0, 4, one, 0)
        message = h_gather.at[a, z]
        pack(lambda b: h_part[:, pl.ds(b * 128, 128)], message, RC, 8)
        for o in (2, 1, 3):
            send("h2", a * 4 + o, message, message, (x, y, turn(z, o), core))

    def rotate(a):
        for o in (1, 2, 3):
            arrive("h2", a * 4 + o, h_gather.at[a, turn(z, 4 - o)])

        def one(pz, carry):
            for b in range(8):
                hi, lo = halves(unpack(h_gather.at[a, pz], b, RC, 8))
                h_parts[pl.ds(pl.multiple_of(pz * RC, RC), RC), pl.ds(b * 128, 128)] = hi
                h_parts[pl.ds(pl.multiple_of((4 + pz) * RC, RC), RC), pl.ds(b * 128, 128)] = lo
            return carry

        lax.fori_loop(0, 4, one, 0)
        for i in range(2):
            at = pl.ds(i * 512, 512)
            both = dot(h_parts[...], right_hi[:, at])
            low = dot(h_parts[pl.ds(0, 4 * RC), :], right_lo[:, at])
            rot_block[:, at] = both[0 : 4 * RC] + both[4 * RC : 8 * RC] + low
        for i in (1, 2, 3, 0):
            jd = turn(xl * 2 + core, i)
            pack(
                lambda b, jd=jd: rot_block[:, pl.ds(pl.multiple_of(jd * 256 + b * 128, 128), 128)],
                rot_out.at[a, i], 4 * RC, 2,
            )
            target = (core * 2 + jd // 2, y, z, jd % 2)
            args = ("p", a * 4 + i, rot_out.at[a, i], rot_in.at[a, x], target, a * 4 + x)
            if i:
                send(*args)
            else:
                send_unless(xh == core, *args)

    def moments(a):
        if a == 0:
            for load in loads:
                load.wait()
        for px in range(4):
            arrive("p", a * 4 + px, rot_in.at[a, px])

        def one(pz, carry):
            rows = pl.ds(pl.multiple_of(pz * 128 + a * RC, RC), RC)
            part = pl.ds(pl.multiple_of(pz * RC, RC), RC)
            for b in range(2):
                rot = None
                for px in range(4):
                    message = rot_in.at[a, px]
                    scale = message[pl.ds(8 * RC, 16), :].astype(F32)[0:1, :]
                    term = decode(message[pl.ds(pl.multiple_of((b * 4 + pz) * RC, RC), RC), :], scale)
                    rot = term if rot is None else rot + term
                at = pl.ds(b * 128, 128)
                moved_first = 0.9 * first[rows, at] + 0.1 * rot
                moved_second = 0.95 * second[rows, at] + 0.05 * rot * rot
                new_first[rows, at] = moved_first
                new_second[rows, at] = moved_second
                d_block[part, at] = (
                    moved_first / (1.0 - 0.9**STEP) / (jnp.sqrt(moved_second / (1.0 - 0.95**STEP)) + 1e-08)
                )
            return carry

        lax.fori_loop(0, 4, one, 0)
        pack(lambda b: d_block[:, pl.ds(b * 128, 128)], d_out.at[a], 4 * RC, 2)
        if a == NC - 1:
            for i, (src, dst) in enumerate(((new_first, first_out), (new_second, second_out))):
                store = pltpu.make_async_copy(src, dst, ls.at[2 + i])
                store.start()
                pending.append(store.wait)
        slot = xl * 2 + core
        for i in (2, 1, 3, 0):
            args = ("d", a * 4 + i, d_out.at[a], d_in.at[a, slot], (turn(x, i), y, z, xh), a * 4 + slot)
            if i:
                send(*args)
            else:
                send_unless(xh == core, *args)

    def back(a):
        for j in range(4):
            arrive("d", a * 4 + j, d_in.at[a, j])
            for b in range(2):
                hi, lo = halves(unpack(d_in.at[a, j], b, 4 * RC, 2))
                at = pl.ds(j * 256 + b * 128, 128)
                d_parts[pl.ds(0, 4 * RC), at] = hi
                d_parts[pl.ds(4 * RC, 4 * RC), at] = lo

        def tile(i, carry):
            at = pl.ds(pl.multiple_of(i * 512, 512), 512)
            both = dot_t(d_parts[...], right_hi[at, :])
            low = dot_t(d_parts[pl.ds(0, 4 * RC), :], right_lo[at, :])
            y_block[:, at] = both[0 : 4 * RC] + both[4 * RC : 8 * RC] + low
            return carry

        lax.fori_loop(0, 2, tile, 0)
        for o in (2, 1, 3, 0):
            pz = turn(z, o)
            rows = pl.ds(pl.multiple_of(pz * RC, RC), RC)
            message = y_out.at[a, o] if o else y_in.at[a, z]
            pack(lambda b, rows=rows: y_block[rows, pl.ds(b * 128, 128)], message, RC, 8)
            if o:
                send("y1", a * 4 + o, message, y_in.at[a, z], (x, y, pz, core))

    def back_sum(a):
        for o in (1, 2, 3):
            arrive("y1", a * 4 + o, y_in.at[a, turn(z, 4 - o)])

        def one(b, carry):
            v = None
            for pz in range(4):
                message = y_in.at[a, pz]
                scale = message[pl.ds(8 * RC, 16), :].astype(F32)[0:1, :]
                term = decode(message[pl.ds(pl.multiple_of(b * RC, RC), RC), :], scale)
                v = term if v is None else v + term
            y_sum[:, pl.ds(pl.multiple_of(b * 128, 128), 128)] = v
            return carry

        lax.fori_loop(0, 8, one, 0)
        for oc, pc in ((1, other), (0, core)):
            message = y_gather_out.at[a] if oc else y_gather.at[a, core, z]
            pack(
                lambda b, pc=pc: y_sum[:, pl.ds(pl.multiple_of(pc * 512 + b * 128, 128), 128)], message, RC, 4
            )
            for o in (2, 1, 3, 0):
                if o or oc:
                    send("y2", (a * 4 + o) * 2 + oc, message, y_gather.at[a, core, z], (x, y, turn(z, o), pc))

    def flip(a):
        def one(i, carry):
            pc, s = i // 8, i % 8
            at = pl.ds(pl.multiple_of(s * 128, 128), 128)
            for part in range(2):
                for sub in range(4 * RC // 128):
                    rows = pl.ds(part * 4 * RC + sub * 128, 128)
                    v = lt[a, pc, rows, at].astype(F32).T.astype(BF16)
                    to = pl.ds(pl.multiple_of(part * 256 + (s % 2) * 128, 128), 128)
                    lf[a, s // 2, to, pl.ds(pl.multiple_of(pc * 4 * RC + sub * 128, 128), 128)] = v
            return carry

        lax.fori_loop(0, 16, one, 0)

    def raised_take(a):
        for o in range(4):
            for oc, pc in both_cores(o):
                arrive("y2", (a * 4 + o) * 2 + oc, y_gather.at[a, pc, turn(z, 4 - o)])

        def one(i, carry):
            rows = pl.ds(pl.multiple_of(i * RC, RC), RC)
            for b in range(4):
                hi, lo = halves(unpack(y_gather.at[a, i // 4, i % 4], b, RC, 4))
                y_hi[rows, pl.ds(b * 128, 128)] = hi
                y_lo[rows, pl.ds(b * 128, 128)] = lo
            return carry

        lax.fori_loop(0, 8, one, 0)

    def raised(a, py):
        both = dot(lf[a, py], y_hi[...])
        v = both[0:256] + both[256:512] + dot(lf[a, py, pl.ds(0, 256), :], y_lo[...])
        u_acc[py] = u_acc[py] + v if a else v

    def right_piece(py, pc):
        def one(px, carry):
            for b in range(2):
                hi, lo = halves(decode(right_in[py, pc, px, pl.ds(b * 128, 128), :], BOUND))
                rows = pl.ds(pl.multiple_of(py * 256 + (px // 2) * 128, 128), 128)
                at = pl.ds(pl.multiple_of((px % 2) * 512 + pc * 256 + b * 128, 128), 128)
                right_hi[rows, at] = hi
                right_lo[rows, at] = lo
            return carry

        lax.fori_loop(0, 4, one, 0)

    def basis_take():
        for o in (1, 3, 2):
            piece = right_in.at[turn(y, 4 - o), core]
            arrive("rg", o, piece)
            send("rc", o, piece, piece, (x, y, z, other))
        for o in (0, 1, 3, 2):
            right_piece(turn(y, 4 - o), core)
        for o in (0, 1, 3, 2):
            py = turn(y, 4 - o)
            arrive("rc", o, right_in.at[py, other])
            right_piece(py, other)

    def step(stage, a):
        if stage == 0:
            if a:
                left_forward(a)
            if a + 2 < NC:
                left_spread(a + 2)
            if a:
                left_take(a)
            turned(a)
        if stage == 1:
            flip(a)
            turned_sum(a)
        if stage == 2:
            if a == 0:
                basis_take()
            rotate(a)
        if stage == 3:
            moments(a)
        if stage == 4:
            back(a)
        if stage == 5:
            back_sum(a)
        if stage == 6 and a < NC - 1:
            raised_take(a)

            def one(py, carry, a=a):
                raised(a, py)
                return carry

            lax.fori_loop(0, 4, one, 0)

    for _, _, stage, a in sorted((s + OFF * a, TIE * a, s, a) for s in range(7) for a in range(NC)):
        step(stage, a)

    raised_take(NC - 1)
    for o in (2, 1, 3, 0):
        py = turn(y, o)
        raised(NC - 1, py)
        for c in range(CC):
            message = u_out.at[c, o] if o else u_in.at[c, y]
            pack(lambda b, py=py, c=c: u_acc[py, :, pl.ds((c * CB + b) * 128, 128)], message, 256, CB)
            if o:
                send("u1", c * 4 + o, message, u_in.at[c, y], (x, py, z, core))
    for c in range(CC):
        for o in (1, 2, 3):
            arrive("u1", c * 4 + o, u_in.at[c, turn(y, 4 - o)])

        def raised_sum(b, carry, c=c):
            v = None
            for py in range(4):
                message = u_in.at[c, py]
                scale = message[pl.ds(256 * CB, 16), :].astype(F32)[0:1, :]
                term = decode(message[pl.ds(pl.multiple_of(b * 256, 256), 256), :], scale)
                v = term if v is None else v + term
            u_sum[:, pl.ds(pl.multiple_of(b * 128, 128), 128)] = v
            return carry

        lax.fori_loop(0, CB, raised_sum, 0)
        for px in range(4):
            for pc in range(2):
                rows = pl.ds(px * 64 + pc * 32, 32)
                pack(lambda b, rows=rows: u_sum[rows, pl.ds(b * 128, 128)], u_last_out.at[c, px, pc], 32, CB)
        for o in (2, 1, 3, 0):
            for oc, pc in both_cores(o):
                px = turn(x, o)
                send("u2", (c * 4 + o) * 2 + oc, u_last_out.at[c, px, pc], u_last_in.at[c, x, core], (px, y, z, pc))
        own = pltpu.make_async_copy(u_last_out.at[c, x, core], u_last_in.at[c, x, core], ls.at[4 + c])
        own.start()
        pending.append(own.wait)
    for c in range(CC):
        for o in range(4):
            for oc, pc in both_cores(o):
                arrive("u2", (c * 4 + o) * 2 + oc, u_last_in.at[c, turn(x, 4 - o), pc])
    for wait in pending:
        wait()


def finish(coded, first, second, update, new_first, new_second):
    new_first[...] = first[...]
    new_second[...] = second[...]
    for c in range(CC):
        for px in range(4):
            for pc in range(2):
                for b in range(CB):
                    at = pl.ds(pc * 2048 + (c * CB + b) * 512 + px * 128, 128)
                    update[:, at] = unpack(coded.at[c, px, pc], b, 32, CB)


SEMAPHORES = (
    ("lz", 4 * NC), ("ly", 4 * NC), ("lg", 4 * NC), ("lc", 4 * NC), ("g1", 8), ("g2", 4),
    ("r1", 4), ("rg", 4), ("rc", 4), ("h1", 8 * NC), ("h2", 4 * NC), ("p", 4 * NC), ("d", 4 * NC),
    ("y1", 4 * NC), ("y2", 8 * NC), ("u1", 4 * CC), ("u2", 8 * CC),
)


def body(grad, left_basis, right_basis, first_moment, second_moment):
    vm = pltpu.VMEM
    count = sum(n for _, n in SEMAPHORES)
    scratch = [
        vm((NC, 4, 2 * RC, 128), BF16),
        vm((NC, 4, 2 * RC, 128), BF16),
        vm((NC, 4, 2, 4, 2 * RC, 128), BF16),
        vm((NC, 2, 8 * RC, 1024), BF16),
        vm((NC, 4, 512, 8 * RC), BF16),
        vm((4, 2, 32, 512), BF16),
        vm((1024, 512), BF16),
        vm((4, 256, 128), BF16),
        vm((4, 2, 4, 256, 128), BF16),
        vm((1024, 1024), BF16),
        vm((1024, 1024), BF16),
        vm((NC, 4, 2, 4 * RC + 16, 128), BF16),
        vm((NC, 4, 2, 4 * RC + 16, 128), BF16),
        vm((NC, 4, 8 * RC + 16, 128), BF16),
        vm((RC, 1024), F32),
        vm((4 * RC, 512), F32),
        vm((8 * RC, 1024), BF16),
        vm((4 * RC, 1024), F32),
        vm((NC, 4, 8 * RC + 16, 128), BF16),
        vm((NC, 4, 8 * RC + 16, 128), BF16),
        vm((4 * RC, 256), F32),
        vm((NC, 8 * RC + 16, 128), BF16),
        vm((NC, 4, 8 * RC + 16, 128), BF16),
        vm((8 * RC, 1024), BF16),
        vm((4 * RC, 1024), F32),
        vm((RC, 1024), F32),
        vm((NC, 4, 8 * RC + 16, 128), BF16),
        vm((NC, 4, 8 * RC + 16, 128), BF16),
        vm((NC, 4 * RC + 16, 128), BF16),
        vm((NC, 2, 4, 4 * RC + 16, 128), BF16),
        vm((8 * RC, 512), BF16),
        vm((8 * RC, 512), BF16),
        vm((4, 256, 512), F32),
        vm((256, 128 * CB), F32),
        vm((CC, 4, 256 * CB + 16, 128), BF16),
        vm((CC, 4, 256 * CB + 16, 128), BF16),
        vm((CC, 4, 2, 32 * CB + 16, 128), BF16),
        vm((512, 256), F32),
        vm((512, 256), F32),
        vm((512, 256), F32),
        vm((512, 256), F32),
        pltpu.SemaphoreType.DMA((count,)),
        pltpu.SemaphoreType.DMA((count,)),
        pltpu.SemaphoreType.DMA((4 + CC,)),
    ]
    whole = pl.BlockSpec(memory_space=pltpu.VMEM)
    there = pl.BlockSpec(memory_space=pl.ANY)
    square = jax.ShapeDtypeStruct((512, 256), F32)
    coded, new_first, new_second = pl.pallas_call(
        kernel,
        out_shape=(jax.ShapeDtypeStruct((CC, 4, 2, 32 * CB + 16, 128), BF16), square, square),
        in_specs=[whole, whole, whole, there, there],
        out_specs=(there,) * 3,
        scratch_shapes=scratch,
        compiler_params=pltpu.CompilerParams(
            collective_id=0, has_side_effects=True, vmem_limit_bytes=56 * 2**20
        ),
    )(grad, left_basis, right_basis, first_moment, second_moment)
    return pl.pallas_call(
        finish,
        out_shape=(jax.ShapeDtypeStruct((32, 4096), F32), square, square),
        in_specs=[whole] * 3,
        out_specs=(whole,) * 3,
    )(coded, new_first, new_second)


def solution(mesh):
    placed = (
        P(("dp", "tensor"), None),
        P("dp", "tensor"),
        P("dp", "tensor"),
        P("dp", "tensor"),
        P("dp", "tensor"),
    )
    return jax.shard_map(
        body,
        mesh=mesh,
        in_specs=placed,
        out_specs=(P(("dp", "tensor"), None), P("dp", "tensor"), P("dp", "tensor")),
        check_vma=False,
    )
```

```python
import functools

import jax
import jax.numpy as jnp
from jax import lax
from jax.experimental import pallas as pl
from jax.experimental.pallas import tpu as pltpu
from jax.sharding import PartitionSpec as P

STEP = 10
F32 = jnp.float32
BF16 = jnp.bfloat16
MESH = pl.DeviceIdType.MESH

SPAN = 250.0
BASE = 124.0
BOUND = 0.09375


def encode(x, inverse):
    t = jnp.maximum(jnp.abs(x) * inverse, 1e-30)
    y = jnp.exp2((t * lax.rsqrt(t)) * SPAN - BASE)
    return jnp.where(x < 0, -y, y).astype(BF16)


def decode(code, scale):
    y = code.astype(F32)
    t = (jnp.log2(jnp.abs(y)) + BASE) * (1.0 / SPAN)
    v = t * t * scale
    return jnp.where(y < 0, -v, v)


def pack(get, message, rows, blocks):
    most = None
    for b in range(blocks):
        a = jnp.max(jnp.abs(get(b)).reshape(rows // 16, 16, 128), axis=0)
        most = a if most is None else jnp.maximum(most, a)
    scale = (most * 1.01 + 1e-30).astype(BF16)
    message[pl.ds(blocks * rows, 16), :] = scale
    inverse = (1.0 / scale.astype(F32))[None]
    for b in range(blocks):
        code = encode(get(b).reshape(rows // 16, 16, 128), inverse)
        message[pl.ds(b * rows, rows), :] = code.reshape(rows, 128)


def unpack_rows(message, start, rows, end):
    scale = message[pl.ds(end, 16), :].astype(F32)[None]
    code = message[pl.ds(start, rows), :].reshape(rows // 16, 16, 128)
    return decode(code, scale).reshape(rows, 128)


def unpack(message, b, rows, blocks):
    return unpack_rows(message, b * rows, rows, blocks * rows)


def halves(x):
    hi = x.astype(BF16)
    return hi, (x - hi.astype(F32)).astype(BF16)


def dot(a, b):
    return lax.dot_general(a, b, (((1,), (0,)), ((), ())), preferred_element_type=F32)


def dot_t(a, b):
    return lax.dot_general(a, b, (((1,), (1,)), ((), ())), preferred_element_type=F32)


NC = 4
RC = 128 // NC
OFF = 1
EARLY = 2
TIE = -1
CC = 4
CB = 4 // CC


def kernel(
    grad, left, right, first_hbm, second_hbm, u_last_in, first_out, second_out,
    left_out, left_mid, left_in, lt, lf, grad_out, grad_in, right_out, right_in, right_hi, right_lo,
    h_out, h_in, h_gather, h_part, h_block, h_parts, rot_block, rot_out, rot_in, d_block, d_out, d_in, d_parts,
    y_block, y_sum, y_out, y_in, y_gather_out, y_gather, y_hi, y_lo, u_acc, u_sum, u_out, u_in, u_last_out,
    first, second, new_first, new_second, ss, rs, ls,
):
    dp = lax.axis_index("dp")
    tensor = lax.axis_index("tensor")
    y, xh = dp // 2, dp % 2
    z, xl, core = tensor // 4, (tensor // 2) % 2, tensor % 2
    x = xh * 2 + xl
    other = 1 - core

    def device(px, py, pz, pc):
        return (py * 2 + px // 2, pz * 4 + (px % 2) * 2 + pc)

    def turn(a, o):
        return (a + o) % 4

    first_sem, send_sem = {}, {}
    total = 0
    for i, (name, count) in enumerate(SEMAPHORES):
        first_sem[name], send_sem[name] = total, i
        total += count

    def remote(name, j, src, dst, target):
        return pltpu.make_async_remote_copy(
            src_ref=src, dst_ref=dst, send_sem=ss.at[send_sem[name]], recv_sem=rs.at[first_sem[name] + j],
            device_id=device(*target), device_id_type=MESH,
        )

    def send(name, j, src, dst, target):
        remote(name, j, src, dst, target).start()

    def send_unless(own, name, j, src, dst, target):
        pl.when(own)(pltpu.make_async_copy(src, dst, rs.at[first_sem[name] + j]).start)
        pl.when(jnp.logical_not(own))(remote(name, j, src, dst, target).start)

    def arrive(name, j, like):
        pltpu.make_async_copy(like, like, rs.at[first_sem[name] + j]).wait()

    def sent(name, like):
        pltpu.make_async_copy(like, like, ss.at[send_sem[name]]).wait()

    def both_cores(o):
        return [(oc, pc) for oc, pc in ((1, other), (0, core)) if o or oc]

    pending = []
    loads = [pltpu.make_async_copy(first_hbm, first, ls.at[0]), pltpu.make_async_copy(second_hbm, second, ls.at[1])]
    for load in loads:
        load.start()

    barrier = pltpu.get_barrier_semaphore()
    peers = [(turn(x, o), y, z, pc) for o in range(4) for _, pc in both_cores(o)]
    peers += [(x, y, turn(z, o), pc) for o in (1, 2, 3) for _, pc in both_cores(o)]
    peers += [(x, turn(y, o), z, core) for o in (1, 2, 3)]
    for peer in peers:
        pl.semaphore_signal(barrier, inc=1, device_id=device(*peer), device_id_type=MESH)

    for b in range(4):
        code = encode(left[pl.ds(b * 128, 128), :].T, 1.0 / BOUND)
        for a in range(NC):
            for h in range(2):
                left_out[a, b, pl.ds(h * RC, RC), :] = code[h * 128 + a * RC : h * 128 + (a + 1) * RC]
    for px in range(4):
        for pc in range(2):
            for b in range(4):
                grad_out[px, pc, :, pl.ds(b * 128, 128)] = grad[:, pl.ds(pc * 2048 + b * 512 + px * 128, 128)]

    pl.semaphore_wait(barrier, len(peers))

    for a in range(NC):
        for o in (2, 1, 3):
            send("lz", a, left_out.at[a, turn(z, o)], left_mid.at[a, z], (x, y, turn(z, o), core))
        left_mid[a, z] = left_out[a, z]
    own_rows = pl.ds(pl.multiple_of(y * 256 + x * 64 + core * 32, 32), 32)
    for o in (2, 1, 3, 0):
        for oc, pc in both_cores(o):
            px = turn(x, o)
            send("g1", 0, grad_out.at[px, pc], grad_in.at[own_rows], (px, y, z, pc))
    grad_in[own_rows] = grad_out[x, core]
    for q in range(4):
        for b in range(2):
            right_out[q, pl.ds(b * 128, 128), :] = encode(
                right[pl.ds(q * 128, 128), pl.ds(b * 128, 128)], 1.0 / BOUND
            )
    for o in (2, 1, 3):
        px = turn(x, o)
        send("r1", 0, right_out.at[px], right_in.at[y, core, x], (px, y, z, core))
    right_in[y, core, x] = right_out[x]

    def ring_start(name, half):
        for up, h, part in ((1, 0, 0), (3, 1, 1), (1, 1, 2), (3, 0, 2)):
            send(name, part, half(y, h), half(y, h), (x, turn(y, up), z, core))

    def ring_pass(name, half):
        for from_, h, to in ((3, 0, 1), (1, 1, 3)):
            piece = half(turn(y, from_), h)
            arrive(name, h, piece)
            send(name, 2, piece, piece, (x, turn(y, to), z, core))

    def grad_half(py, h):
        return grad_in.at[pl.ds(pl.multiple_of(py * 256 + h * 128, 128), 128)]

    def right_half(py, h):
        return right_in.at[py, core, pl.ds(h * 2, 2)]

    def left_turn(a):
        arrive("lz", a, left_mid.at[a, pl.ds(0, 3)])
        for o in (2, 1, 3):
            to = turn(y, o)
            send("ly", a, left_mid.at[a, to], left_in.at[a, x, core, y], (x, to, z, core))
        left_in[a, x, core, y] = left_mid[a, y]

    def left_spread(a):
        piece = left_in.at[a, x, core]
        arrive("ly", a, piece.at[pl.ds(0, 3)])
        for o in (2, 1, 3):
            send("lg", a, piece, piece, (turn(x, o), y, z, core))
        send("lc", a, piece, piece, (x, y, z, other))

    def left_forward(a):
        arrive("lg", a, left_in.at[a, pl.ds(0, 3), core])
        for o in (1, 3, 2):
            piece = left_in.at[a, turn(x, 4 - o), core]
            send("lc", a, piece, piece, (x, y, z, other))

    def left_take(a):
        def one(px, carry, pc):
            for ry in range(4):
                hi, lo = halves(decode(left_in[a, px, pc, ry], BOUND))
                at = pl.ds(pl.multiple_of(ry * 256 + (px // 2) * 128, 128), 128)
                for h in range(2):
                    rows = (pc * 2 + h) * RC
                    lt[a, px % 2, pl.ds(pl.multiple_of(rows, RC), RC), at] = hi[h * RC : (h + 1) * RC]
                    lt[a, px % 2, pl.ds(pl.multiple_of(4 * RC + rows, RC), RC), at] = lo[h * RC : (h + 1) * RC]
            return carry

        lax.fori_loop(0, 4, functools.partial(one, pc=core), 0)
        arrive("lc", a, left_in.at[a, :, other])
        lax.fori_loop(0, 4, functools.partial(one, pc=other), 0)

    def flip(a):
        def one(s, carry):
            at = pl.ds(pl.multiple_of(s * 128, 128), 128)
            for pc in range(2):
                for part in range(2):
                    for sub in range(4 * RC // 128):
                        v = lt[a, pc, pl.ds(part * 4 * RC + sub * 128, 128), at].T
                        to = pl.ds(pl.multiple_of(part * 256 + (s % 2) * 128, 128), 128)
                        lf[a, s // 2, to, pl.ds(pc * 4 * RC + sub * 128, 128)] = v
            return carry

        lax.fori_loop(0, 8, one, 0)

    for a in range(NC):
        left_turn(a)
    arrive("g1", 0, grad_in.at[pl.ds(0, 224)])
    ring_start("g2", grad_half)
    left_spread(0)
    left_spread(1)
    ring_pass("g2", grad_half)
    arrive("r1", 0, right_in.at[0, 0, pl.ds(0, 3)])
    ring_start("rg", right_half)
    send("rc", 0, right_in.at[y, core], right_in.at[y, core], (x, y, z, other))
    left_forward(0)
    left_spread(2)
    left_take(0)
    flip(0)
    for a in range(1, EARLY):
        left_forward(a)
        if a + 2 < NC:
            left_spread(a + 2)
        left_take(a)
        flip(a)
    arrive("g2", 2, grad_in.at[pl.ds(0, 512)])

    def turned(a):
        for oc, pc in ((1, other), (0, core)):
            both = dot(lt[a, pc], grad_in[...])
            h_block[...] = both[0 : 4 * RC] + both[4 * RC : 8 * RC]
            for o in (2, 1, 3, 0):
                pz = turn(z, o)
                rows = pl.ds(pl.multiple_of(pz * RC, RC), RC)
                here = h_in.at[a, z * 2 + core]
                message = h_out.at[a, o, oc] if o or oc else here
                pack(lambda b, rows=rows: h_block[rows, pl.ds(b * 128, 128)], message, RC, 4)
                if o or oc:
                    send("h1", a, message, here, (x, y, pz, pc))

    def turned_sum(a):
        arrive("h1", a, h_in.at[a, pl.ds(0, 7)])

        def one(b, carry):
            for pc in range(2):
                v = None
                for pz in range(4):
                    start = pl.multiple_of(b * RC, RC)
                    term = unpack_rows(h_in.at[a, pz * 2 + pc], start, RC, 4 * RC)
                    v = term if v is None else v + term
                h_part[:, pl.ds(pl.multiple_of(pc * 512 + b * 128, 128), 128)] = v
            return carry

        lax.fori_loop(0, 4, one, 0)
        message = h_gather.at[a, z]
        pack(lambda b: h_part[:, pl.ds(b * 128, 128)], message, RC, 8)
        for o in (2, 1, 3):
            send("h2", a, message, message, (x, y, turn(z, o), core))

    def rotate(a):
        arrive("h2", a, h_gather.at[a, pl.ds(0, 3)])

        def one(pz, carry):
            for b in range(8):
                hi, lo = halves(unpack(h_gather.at[a, pz], b, RC, 8))
                h_parts[pl.ds(pl.multiple_of(pz * RC, RC), RC), pl.ds(b * 128, 128)] = hi
                h_parts[pl.ds(pl.multiple_of((4 + pz) * RC, RC), RC), pl.ds(b * 128, 128)] = lo
            return carry

        lax.fori_loop(0, 4, one, 0)
        for i in range(2):
            at = pl.ds(i * 512, 512)
            both = dot(h_parts[...], right_hi[:, at])
            low = dot(h_parts[pl.ds(0, 4 * RC), :], right_lo[:, at])
            rot_block[:, at] = both[0 : 4 * RC] + both[4 * RC : 8 * RC] + low
        for i in (1, 2, 3, 0):
            jd = turn(xl * 2 + core, i)
            pack(
                lambda b, jd=jd: rot_block[:, pl.ds(pl.multiple_of(jd * 256 + b * 128, 128), 128)],
                rot_out.at[a, i], 4 * RC, 2,
            )
            target = (core * 2 + jd // 2, y, z, jd % 2)
            args = ("p", a, rot_out.at[a, i], rot_in.at[a, x], target)
            if i:
                send(*args)
            else:
                send_unless(xh == core, *args)

    def moments(a):
        if a == 0:
            for load in loads:
                load.wait()
        arrive("p", a, rot_in.at[a])

        def one(pz, carry):
            rows = pl.ds(pl.multiple_of(pz * 128 + a * RC, RC), RC)
            part = pl.ds(pl.multiple_of(pz * RC, RC), RC)
            for b in range(2):
                rot = None
                for px in range(4):
                    start = pl.multiple_of((b * 4 + pz) * RC, RC)
                    term = unpack_rows(rot_in.at[a, px], start, RC, 8 * RC)
                    rot = term if rot is None else rot + term
                at = pl.ds(b * 128, 128)
                moved_first = 0.9 * first[rows, at] + 0.1 * rot
                moved_second = 0.95 * second[rows, at] + 0.05 * rot * rot
                new_first[rows, at] = moved_first
                new_second[rows, at] = moved_second
                d_block[part, at] = (
                    moved_first / (1.0 - 0.9**STEP) / (jnp.sqrt(moved_second / (1.0 - 0.95**STEP)) + 1e-08)
                )
            return carry

        lax.fori_loop(0, 4, one, 0)
        pack(lambda b: d_block[:, pl.ds(b * 128, 128)], d_out.at[a], 4 * RC, 2)
        if a == NC - 1:
            for i, (src, dst) in enumerate(((new_first, first_out), (new_second, second_out))):
                store = pltpu.make_async_copy(src, dst, ls.at[2 + i])
                store.start()
                pending.append(store.wait)
        slot = xl * 2 + core
        for i in (2, 1, 3, 0):
            args = ("d", a, d_out.at[a], d_in.at[a, slot], (turn(x, i), y, z, xh))
            if i:
                send(*args)
            else:
                send_unless(xh == core, *args)

    def back(a):
        arrive("d", a, d_in.at[a])
        for j in range(4):
            for b in range(2):
                hi, lo = halves(unpack(d_in.at[a, j], b, 4 * RC, 2))
                at = pl.ds(j * 256 + b * 128, 128)
                d_parts[pl.ds(0, 4 * RC), at] = hi
                d_parts[pl.ds(4 * RC, 4 * RC), at] = lo

        both = dot_t(d_parts[...], right_hi[...])
        low = dot_t(d_parts[pl.ds(0, 4 * RC), :], right_lo[...])
        y_block[...] = both[0 : 4 * RC] + both[4 * RC : 8 * RC] + low
        for o in (2, 1, 3, 0):
            pz = turn(z, o)
            rows = pl.ds(pl.multiple_of(pz * RC, RC), RC)
            message = y_out.at[a, o] if o else y_in.at[a, z]
            pack(lambda b, rows=rows: y_block[rows, pl.ds(b * 128, 128)], message, RC, 8)
            if o:
                send("y1", a, message, y_in.at[a, z], (x, y, pz, core))

    def back_sum(a):
        arrive("y1", a, y_in.at[a, pl.ds(0, 3)])

        def one(b, carry):
            v = None
            for pz in range(4):
                term = unpack_rows(y_in.at[a, pz], pl.multiple_of(b * RC, RC), RC, 8 * RC)
                v = term if v is None else v + term
            y_sum[:, pl.ds(pl.multiple_of(b * 128, 128), 128)] = v
            return carry

        lax.fori_loop(0, 8, one, 0)
        for oc, pc in ((1, other), (0, core)):
            here = y_gather.at[a, core * 4 + z]
            message = y_gather_out.at[a] if oc else here
            pack(
                lambda b, pc=pc: y_sum[:, pl.ds(pl.multiple_of(pc * 512 + b * 128, 128), 128)], message, RC, 4
            )
            for o in (2, 1, 3, 0):
                if o or oc:
                    send("y2", a, message, here, (x, y, turn(z, o), pc))

    def raised_take(a):
        arrive("y2", a, y_gather.at[a, pl.ds(0, 7)])

        def one(i, carry):
            rows = pl.ds(pl.multiple_of(i * RC, RC), RC)
            for b in range(4):
                hi, lo = halves(unpack(y_gather.at[a, i], b, RC, 4))
                y_hi[rows, pl.ds(b * 128, 128)] = hi
                y_lo[rows, pl.ds(b * 128, 128)] = lo
            return carry

        lax.fori_loop(0, 8, one, 0)

    def raised(a, py):
        both = dot(lf[a, py], y_hi[...])
        v = both[0:256] + both[256:512] + dot(lf[a, py, pl.ds(0, 256), :], y_lo[...])
        u_acc[py] = u_acc[py] + v if a else v

    def right_piece(py, pc):
        def one(px, carry):
            for b in range(2):
                hi, lo = halves(decode(right_in[py, pc, px, pl.ds(b * 128, 128), :], BOUND))
                rows = pl.ds(pl.multiple_of(py * 256 + (px // 2) * 128, 128), 128)
                at = pl.ds(pl.multiple_of((px % 2) * 512 + pc * 256 + b * 128, 128), 128)
                right_hi[rows, at] = hi
                right_lo[rows, at] = lo
            return carry

        lax.fori_loop(0, 4, one, 0)

    def basis_take():
        arrive("rg", 2, right_in.at[pl.ds(0, 2), core])
        for o in (1, 3, 2):
            piece = right_in.at[turn(y, 4 - o), core]
            send("rc", 0, piece, piece, (x, y, z, other))
        for o in (0, 1, 3, 2):
            right_piece(turn(y, 4 - o), core)
        arrive("rc", 0, right_in.at[:, other])
        for o in (0, 1, 3, 2):
            right_piece(turn(y, 4 - o), other)

    def step(stage, a):
        if stage == 0:
            if a >= EARLY:
                left_forward(a)
                if a + 2 < NC:
                    left_spread(a + 2)
                left_take(a)
            turned(a)
            if a == 0:
                ring_pass("rg", right_half)
        if stage == 1:
            if a >= EARLY:
                flip(a)
            turned_sum(a)
            if a == 0:
                basis_take()
        if stage == 2:
            rotate(a)
        if stage == 3:
            moments(a)
        if stage == 4:
            back(a)
        if stage == 5:
            back_sum(a)
        if stage == 6 and a < NC - 1:
            raised_take(a)

            def one(py, carry, a=a):
                raised(a, py)
                return carry

            lax.fori_loop(0, 4, one, 0)

    for _, _, stage, a in sorted((s + OFF * a, TIE * a, s, a) for s in range(7) for a in range(NC)):
        step(stage, a)

    raised_take(NC - 1)
    for py in range(4):
        raised(NC - 1, py)
    for c in range(CC):
        for o in (2, 1, 3, 0):
            py = turn(y, o)
            message = u_out.at[c, o] if o else u_in.at[c, y]
            pack(lambda b, py=py, c=c: u_acc[py, :, pl.ds((c * CB + b) * 128, 128)], message, 256, CB)
            if o:
                send("u1", c, message, u_in.at[c, y], (x, py, z, core))
    for c in range(CC):
        arrive("u1", c, u_in.at[c, pl.ds(0, 3)])
        for b in range(CB):
            v = None
            for py in range(4):
                term = unpack(u_in.at[c, py], b, 256, CB)
                v = term if v is None else v + term
            u_sum[:, pl.ds(b * 128, 128)] = v
        here = u_last_in.at[c, x * 2 + core]
        for px in range(4):
            for pc in range(2):
                rows = pl.ds(px * 64 + pc * 32, 32)
                pack(lambda b, rows=rows: u_sum[rows, pl.ds(b * 128, 128)], u_last_out.at[c, px, pc], 32, CB)
        for o in (2, 1, 3, 0):
            for oc, pc in both_cores(o):
                px = turn(x, o)
                send("u2", c, u_last_out.at[c, px, pc], here, (px, y, z, pc))
        own = pltpu.make_async_copy(u_last_out.at[c, x, core], here, ls.at[4 + c])
        own.start()
        pending.append(own.wait)

    sent("lz", left_mid.at[:, pl.ds(0, 3)])
    sent("ly", left_in.at[:, 0, 0, pl.ds(0, 3)])
    sent("lg", left_in.at[:, pl.ds(0, 3), 0])
    sent("lc", left_in.at[:, :, 0])
    sent("g1", grad_in.at[pl.ds(0, 224)])
    sent("g2", grad_in.at[pl.ds(0, 768)])
    sent("r1", right_in.at[0, 0, pl.ds(0, 3)])
    sent("rg", right_in.at[pl.ds(0, 3), 0])
    sent("rc", right_in.at[:, 0])
    sent("h1", h_in.at[:, pl.ds(0, 7)])
    sent("h2", h_gather.at[:, pl.ds(0, 3)])
    for name, like in (("p", rot_in), ("d", d_in)):
        pl.when(xh == core)(lambda name=name, like=like: sent(name, like.at[:, pl.ds(0, 3)]))
        pl.when(xh != core)(lambda name=name, like=like: sent(name, like))
    sent("y1", y_in.at[:, pl.ds(0, 3)])
    sent("y2", y_gather.at[:, pl.ds(0, 7)])
    sent("u1", u_in.at[:, pl.ds(0, 3)])
    for c in range(CC):
        arrive("u2", c, u_last_in.at[c, pl.ds(0, 7)])
    sent("u2", u_last_in.at[:, pl.ds(0, 7)])
    for wait in pending:
        wait()


def finish(coded, first, second, update, new_first, new_second):
    new_first[...] = first[...]
    new_second[...] = second[...]
    for c in range(CC):
        for px in range(4):
            for pc in range(2):
                for b in range(CB):
                    at = pl.ds(pc * 2048 + (c * CB + b) * 512 + px * 128, 128)
                    update[:, at] = unpack(coded.at[c, px * 2 + pc], b, 32, CB)


SEMAPHORES = (
    ("lz", NC), ("ly", NC), ("lg", NC), ("lc", NC), ("g1", 1), ("g2", 3), ("r1", 1), ("rg", 3), ("rc", 1),
    ("h1", NC), ("h2", NC), ("p", NC), ("d", NC), ("y1", NC), ("y2", NC), ("u1", CC), ("u2", CC),
)


def body(grad, left_basis, right_basis, first_moment, second_moment):
    vm = pltpu.VMEM
    count = sum(n for _, n in SEMAPHORES)
    scratch = [
        vm((NC, 4, 2 * RC, 128), BF16),
        vm((NC, 4, 2 * RC, 128), BF16),
        vm((NC, 4, 2, 4, 2 * RC, 128), BF16),
        vm((NC, 2, 8 * RC, 1024), BF16),
        vm((NC, 4, 512, 8 * RC), BF16),
        vm((4, 2, 32, 512), BF16),
        vm((1024, 512), BF16),
        vm((4, 256, 128), BF16),
        vm((4, 2, 4, 256, 128), BF16),
        vm((1024, 1024), BF16),
        vm((1024, 1024), BF16),
        vm((NC, 4, 2, 4 * RC + 16, 128), BF16),
        vm((NC, 8, 4 * RC + 16, 128), BF16),
        vm((NC, 4, 8 * RC + 16, 128), BF16),
        vm((RC, 1024), F32),
        vm((4 * RC, 512), F32),
        vm((8 * RC, 1024), BF16),
        vm((4 * RC, 1024), F32),
        vm((NC, 4, 8 * RC + 16, 128), BF16),
        vm((NC, 4, 8 * RC + 16, 128), BF16),
        vm((4 * RC, 256), F32),
        vm((NC, 8 * RC + 16, 128), BF16),
        vm((NC, 4, 8 * RC + 16, 128), BF16),
        vm((8 * RC, 1024), BF16),
        vm((4 * RC, 1024), F32),
        vm((RC, 1024), F32),
        vm((NC, 4, 8 * RC + 16, 128), BF16),
        vm((NC, 4, 8 * RC + 16, 128), BF16),
        vm((NC, 4 * RC + 16, 128), BF16),
        vm((NC, 8, 4 * RC + 16, 128), BF16),
        vm((8 * RC, 512), BF16),
        vm((8 * RC, 512), BF16),
        vm((4, 256, 512), F32),
        vm((256, 128 * CB), F32),
        vm((CC, 4, 256 * CB + 16, 128), BF16),
        vm((CC, 4, 256 * CB + 16, 128), BF16),
        vm((CC, 4, 2, 32 * CB + 16, 128), BF16),
        vm((512, 256), F32),
        vm((512, 256), F32),
        vm((512, 256), F32),
        vm((512, 256), F32),
        pltpu.SemaphoreType.DMA((len(SEMAPHORES),)),
        pltpu.SemaphoreType.DMA((count,)),
        pltpu.SemaphoreType.DMA((4 + CC,)),
    ]
    whole = pl.BlockSpec(memory_space=pltpu.VMEM)
    there = pl.BlockSpec(memory_space=pl.ANY)
    square = jax.ShapeDtypeStruct((512, 256), F32)
    coded, new_first, new_second = pl.pallas_call(
        kernel,
        out_shape=(jax.ShapeDtypeStruct((CC, 8, 32 * CB + 16, 128), BF16), square, square),
        in_specs=[whole, whole, whole, there, there],
        out_specs=(there,) * 3,
        scratch_shapes=scratch,
        compiler_params=pltpu.CompilerParams(
            collective_id=0, has_side_effects=True, vmem_limit_bytes=56 * 2**20
        ),
    )(grad, left_basis, right_basis, first_moment, second_moment)
    return pl.pallas_call(
        finish,
        out_shape=(jax.ShapeDtypeStruct((32, 4096), F32), square, square),
        in_specs=[whole] * 3,
        out_specs=(whole,) * 3,
    )(coded, new_first, new_second)


def solution(mesh):
    placed = (
        P(("dp", "tensor"), None),
        P("dp", "tensor"),
        P("dp", "tensor"),
        P("dp", "tensor"),
        P("dp", "tensor"),
    )
    return jax.shard_map(
        body,
        mesh=mesh,
        in_specs=placed,
        out_specs=(P(("dp", "tensor"), None), P("dp", "tensor"), P("dp", "tensor")),
        check_vma=False,
    )
```

```python
import functools

import jax
import jax.numpy as jnp
from jax import lax
from jax.experimental import pallas as pl
from jax.experimental.pallas import tpu as pltpu
from jax.sharding import PartitionSpec as P

STEP = 10
F32 = jnp.float32
BF16 = jnp.bfloat16
MESH = pl.DeviceIdType.MESH

SPAN = 250.0
BASE = 124.0
BOUND = 0.09375


def encode(x, inverse):
    t = jnp.maximum(jnp.abs(x) * inverse, 1e-30)
    y = jnp.exp2((t * lax.rsqrt(t)) * SPAN - BASE)
    return jnp.where(x < 0, -y, y).astype(BF16)


def decode(code, scale):
    y = code.astype(F32)
    t = (jnp.log2(jnp.abs(y)) + BASE) * (1.0 / SPAN)
    v = t * t * scale
    return jnp.where(y < 0, -v, v)


def pack(get, message, rows, blocks):
    most = None
    for b in range(blocks):
        a = jnp.max(jnp.abs(get(b)).reshape(rows // 16, 16, 128), axis=0)
        most = a if most is None else jnp.maximum(most, a)
    scale = (most * 1.01 + 1e-30).astype(BF16)
    message[pl.ds(blocks * rows, 16), :] = scale
    inverse = (1.0 / scale.astype(F32))[None]
    for b in range(blocks):
        code = encode(get(b).reshape(rows // 16, 16, 128), inverse)
        message[pl.ds(b * rows, rows), :] = code.reshape(rows, 128)


def unpack_rows(message, start, rows, end):
    scale = message[pl.ds(end, 16), :].astype(F32)[None]
    code = message[pl.ds(start, rows), :].reshape(rows // 16, 16, 128)
    return decode(code, scale).reshape(rows, 128)


def unpack(message, b, rows, blocks):
    return unpack_rows(message, b * rows, rows, blocks * rows)


def halves(x):
    hi = x.astype(BF16)
    return hi, (x - hi.astype(F32)).astype(BF16)


def dot(a, b):
    return lax.dot_general(a, b, (((1,), (0,)), ((), ())), preferred_element_type=F32)


def dot_t(a, b):
    return lax.dot_general(a, b, (((1,), (1,)), ((), ())), preferred_element_type=F32)


NC = 4
RC = 128 // NC
GRAD_FIRST = False
ORDER = (
    "turned0", "pass0", "turned1", "forward2", "take2", "turned2", "turned_sum0", "forward3", "take3", "turned_sum1",
    "turned3", "basis0", "turned_sum2", "rotate0", "rotate1", "flip1", "turned_sum3", "moments0", "flip2", "rotate2",
    "moments1", "rotate3", "back0", "back1", "moments2", "flip3", "back_sum0", "moments3", "back_sum1", "back2",
    "back3", "raise0", "back_sum2", "raise1", "back_sum3", "raise2",
)
CC = 2
CB = 4 // CC


def kernel(
    grad, left, right, first_hbm, second_hbm, u_last_in, first_out, second_out,
    left_out, left_mid, left_in, lt, lf, grad_out, grad_in, right_out, right_in, right_hi, right_lo,
    h_out, h_in, h_gather, h_part, h_block, h_parts, rot_block, rot_out, rot_in, d_block, d_out, d_in, d_parts,
    y_block, y_sum, y_out, y_in, y_gather_out, y_gather, y_hi, y_lo, u_acc, u_sum, u_far_out, u_far_in, u_out, u_in, u_last_out,
    first, second, new_first, new_second, ss, rs, ls,
):
    dp = lax.axis_index("dp")
    tensor = lax.axis_index("tensor")
    y, xh = dp // 2, dp % 2
    z, xl, core = tensor // 4, (tensor // 2) % 2, tensor % 2
    x = xh * 2 + xl
    other = 1 - core

    def device(px, py, pz, pc):
        return (py * 2 + px // 2, pz * 4 + (px % 2) * 2 + pc)

    def turn(a, o):
        return (a + o) % 4

    first_sem, send_sem = {}, {}
    total = 0
    for i, (name, count) in enumerate(SEMAPHORES):
        first_sem[name], send_sem[name] = total, i
        total += count

    def remote(name, j, src, dst, target):
        return pltpu.make_async_remote_copy(
            src_ref=src, dst_ref=dst, send_sem=ss.at[send_sem[name]], recv_sem=rs.at[first_sem[name] + j],
            device_id=device(*target), device_id_type=MESH,
        )

    def send(name, j, src, dst, target):
        remote(name, j, src, dst, target).start()

    def send_unless(own, name, j, src, dst, target):
        pl.when(own)(pltpu.make_async_copy(src, dst, rs.at[first_sem[name] + j]).start)
        pl.when(jnp.logical_not(own))(remote(name, j, src, dst, target).start)

    def arrive(name, j, like):
        pltpu.make_async_copy(like, like, rs.at[first_sem[name] + j]).wait()

    def sent(name, like):
        pltpu.make_async_copy(like, like, ss.at[send_sem[name]]).wait()

    def both_cores(o):
        return [(oc, pc) for oc, pc in ((1, other), (0, core)) if o or oc]

    pending = []
    loads = [pltpu.make_async_copy(first_hbm, first, ls.at[0]), pltpu.make_async_copy(second_hbm, second, ls.at[1])]
    for load in loads:
        load.start()

    barrier = pltpu.get_barrier_semaphore()
    peers = [(turn(x, o), y, z, pc) for o in range(4) for _, pc in both_cores(o)]
    peers += [(x, y, turn(z, o), pc) for o in (1, 2, 3) for _, pc in both_cores(o)]
    peers += [(x, turn(y, o), z, core) for o in (1, 2, 3)]
    for peer in peers:
        pl.semaphore_signal(barrier, inc=1, device_id=device(*peer), device_id_type=MESH)

    for b in range(4):
        code = encode(left[pl.ds(b * 128, 128), :].T, 1.0 / BOUND)
        for a in range(NC):
            for h in range(2):
                left_out[a, b, pl.ds(h * RC, RC), :] = code[h * 128 + a * RC : h * 128 + (a + 1) * RC]
    for px in range(4):
        for pc in range(2):
            for b in range(4):
                grad_out[px, pc, :, pl.ds(b * 128, 128)] = grad[:, pl.ds(pc * 2048 + b * 512 + px * 128, 128)]

    pl.semaphore_wait(barrier, len(peers))

    for a in range(NC):
        for o in (2, 1, 3):
            send("lz", a, left_out.at[a, turn(z, o)], left_mid.at[a, z], (x, y, turn(z, o), core))
        left_mid[a, z] = left_out[a, z]
    own_rows = pl.ds(pl.multiple_of(y * 256 + x * 64 + core * 32, 32), 32)
    for o in (2, 1, 3, 0):
        for oc, pc in both_cores(o):
            px = turn(x, o)
            send("g1", 0, grad_out.at[px, pc], grad_in.at[own_rows], (px, y, z, pc))
    grad_in[own_rows] = grad_out[x, core]
    def ring_start(name, half):
        for up, h, part in ((1, 0, 0), (3, 1, 1), (1, 1, 2), (3, 0, 2)):
            send(name, part, half(y, h), half(y, h), (x, turn(y, up), z, core))

    def ring_pass(name, half):
        for from_, h, to in ((3, 0, 1), (1, 1, 3)):
            piece = half(turn(y, from_), h)
            arrive(name, h, piece)
            send(name, 2, piece, piece, (x, turn(y, to), z, core))

    def grad_half(py, h):
        return grad_in.at[pl.ds(pl.multiple_of(py * 256 + h * 128, 128), 128)]

    def right_half(py, h):
        return right_in.at[py, core, pl.ds(h * 2, 2)]

    def left_turn(a):
        arrive("lz", a, left_mid.at[a, pl.ds(0, 3)])
        for o in (2, 1, 3):
            to = turn(y, o)
            send("ly", a, left_mid.at[a, to], left_in.at[a, x, core, y], (x, to, z, core))
        left_in[a, x, core, y] = left_mid[a, y]

    def left_spread(a):
        piece = left_in.at[a, x, core]
        arrive("ly", a, piece.at[pl.ds(0, 3)])
        for o in (2, 1, 3):
            send("lg", a, piece, piece, (turn(x, o), y, z, core))
        send("lc", a, piece, piece, (x, y, z, other))

    def left_forward(a):
        arrive("lg", a, left_in.at[a, pl.ds(0, 3), core])
        for o in (1, 3, 2):
            piece = left_in.at[a, turn(x, 4 - o), core]
            send("lc", a, piece, piece, (x, y, z, other))

    def left_take(a):
        def one(px, carry, pc):
            for ry in range(4):
                hi, lo = halves(decode(left_in[a, px, pc, ry], BOUND))
                at = pl.ds(pl.multiple_of(ry * 256 + (px // 2) * 128, 128), 128)
                for h in range(2):
                    rows = (pc * 2 + h) * RC
                    lt[a, px % 2, pl.ds(pl.multiple_of(rows, RC), RC), at] = hi[h * RC : (h + 1) * RC]
                    lt[a, px % 2, pl.ds(pl.multiple_of(4 * RC + rows, RC), RC), at] = lo[h * RC : (h + 1) * RC]
            return carry

        lax.fori_loop(0, 4, functools.partial(one, pc=core), 0)
        arrive("lc", a, left_in.at[a, :, other])
        lax.fori_loop(0, 4, functools.partial(one, pc=other), 0)

    def flip(a):
        def one(s, carry):
            at = pl.ds(pl.multiple_of(s * 128, 128), 128)
            for pc in range(2):
                for part in range(2):
                    for sub in range(4 * RC // 128):
                        v = lt[a, pc, pl.ds(part * 4 * RC + sub * 128, 128), at].T
                        to = pl.ds(pl.multiple_of(part * 256 + (s % 2) * 128, 128), 128)
                        lf[a, s // 2, to, pl.ds(pc * 4 * RC + sub * 128, 128)] = v
            return carry

        lax.fori_loop(0, 8, one, 0)

    left_turn(0)
    for q in range(4):
        for b in range(2):
            right_out[q, pl.ds(b * 128, 128), :] = encode(
                right[pl.ds(q * 128, 128), pl.ds(b * 128, 128)], 1.0 / BOUND
            )
    right_in[y, core, x] = right_out[x]
    if GRAD_FIRST:
        arrive("g1", 0, grad_in.at[pl.ds(0, 224)])
        ring_start("g2", grad_half)
    for a in range(1, NC):
        left_turn(a)
    if not GRAD_FIRST:
        arrive("g1", 0, grad_in.at[pl.ds(0, 224)])
        ring_start("g2", grad_half)
    for o in (2, 1, 3):
        px = turn(x, o)
        send("r1", 0, right_out.at[px], right_in.at[y, core, x], (px, y, z, core))
    left_spread(0)
    left_spread(1)
    ring_pass("g2", grad_half)
    arrive("r1", 0, right_in.at[0, 0, pl.ds(0, 3)])
    ring_start("rg", right_half)
    send("rc", 0, right_in.at[y, core], right_in.at[y, core], (x, y, z, other))
    left_forward(0)
    left_spread(2)
    left_take(0)
    flip(0)
    left_forward(1)
    left_spread(3)
    left_take(1)
    arrive("g2", 2, grad_in.at[pl.ds(0, 512)])

    def turned(a):
        for oc, pc in ((1, other), (0, core)):
            both = dot(lt[a, pc], grad_in[...])
            h_block[...] = both[0 : 4 * RC] + both[4 * RC : 8 * RC]
            for o in (2, 1, 3, 0):
                pz = turn(z, o)
                rows = pl.ds(pl.multiple_of(pz * RC, RC), RC)
                here = h_in.at[a, z * 2 + core]
                message = h_out.at[a, o, oc] if o or oc else here
                pack(lambda b, rows=rows: h_block[rows, pl.ds(b * 128, 128)], message, RC, 4)
                if o or oc:
                    send("h1", a, message, here, (x, y, pz, pc))

    def turned_sum(a):
        arrive("h1", a, h_in.at[a, pl.ds(0, 7)])

        def one(b, carry):
            for pc in range(2):
                v = None
                for pz in range(4):
                    start = pl.multiple_of(b * RC, RC)
                    term = unpack_rows(h_in.at[a, pz * 2 + pc], start, RC, 4 * RC)
                    v = term if v is None else v + term
                h_part[:, pl.ds(pl.multiple_of(pc * 512 + b * 128, 128), 128)] = v
            return carry

        lax.fori_loop(0, 4, one, 0)
        message = h_gather.at[a, z]
        pack(lambda b: h_part[:, pl.ds(b * 128, 128)], message, RC, 8)
        for o in (2, 1, 3):
            send("h2", a, message, message, (x, y, turn(z, o), core))

    def rotate(a):
        arrive("h2", a, h_gather.at[a, pl.ds(0, 3)])

        def one(pz, carry):
            for b in range(8):
                hi, lo = halves(unpack(h_gather.at[a, pz], b, RC, 8))
                h_parts[pl.ds(pl.multiple_of(pz * RC, RC), RC), pl.ds(b * 128, 128)] = hi
                h_parts[pl.ds(pl.multiple_of((4 + pz) * RC, RC), RC), pl.ds(b * 128, 128)] = lo
            return carry

        lax.fori_loop(0, 4, one, 0)
        for i in range(2):
            at = pl.ds(i * 512, 512)
            both = dot(h_parts[...], right_hi[:, at])
            low = dot(h_parts[pl.ds(0, 4 * RC), :], right_lo[:, at])
            rot_block[:, at] = both[0 : 4 * RC] + both[4 * RC : 8 * RC] + low
        for i in (1, 2, 3, 0):
            jd = turn(xl * 2 + core, i)
            pack(
                lambda b, jd=jd: rot_block[:, pl.ds(pl.multiple_of(jd * 256 + b * 128, 128), 128)],
                rot_out.at[a, i], 4 * RC, 2,
            )
            target = (core * 2 + jd // 2, y, z, jd % 2)
            args = ("p", a, rot_out.at[a, i], rot_in.at[a, x], target)
            if i:
                send(*args)
            else:
                send_unless(xh == core, *args)

    def moments(a):
        if a == 0:
            for load in loads:
                load.wait()
        arrive("p", a, rot_in.at[a])

        def one(pz, carry):
            rows = pl.ds(pl.multiple_of(pz * 128 + a * RC, RC), RC)
            part = pl.ds(pl.multiple_of(pz * RC, RC), RC)
            for b in range(2):
                rot = None
                for px in range(4):
                    start = pl.multiple_of((b * 4 + pz) * RC, RC)
                    term = unpack_rows(rot_in.at[a, px], start, RC, 8 * RC)
                    rot = term if rot is None else rot + term
                at = pl.ds(b * 128, 128)
                moved_first = 0.9 * first[rows, at] + 0.1 * rot
                moved_second = 0.95 * second[rows, at] + 0.05 * rot * rot
                new_first[rows, at] = moved_first
                new_second[rows, at] = moved_second
                d_block[part, at] = (
                    moved_first / (1.0 - 0.9**STEP) / (jnp.sqrt(moved_second / (1.0 - 0.95**STEP)) + 1e-08)
                )
            return carry

        lax.fori_loop(0, 4, one, 0)
        pack(lambda b: d_block[:, pl.ds(b * 128, 128)], d_out.at[a], 4 * RC, 2)
        if a == NC - 1:
            for i, (src, dst) in enumerate(((new_first, first_out), (new_second, second_out))):
                store = pltpu.make_async_copy(src, dst, ls.at[2 + i])
                store.start()
                pending.append(store.wait)
        slot = xl * 2 + core
        for i in (2, 1, 3, 0):
            args = ("d", a, d_out.at[a], d_in.at[a, slot], (turn(x, i), y, z, xh))
            if i:
                send(*args)
            else:
                send_unless(xh == core, *args)

    def back(a):
        arrive("d", a, d_in.at[a])
        for j in range(4):
            for b in range(2):
                hi, lo = halves(unpack(d_in.at[a, j], b, 4 * RC, 2))
                at = pl.ds(j * 256 + b * 128, 128)
                d_parts[pl.ds(0, 4 * RC), at] = hi
                d_parts[pl.ds(4 * RC, 4 * RC), at] = lo

        both = dot_t(d_parts[...], right_hi[...])
        low = dot_t(d_parts[pl.ds(0, 4 * RC), :], right_lo[...])
        y_block[...] = both[0 : 4 * RC] + both[4 * RC : 8 * RC] + low
        for o in (2, 1, 3, 0):
            pz = turn(z, o)
            rows = pl.ds(pl.multiple_of(pz * RC, RC), RC)
            message = y_out.at[a, o] if o else y_in.at[a, z]
            pack(lambda b, rows=rows: y_block[rows, pl.ds(b * 128, 128)], message, RC, 8)
            if o:
                send("y1", a, message, y_in.at[a, z], (x, y, pz, core))

    def back_sum(a):
        arrive("y1", a, y_in.at[a, pl.ds(0, 3)])

        def one(b, carry):
            v = None
            for pz in range(4):
                term = unpack_rows(y_in.at[a, pz], pl.multiple_of(b * RC, RC), RC, 8 * RC)
                v = term if v is None else v + term
            y_sum[:, pl.ds(pl.multiple_of(b * 128, 128), 128)] = v
            return carry

        lax.fori_loop(0, 8, one, 0)
        for oc, pc in ((1, other), (0, core)):
            here = y_gather.at[a, core * 4 + z]
            message = y_gather_out.at[a] if oc else here
            pack(
                lambda b, pc=pc: y_sum[:, pl.ds(pl.multiple_of(pc * 512 + b * 128, 128), 128)], message, RC, 4
            )
            for o in (2, 1, 3, 0):
                if o or oc:
                    send("y2", a, message, here, (x, y, turn(z, o), pc))

    def raised_take(a):
        arrive("y2", a, y_gather.at[a, pl.ds(0, 7)])

        def one(i, carry):
            rows = pl.ds(pl.multiple_of(i * RC, RC), RC)
            for b in range(4):
                hi, lo = halves(unpack(y_gather.at[a, i], b, RC, 4))
                y_hi[rows, pl.ds(b * 128, 128)] = hi
                y_lo[rows, pl.ds(b * 128, 128)] = lo
            return carry

        lax.fori_loop(0, 8, one, 0)

    def raised(a, py):
        both = dot(lf[a, py], y_hi[...])
        v = both[0:256] + both[256:512] + dot(lf[a, py, pl.ds(0, 256), :], y_lo[...])
        u_acc[py] = u_acc[py] + v if a else v

    def right_piece(py, pc):
        def one(px, carry):
            for b in range(2):
                hi, lo = halves(decode(right_in[py, pc, px, pl.ds(b * 128, 128), :], BOUND))
                rows = pl.ds(pl.multiple_of(py * 256 + (px // 2) * 128, 128), 128)
                at = pl.ds(pl.multiple_of((px % 2) * 512 + pc * 256 + b * 128, 128), 128)
                right_hi[rows, at] = hi
                right_lo[rows, at] = lo
            return carry

        lax.fori_loop(0, 4, one, 0)

    def basis_take():
        arrive("rg", 2, right_in.at[pl.ds(0, 2), core])
        for o in (1, 3, 2):
            piece = right_in.at[turn(y, 4 - o), core]
            send("rc", 0, piece, piece, (x, y, z, other))
        for o in (0, 1, 3, 2):
            right_piece(turn(y, 4 - o), core)
        arrive("rc", 0, right_in.at[:, other])
        for o in (0, 1, 3, 2):
            right_piece(turn(y, 4 - o), other)

    def raise_all(a):
        raised_take(a)

        def one(py, carry):
            raised(a, py)
            return carry

        lax.fori_loop(0, 4, one, 0)

    steps = {
        "turned": turned, "pass": lambda a: ring_pass("rg", right_half), "forward": left_forward, "take": left_take,
        "turned_sum": turned_sum, "basis": lambda a: basis_take(), "rotate": rotate, "moments": moments, "flip": flip,
        "back": back, "back_sum": back_sum, "raise": raise_all,
    }
    for name in ORDER:
        steps[name[:-1]](int(name[-1]))

    raised_take(NC - 1)
    def rows_of(py, h, c, b):
        return u_acc[py, pl.ds(h * 128, 128), pl.ds((c * CB + b) * 128, 128)]

    def to_neighbour(name, c, h, up, py, message, dst):
        pack(lambda b: rows_of(py, h, c, b), message, 128, CB)
        send(name, c, message, dst, (x, turn(y, up), z, core))

    raised(NC - 1, turn(y, 2))
    for c in range(CC):
        for h, up in ((0, 1), (1, 3)):
            to_neighbour("uf", c, h, up, turn(y, 2), u_far_out.at[c, h], u_far_in.at[c, h])
    raised(NC - 1, turn(y, 1))
    raised(NC - 1, turn(y, 3))
    for c in range(CC):
        for h, up, slot in ((1, 1, 0), (0, 3, 1)):
            to_neighbour("u1", c, h, up, turn(y, up), u_out.at[c, slot, h], u_in.at[c, slot, h])
    for c in range(CC):
        arrive("uf", c, u_far_in.at[c])
        for h, up, slot in ((0, 1, 0), (1, 3, 1)):
            py = turn(y, up)
            for b in range(CB):
                at = pl.ds((c * CB + b) * 128, 128)
                u_acc[py, pl.ds(h * 128, 128), at] += unpack(u_far_in.at[c, h], b, 128, CB)
            to_neighbour("u1", c, h, up, py, u_out.at[c, slot, h], u_in.at[c, slot, h])
    raised(NC - 1, y)
    for c in range(CC):
        arrive("u1", c, u_in.at[c])
        for b in range(CB):
            for h in range(2):
                v = rows_of(y, h, c, b)
                for slot in range(2):
                    v = v + unpack(u_in.at[c, slot, h], b, 128, CB)
                u_sum[pl.ds(h * 128, 128), pl.ds(b * 128, 128)] = v
        here = u_last_in.at[c, x * 2 + core]
        for px in range(4):
            for pc in range(2):
                rows = pl.ds(px * 64 + pc * 32, 32)
                pack(lambda b, rows=rows: u_sum[rows, pl.ds(b * 128, 128)], u_last_out.at[c, px, pc], 32, CB)
        for o in (2, 1, 3, 0):
            for oc, pc in both_cores(o):
                px = turn(x, o)
                send("u2", c, u_last_out.at[c, px, pc], here, (px, y, z, pc))
        own = pltpu.make_async_copy(u_last_out.at[c, x, core], here, ls.at[4 + c])
        own.start()
        pending.append(own.wait)

    sent("lz", left_mid.at[:, pl.ds(0, 3)])
    sent("ly", left_in.at[:, 0, 0, pl.ds(0, 3)])
    sent("lg", left_in.at[:, pl.ds(0, 3), 0])
    sent("lc", left_in.at[:, :, 0])
    sent("g1", grad_in.at[pl.ds(0, 224)])
    sent("g2", grad_in.at[pl.ds(0, 768)])
    sent("r1", right_in.at[0, 0, pl.ds(0, 3)])
    sent("rg", right_in.at[pl.ds(0, 3), 0])
    sent("rc", right_in.at[:, 0])
    sent("h1", h_in.at[:, pl.ds(0, 7)])
    sent("h2", h_gather.at[:, pl.ds(0, 3)])
    for name, like in (("p", rot_in), ("d", d_in)):
        pl.when(xh == core)(lambda name=name, like=like: sent(name, like.at[:, pl.ds(0, 3)]))
        pl.when(xh != core)(lambda name=name, like=like: sent(name, like))
    sent("y1", y_in.at[:, pl.ds(0, 3)])
    sent("y2", y_gather.at[:, pl.ds(0, 7)])
    sent("uf", u_far_in)
    sent("u1", u_in)
    for c in range(CC):
        arrive("u2", c, u_last_in.at[c, pl.ds(0, 7)])
    sent("u2", u_last_in.at[:, pl.ds(0, 7)])
    for wait in pending:
        wait()


def finish(coded, first, second, update, new_first, new_second):
    new_first[...] = first[...]
    new_second[...] = second[...]
    for c in range(CC):
        for px in range(4):
            for pc in range(2):
                for b in range(CB):
                    at = pl.ds(pc * 2048 + (c * CB + b) * 512 + px * 128, 128)
                    update[:, at] = unpack(coded.at[c, px * 2 + pc], b, 32, CB)


SEMAPHORES = (
    ("lz", NC), ("ly", NC), ("lg", NC), ("lc", NC), ("g1", 1), ("g2", 3), ("r1", 1), ("rg", 3), ("rc", 1),
    ("h1", NC), ("h2", NC), ("p", NC), ("d", NC), ("y1", NC), ("y2", NC), ("uf", CC), ("u1", CC), ("u2", CC),
)


def body(grad, left_basis, right_basis, first_moment, second_moment):
    vm = pltpu.VMEM
    count = sum(n for _, n in SEMAPHORES)
    scratch = [
        vm((NC, 4, 2 * RC, 128), BF16),
        vm((NC, 4, 2 * RC, 128), BF16),
        vm((NC, 4, 2, 4, 2 * RC, 128), BF16),
        vm((NC, 2, 8 * RC, 1024), BF16),
        vm((NC, 4, 512, 8 * RC), BF16),
        vm((4, 2, 32, 512), BF16),
        vm((1024, 512), BF16),
        vm((4, 256, 128), BF16),
        vm((4, 2, 4, 256, 128), BF16),
        vm((1024, 1024), BF16),
        vm((1024, 1024), BF16),
        vm((NC, 4, 2, 4 * RC + 16, 128), BF16),
        vm((NC, 8, 4 * RC + 16, 128), BF16),
        vm((NC, 4, 8 * RC + 16, 128), BF16),
        vm((RC, 1024), F32),
        vm((4 * RC, 512), F32),
        vm((8 * RC, 1024), BF16),
        vm((4 * RC, 1024), F32),
        vm((NC, 4, 8 * RC + 16, 128), BF16),
        vm((NC, 4, 8 * RC + 16, 128), BF16),
        vm((4 * RC, 256), F32),
        vm((NC, 8 * RC + 16, 128), BF16),
        vm((NC, 4, 8 * RC + 16, 128), BF16),
        vm((8 * RC, 1024), BF16),
        vm((4 * RC, 1024), F32),
        vm((RC, 1024), F32),
        vm((NC, 4, 8 * RC + 16, 128), BF16),
        vm((NC, 4, 8 * RC + 16, 128), BF16),
        vm((NC, 4 * RC + 16, 128), BF16),
        vm((NC, 8, 4 * RC + 16, 128), BF16),
        vm((8 * RC, 512), BF16),
        vm((8 * RC, 512), BF16),
        vm((4, 256, 512), F32),
        vm((256, 128 * CB), F32),
        vm((CC, 2, 128 * CB + 16, 128), BF16),
        vm((CC, 2, 128 * CB + 16, 128), BF16),
        vm((CC, 2, 2, 128 * CB + 16, 128), BF16),
        vm((CC, 2, 2, 128 * CB + 16, 128), BF16),
        vm((CC, 4, 2, 32 * CB + 16, 128), BF16),
        vm((512, 256), F32),
        vm((512, 256), F32),
        vm((512, 256), F32),
        vm((512, 256), F32),
        pltpu.SemaphoreType.DMA((len(SEMAPHORES),)),
        pltpu.SemaphoreType.DMA((count,)),
        pltpu.SemaphoreType.DMA((4 + CC,)),
    ]
    whole = pl.BlockSpec(memory_space=pltpu.VMEM)
    there = pl.BlockSpec(memory_space=pl.ANY)
    square = jax.ShapeDtypeStruct((512, 256), F32)
    coded, new_first, new_second = pl.pallas_call(
        kernel,
        out_shape=(jax.ShapeDtypeStruct((CC, 8, 32 * CB + 16, 128), BF16), square, square),
        in_specs=[whole, whole, whole, there, there],
        out_specs=(there,) * 3,
        scratch_shapes=scratch,
        compiler_params=pltpu.CompilerParams(
            collective_id=0, has_side_effects=True, vmem_limit_bytes=56 * 2**20
        ),
    )(grad, left_basis, right_basis, first_moment, second_moment)
    return pl.pallas_call(
        finish,
        out_shape=(jax.ShapeDtypeStruct((32, 4096), F32), square, square),
        in_specs=[whole] * 3,
        out_specs=(whole,) * 3,
    )(coded, new_first, new_second)


def solution(mesh):
    placed = (
        P(("dp", "tensor"), None),
        P("dp", "tensor"),
        P("dp", "tensor"),
        P("dp", "tensor"),
        P("dp", "tensor"),
    )
    return jax.shard_map(
        body,
        mesh=mesh,
        in_specs=placed,
        out_specs=(P(("dp", "tensor"), None), P("dp", "tensor"), P("dp", "tensor")),
        check_vma=False,
    )
```

```python
import functools

import jax
import jax.numpy as jnp
from jax import lax
from jax.experimental import pallas as pl
from jax.experimental.pallas import tpu as pltpu
from jax.sharding import PartitionSpec as P

STEP = 10
F32 = jnp.float32
BF16 = jnp.bfloat16
MESH = pl.DeviceIdType.MESH

SPAN = 250.0
BASE = 124.0
BOUND = 0.09375


def encode(x, inverse):
    t = jnp.maximum(jnp.abs(x) * inverse, 1e-30)
    y = jnp.exp2((t * lax.rsqrt(t)) * SPAN - BASE)
    return jnp.where(x < 0, -y, y).astype(BF16)


def decode(code, scale):
    y = code.astype(F32)
    t = (jnp.log2(jnp.abs(y)) + BASE) * (1.0 / SPAN)
    v = t * t * scale
    return jnp.where(y < 0, -v, v)


def pack(get, message, rows, blocks):
    most = None
    for b in range(blocks):
        a = jnp.max(jnp.abs(get(b)).reshape(rows // 16, 16, 128), axis=0)
        most = a if most is None else jnp.maximum(most, a)
    scale = (most * 1.01 + 1e-30).astype(BF16)
    message[pl.ds(blocks * rows, 16), :] = scale
    inverse = (1.0 / scale.astype(F32))[None]
    for b in range(blocks):
        code = encode(get(b).reshape(rows // 16, 16, 128), inverse)
        message[pl.ds(b * rows, rows), :] = code.reshape(rows, 128)


def unpack_rows(message, start, rows, end):
    scale = message[pl.ds(end, 16), :].astype(F32)[None]
    code = message[pl.ds(start, rows), :].reshape(rows // 16, 16, 128)
    return decode(code, scale).reshape(rows, 128)


def unpack(message, b, rows, blocks):
    return unpack_rows(message, b * rows, rows, blocks * rows)


def halves(x):
    hi = x.astype(BF16)
    return hi, (x - hi.astype(F32)).astype(BF16)


def dot(a, b):
    return lax.dot_general(a, b, (((1,), (0,)), ((), ())), preferred_element_type=F32)


def dot_t(a, b):
    return lax.dot_general(a, b, (((1,), (1,)), ((), ())), preferred_element_type=F32)


NC = 4
RC = 128 // NC
RIGHT_LATE = True
GRAD_FIRST = False
ORDER = (
    "turned0", "take1", "pass0", "turned1", "forward2", "take2", "turned_sum0", "forward3", "take3", "basis0",
    "turned_sum1", "basis1", "turned2", "rotate0", "turned3", "rotate1", "turned_sum2", "moments0", "flip0",
    "turned_sum3", "moments1", "flip1", "flip2", "rotate2", "back0", "rotate3", "back1", "moments2", "back_sum0",
    "moments3", "back_sum1", "back2", "raise0", "back3", "raise1", "back_sum2", "flip3", "back_sum3", "raise2",
)
CC = 2
CB = 4 // CC


def kernel(
    grad, left, right, first_hbm, second_hbm, u_last_in, first_out, second_out,
    left_out, left_mid, left_in, lt, lf, grad_out, grad_in, right_out, right_in, right_hi, right_lo,
    h_out, h_in, h_gather, h_part, h_block, h_parts, rot_block, rot_out, rot_in, d_block, d_out, d_in, d_parts,
    y_block, y_sum, y_out, y_in, y_gather_out, y_gather, y_hi, y_lo, u_acc, u_sum, u_far_out, u_far_in, u_out, u_in, u_last_out,
    first, second, new_first, new_second, ss, rs, ls,
):
    dp = lax.axis_index("dp")
    tensor = lax.axis_index("tensor")
    y, xh = dp // 2, dp % 2
    z, xl, core = tensor // 4, (tensor // 2) % 2, tensor % 2
    x = xh * 2 + xl
    other = 1 - core

    def device(px, py, pz, pc):
        return (py * 2 + px // 2, pz * 4 + (px % 2) * 2 + pc)

    def turn(a, o):
        return (a + o) % 4

    first_sem, send_sem = {}, {}
    total = 0
    for i, (name, count) in enumerate(SEMAPHORES):
        first_sem[name], send_sem[name] = total, i
        total += count

    def remote(name, j, src, dst, target):
        return pltpu.make_async_remote_copy(
            src_ref=src, dst_ref=dst, send_sem=ss.at[send_sem[name]], recv_sem=rs.at[first_sem[name] + j],
            device_id=device(*target), device_id_type=MESH,
        )

    def send(name, j, src, dst, target):
        remote(name, j, src, dst, target).start()

    def send_unless(own, name, j, src, dst, target):
        pl.when(own)(pltpu.make_async_copy(src, dst, rs.at[first_sem[name] + j]).start)
        pl.when(jnp.logical_not(own))(remote(name, j, src, dst, target).start)

    def arrive(name, j, like):
        pltpu.make_async_copy(like, like, rs.at[first_sem[name] + j]).wait()

    def sent(name, like):
        pltpu.make_async_copy(like, like, ss.at[send_sem[name]]).wait()

    def both_cores(o):
        return [(oc, pc) for oc, pc in ((1, other), (0, core)) if o or oc]

    pending = []
    loads = [pltpu.make_async_copy(first_hbm, first, ls.at[0]), pltpu.make_async_copy(second_hbm, second, ls.at[1])]
    for load in loads:
        load.start()

    barrier = pltpu.get_barrier_semaphore()
    peers = [(turn(x, o), y, z, pc) for o in range(4) for _, pc in both_cores(o)]
    peers += [(x, y, turn(z, o), pc) for o in (1, 2, 3) for _, pc in both_cores(o)]
    peers += [(x, turn(y, o), z, core) for o in (1, 2, 3)]
    for peer in peers:
        pl.semaphore_signal(barrier, inc=1, device_id=device(*peer), device_id_type=MESH)

    for b in range(4):
        code = encode(left[pl.ds(b * 128, 128), :].T, 1.0 / BOUND)
        for a in range(NC):
            for h in range(2):
                left_out[a, b, pl.ds(h * RC, RC), :] = code[h * 128 + a * RC : h * 128 + (a + 1) * RC]
    for px in range(4):
        for pc in range(2):
            for b in range(4):
                grad_out[px, pc, :, pl.ds(b * 128, 128)] = grad[:, pl.ds(pc * 2048 + b * 512 + px * 128, 128)]

    pl.semaphore_wait(barrier, len(peers))

    for a in range(NC):
        for o in (2, 1, 3):
            send("lz", a, left_out.at[a, turn(z, o)], left_mid.at[a, z], (x, y, turn(z, o), core))
        left_mid[a, z] = left_out[a, z]
    own_rows = pl.ds(pl.multiple_of(y * 256 + x * 64 + core * 32, 32), 32)
    for o in (2, 1, 3, 0):
        for oc, pc in both_cores(o):
            px = turn(x, o)
            send("g1", 0, grad_out.at[px, pc], grad_in.at[own_rows], (px, y, z, pc))
    grad_in[own_rows] = grad_out[x, core]
    def ring_start(name, half):
        for up, h, part in ((1, 0, 0), (3, 1, 1), (1, 1, 2), (3, 0, 2)):
            send(name, part, half(y, h), half(y, h), (x, turn(y, up), z, core))

    def ring_pass(name, half):
        for from_, h, to in ((3, 0, 1), (1, 1, 3)):
            piece = half(turn(y, from_), h)
            arrive(name, h, piece)
            send(name, 2, piece, piece, (x, turn(y, to), z, core))

    def grad_half(py, h):
        return grad_in.at[pl.ds(pl.multiple_of(py * 256 + h * 128, 128), 128)]

    def right_half(py, h):
        return right_in.at[py, core, pl.ds(h * 2, 2)]

    def left_turn(a):
        arrive("lz", a, left_mid.at[a, pl.ds(0, 3)])
        for o in (2, 1, 3):
            to = turn(y, o)
            send("ly", a, left_mid.at[a, to], left_in.at[a, x, core, y], (x, to, z, core))
        left_in[a, x, core, y] = left_mid[a, y]

    def left_spread(a):
        piece = left_in.at[a, x, core]
        arrive("ly", a, piece.at[pl.ds(0, 3)])
        for o in (2, 1, 3):
            send("lg", a, piece, piece, (turn(x, o), y, z, core))
        send("lc", a, piece, piece, (x, y, z, other))

    def left_forward(a):
        arrive("lg", a, left_in.at[a, pl.ds(0, 3), core])
        for o in (1, 3, 2):
            piece = left_in.at[a, turn(x, 4 - o), core]
            send("lc", a, piece, piece, (x, y, z, other))

    def left_take(a):
        def one(px, carry, pc):
            for ry in range(4):
                hi, lo = halves(decode(left_in[a, px, pc, ry], BOUND))
                at = pl.ds(pl.multiple_of(ry * 256 + (px // 2) * 128, 128), 128)
                for h in range(2):
                    rows = (pc * 2 + h) * RC
                    lt[a, px % 2, pl.ds(pl.multiple_of(rows, RC), RC), at] = hi[h * RC : (h + 1) * RC]
                    lt[a, px % 2, pl.ds(pl.multiple_of(4 * RC + rows, RC), RC), at] = lo[h * RC : (h + 1) * RC]
            return carry

        lax.fori_loop(0, 4, functools.partial(one, pc=core), 0)
        arrive("lc", a, left_in.at[a, :, other])
        lax.fori_loop(0, 4, functools.partial(one, pc=other), 0)

    def flip(a):
        def one(s, carry):
            at = pl.ds(pl.multiple_of(s * 128, 128), 128)
            for pc in range(2):
                for part in range(2):
                    for sub in range(4 * RC // 128):
                        v = lt[a, pc, pl.ds(part * 4 * RC + sub * 128, 128), at].T
                        to = pl.ds(pl.multiple_of(part * 256 + (s % 2) * 128, 128), 128)
                        lf[a, s // 2, to, pl.ds(pc * 4 * RC + sub * 128, 128)] = v
            return carry

        lax.fori_loop(0, 8, one, 0)

    left_turn(0)
    for q in range(4):
        for b in range(2):
            right_out[q, pl.ds(b * 128, 128), :] = encode(
                right[pl.ds(q * 128, 128), pl.ds(b * 128, 128)], 1.0 / BOUND
            )
    right_in[y, core, x] = right_out[x]
    if GRAD_FIRST:
        arrive("g1", 0, grad_in.at[pl.ds(0, 224)])
        ring_start("g2", grad_half)
    for a in range(1, NC):
        left_turn(a)
    if not GRAD_FIRST:
        arrive("g1", 0, grad_in.at[pl.ds(0, 224)])
        ring_start("g2", grad_half)
    for o in (2, 1, 3):
        px = turn(x, o)
        send("r1", 0, right_out.at[px], right_in.at[y, core, x], (px, y, z, core))
    left_spread(0)
    left_spread(1)
    ring_pass("g2", grad_half)
    arrive("r1", 0, right_in.at[0, 0, pl.ds(0, 3)])
    if not RIGHT_LATE:
        ring_start("rg", right_half)
    send("rc", 0, right_in.at[y, core], right_in.at[y, core], (x, y, z, other))
    left_forward(0)
    left_spread(2)
    left_take(0)
    if RIGHT_LATE:
        ring_start("rg", right_half)
    left_forward(1)
    left_spread(3)
    arrive("g2", 2, grad_in.at[pl.ds(0, 512)])

    def turned(a):
        for oc, pc in ((1, other), (0, core)):
            both = dot(lt[a, pc], grad_in[...])
            h_block[...] = both[0 : 4 * RC] + both[4 * RC : 8 * RC]
            for o in (2, 1, 3, 0):
                pz = turn(z, o)
                rows = pl.ds(pl.multiple_of(pz * RC, RC), RC)
                here = h_in.at[a, z * 2 + core]
                message = h_out.at[a, o, oc] if o or oc else here
                pack(lambda b, rows=rows: h_block[rows, pl.ds(b * 128, 128)], message, RC, 4)
                if o or oc:
                    send("h1", a, message, here, (x, y, pz, pc))

    def turned_sum(a):
        arrive("h1", a, h_in.at[a, pl.ds(0, 7)])

        def one(b, carry):
            for pc in range(2):
                v = None
                for pz in range(4):
                    start = pl.multiple_of(b * RC, RC)
                    term = unpack_rows(h_in.at[a, pz * 2 + pc], start, RC, 4 * RC)
                    v = term if v is None else v + term
                h_part[:, pl.ds(pl.multiple_of(pc * 512 + b * 128, 128), 128)] = v
            return carry

        lax.fori_loop(0, 4, one, 0)
        message = h_gather.at[a, z]
        pack(lambda b: h_part[:, pl.ds(b * 128, 128)], message, RC, 8)
        for o in (2, 1, 3):
            send("h2", a, message, message, (x, y, turn(z, o), core))

    def rotate(a):
        arrive("h2", a, h_gather.at[a, pl.ds(0, 3)])

        def one(pz, carry):
            for b in range(8):
                hi, lo = halves(unpack(h_gather.at[a, pz], b, RC, 8))
                h_parts[pl.ds(pl.multiple_of(pz * RC, RC), RC), pl.ds(b * 128, 128)] = hi
                h_parts[pl.ds(pl.multiple_of((4 + pz) * RC, RC), RC), pl.ds(b * 128, 128)] = lo
            return carry

        lax.fori_loop(0, 4, one, 0)
        for i in range(2):
            at = pl.ds(i * 512, 512)
            both = dot(h_parts[...], right_hi[:, at])
            low = dot(h_parts[pl.ds(0, 4 * RC), :], right_lo[:, at])
            rot_block[:, at] = both[0 : 4 * RC] + both[4 * RC : 8 * RC] + low
        for i in (1, 2, 3, 0):
            jd = turn(xl * 2 + core, i)
            pack(
                lambda b, jd=jd: rot_block[:, pl.ds(pl.multiple_of(jd * 256 + b * 128, 128), 128)],
                rot_out.at[a, i], 4 * RC, 2,
            )
            target = (core * 2 + jd // 2, y, z, jd % 2)
            args = ("p", a, rot_out.at[a, i], rot_in.at[a, x], target)
            if i:
                send(*args)
            else:
                send_unless(xh == core, *args)

    def moments(a):
        if a == 0:
            for load in loads:
                load.wait()
        arrive("p", a, rot_in.at[a])

        def one(pz, carry):
            rows = pl.ds(pl.multiple_of(pz * 128 + a * RC, RC), RC)
            part = pl.ds(pl.multiple_of(pz * RC, RC), RC)
            for b in range(2):
                rot = None
                for px in range(4):
                    start = pl.multiple_of((b * 4 + pz) * RC, RC)
                    term = unpack_rows(rot_in.at[a, px], start, RC, 8 * RC)
                    rot = term if rot is None else rot + term
                at = pl.ds(b * 128, 128)
                moved_first = 0.9 * first[rows, at] + 0.1 * rot
                moved_second = 0.95 * second[rows, at] + 0.05 * rot * rot
                new_first[rows, at] = moved_first
                new_second[rows, at] = moved_second
                d_block[part, at] = (
                    moved_first / (1.0 - 0.9**STEP) / (jnp.sqrt(moved_second / (1.0 - 0.95**STEP)) + 1e-08)
                )
            return carry

        lax.fori_loop(0, 4, one, 0)
        pack(lambda b: d_block[:, pl.ds(b * 128, 128)], d_out.at[a], 4 * RC, 2)
        if a == NC - 1:
            for i, (src, dst) in enumerate(((new_first, first_out), (new_second, second_out))):
                store = pltpu.make_async_copy(src, dst, ls.at[2 + i])
                store.start()
                pending.append(store.wait)
        slot = xl * 2 + core
        for i in (2, 1, 3, 0):
            args = ("d", a, d_out.at[a], d_in.at[a, slot], (turn(x, i), y, z, xh))
            if i:
                send(*args)
            else:
                send_unless(xh == core, *args)

    def back(a):
        arrive("d", a, d_in.at[a])
        for j in range(4):
            for b in range(2):
                hi, lo = halves(unpack(d_in.at[a, j], b, 4 * RC, 2))
                at = pl.ds(j * 256 + b * 128, 128)
                d_parts[pl.ds(0, 4 * RC), at] = hi
                d_parts[pl.ds(4 * RC, 4 * RC), at] = lo

        both = dot_t(d_parts[...], right_hi[...])
        low = dot_t(d_parts[pl.ds(0, 4 * RC), :], right_lo[...])
        y_block[...] = both[0 : 4 * RC] + both[4 * RC : 8 * RC] + low
        for o in (2, 1, 3, 0):
            pz = turn(z, o)
            rows = pl.ds(pl.multiple_of(pz * RC, RC), RC)
            message = y_out.at[a, o] if o else y_in.at[a, z]
            pack(lambda b, rows=rows: y_block[rows, pl.ds(b * 128, 128)], message, RC, 8)
            if o:
                send("y1", a, message, y_in.at[a, z], (x, y, pz, core))

    def back_sum(a):
        arrive("y1", a, y_in.at[a, pl.ds(0, 3)])

        def one(b, carry):
            v = None
            for pz in range(4):
                term = unpack_rows(y_in.at[a, pz], pl.multiple_of(b * RC, RC), RC, 8 * RC)
                v = term if v is None else v + term
            y_sum[:, pl.ds(pl.multiple_of(b * 128, 128), 128)] = v
            return carry

        lax.fori_loop(0, 8, one, 0)
        for oc, pc in ((1, other), (0, core)):
            here = y_gather.at[a, core * 4 + z]
            message = y_gather_out.at[a] if oc else here
            pack(
                lambda b, pc=pc: y_sum[:, pl.ds(pl.multiple_of(pc * 512 + b * 128, 128), 128)], message, RC, 4
            )
            for o in (2, 1, 3, 0):
                if o or oc:
                    send("y2", a, message, here, (x, y, turn(z, o), pc))

    def raised_take(a):
        arrive("y2", a, y_gather.at[a, pl.ds(0, 7)])

        def one(i, carry):
            rows = pl.ds(pl.multiple_of(i * RC, RC), RC)
            for b in range(4):
                hi, lo = halves(unpack(y_gather.at[a, i], b, RC, 4))
                y_hi[rows, pl.ds(b * 128, 128)] = hi
                y_lo[rows, pl.ds(b * 128, 128)] = lo
            return carry

        lax.fori_loop(0, 8, one, 0)

    def raised(a, py):
        both = dot(lf[a, py], y_hi[...])
        v = both[0:256] + both[256:512] + dot(lf[a, py, pl.ds(0, 256), :], y_lo[...])
        u_acc[py] = u_acc[py] + v if a else v

    def right_piece(py, pc):
        def one(px, carry):
            for b in range(2):
                hi, lo = halves(decode(right_in[py, pc, px, pl.ds(b * 128, 128), :], BOUND))
                rows = pl.ds(pl.multiple_of(py * 256 + (px // 2) * 128, 128), 128)
                at = pl.ds(pl.multiple_of((px % 2) * 512 + pc * 256 + b * 128, 128), 128)
                right_hi[rows, at] = hi
                right_lo[rows, at] = lo
            return carry

        lax.fori_loop(0, 4, one, 0)

    def basis_take(part):
        if part == 0:
            arrive("rg", 2, right_in.at[pl.ds(0, 2), core])
            for o in (1, 3, 2):
                piece = right_in.at[turn(y, 4 - o), core]
                send("rc", 0, piece, piece, (x, y, z, other))
            for o in (0, 1, 3, 2):
                right_piece(turn(y, 4 - o), core)
        else:
            arrive("rc", 0, right_in.at[:, other])
            for o in (0, 1, 3, 2):
                right_piece(turn(y, 4 - o), other)

    def raise_all(a):
        raised_take(a)

        def one(py, carry):
            raised(a, py)
            return carry

        lax.fori_loop(0, 4, one, 0)

    steps = {
        "turned": turned, "pass": lambda a: ring_pass("rg", right_half), "forward": left_forward, "take": left_take,
        "turned_sum": turned_sum, "basis": basis_take, "rotate": rotate, "moments": moments, "flip": flip,
        "back": back, "back_sum": back_sum, "raise": raise_all,
    }
    for name in ORDER:
        steps[name[:-1]](int(name[-1]))

    raised_take(NC - 1)
    def rows_of(py, h, c, b):
        return u_acc[py, pl.ds(h * 128, 128), pl.ds((c * CB + b) * 128, 128)]

    def to_neighbour(name, c, h, up, py, message, dst):
        pack(lambda b: rows_of(py, h, c, b), message, 128, CB)
        send(name, c, message, dst, (x, turn(y, up), z, core))

    raised(NC - 1, turn(y, 2))
    for c in range(CC):
        for h, up in ((0, 1), (1, 3)):
            to_neighbour("uf", c, h, up, turn(y, 2), u_far_out.at[c, h], u_far_in.at[c, h])
    raised(NC - 1, turn(y, 1))
    raised(NC - 1, turn(y, 3))
    for c in range(CC):
        for h, up, slot in ((1, 1, 0), (0, 3, 1)):
            to_neighbour("u1", c, h, up, turn(y, up), u_out.at[c, slot, h], u_in.at[c, slot, h])
    for c in range(CC):
        arrive("uf", c, u_far_in.at[c])
        for h, up, slot in ((0, 1, 0), (1, 3, 1)):
            py = turn(y, up)
            for b in range(CB):
                at = pl.ds((c * CB + b) * 128, 128)
                u_acc[py, pl.ds(h * 128, 128), at] += unpack(u_far_in.at[c, h], b, 128, CB)
            to_neighbour("u1", c, h, up, py, u_out.at[c, slot, h], u_in.at[c, slot, h])
    raised(NC - 1, y)
    for c in range(CC):
        arrive("u1", c, u_in.at[c])
        for b in range(CB):
            for h in range(2):
                v = rows_of(y, h, c, b)
                for slot in range(2):
                    v = v + unpack(u_in.at[c, slot, h], b, 128, CB)
                u_sum[pl.ds(h * 128, 128), pl.ds(b * 128, 128)] = v
        here = u_last_in.at[c, x * 2 + core]
        for px in range(4):
            for pc in range(2):
                rows = pl.ds(px * 64 + pc * 32, 32)
                pack(lambda b, rows=rows: u_sum[rows, pl.ds(b * 128, 128)], u_last_out.at[c, px, pc], 32, CB)
        for o in (2, 1, 3, 0):
            for oc, pc in both_cores(o):
                px = turn(x, o)
                send("u2", c, u_last_out.at[c, px, pc], here, (px, y, z, pc))
        own = pltpu.make_async_copy(u_last_out.at[c, x, core], here, ls.at[4 + c])
        own.start()
        pending.append(own.wait)

    sent("lz", left_mid.at[:, pl.ds(0, 3)])
    sent("ly", left_in.at[:, 0, 0, pl.ds(0, 3)])
    sent("lg", left_in.at[:, pl.ds(0, 3), 0])
    sent("lc", left_in.at[:, :, 0])
    sent("g1", grad_in.at[pl.ds(0, 224)])
    sent("g2", grad_in.at[pl.ds(0, 768)])
    sent("r1", right_in.at[0, 0, pl.ds(0, 3)])
    sent("rg", right_in.at[pl.ds(0, 3), 0])
    sent("rc", right_in.at[:, 0])
    sent("h1", h_in.at[:, pl.ds(0, 7)])
    sent("h2", h_gather.at[:, pl.ds(0, 3)])
    for name, like in (("p", rot_in), ("d", d_in)):
        pl.when(xh == core)(lambda name=name, like=like: sent(name, like.at[:, pl.ds(0, 3)]))
        pl.when(xh != core)(lambda name=name, like=like: sent(name, like))
    sent("y1", y_in.at[:, pl.ds(0, 3)])
    sent("y2", y_gather.at[:, pl.ds(0, 7)])
    sent("uf", u_far_in)
    sent("u1", u_in)
    for c in range(CC):
        arrive("u2", c, u_last_in.at[c, pl.ds(0, 7)])
    sent("u2", u_last_in.at[:, pl.ds(0, 7)])
    for wait in pending:
        wait()


def finish(coded, first, second, update, new_first, new_second):
    new_first[...] = first[...]
    new_second[...] = second[...]
    for c in range(CC):
        for px in range(4):
            for pc in range(2):
                for b in range(CB):
                    at = pl.ds(pc * 2048 + (c * CB + b) * 512 + px * 128, 128)
                    update[:, at] = unpack(coded.at[c, px * 2 + pc], b, 32, CB)


SEMAPHORES = (
    ("lz", NC), ("ly", NC), ("lg", NC), ("lc", NC), ("g1", 1), ("g2", 3), ("r1", 1), ("rg", 3), ("rc", 1),
    ("h1", NC), ("h2", NC), ("p", NC), ("d", NC), ("y1", NC), ("y2", NC), ("uf", CC), ("u1", CC), ("u2", CC),
)


def body(grad, left_basis, right_basis, first_moment, second_moment):
    vm = pltpu.VMEM
    count = sum(n for _, n in SEMAPHORES)
    scratch = [
        vm((NC, 4, 2 * RC, 128), BF16),
        vm((NC, 4, 2 * RC, 128), BF16),
        vm((NC, 4, 2, 4, 2 * RC, 128), BF16),
        vm((NC, 2, 8 * RC, 1024), BF16),
        vm((NC, 4, 512, 8 * RC), BF16),
        vm((4, 2, 32, 512), BF16),
        vm((1024, 512), BF16),
        vm((4, 256, 128), BF16),
        vm((4, 2, 4, 256, 128), BF16),
        vm((1024, 1024), BF16),
        vm((1024, 1024), BF16),
        vm((NC, 4, 2, 4 * RC + 16, 128), BF16),
        vm((NC, 8, 4 * RC + 16, 128), BF16),
        vm((NC, 4, 8 * RC + 16, 128), BF16),
        vm((RC, 1024), F32),
        vm((4 * RC, 512), F32),
        vm((8 * RC, 1024), BF16),
        vm((4 * RC, 1024), F32),
        vm((NC, 4, 8 * RC + 16, 128), BF16),
        vm((NC, 4, 8 * RC + 16, 128), BF16),
        vm((4 * RC, 256), F32),
        vm((NC, 8 * RC + 16, 128), BF16),
        vm((NC, 4, 8 * RC + 16, 128), BF16),
        vm((8 * RC, 1024), BF16),
        vm((4 * RC, 1024), F32),
        vm((RC, 1024), F32),
        vm((NC, 4, 8 * RC + 16, 128), BF16),
        vm((NC, 4, 8 * RC + 16, 128), BF16),
        vm((NC, 4 * RC + 16, 128), BF16),
        vm((NC, 8, 4 * RC + 16, 128), BF16),
        vm((8 * RC, 512), BF16),
        vm((8 * RC, 512), BF16),
        vm((4, 256, 512), F32),
        vm((256, 128 * CB), F32),
        vm((CC, 2, 128 * CB + 16, 128), BF16),
        vm((CC, 2, 128 * CB + 16, 128), BF16),
        vm((CC, 2, 2, 128 * CB + 16, 128), BF16),
        vm((CC, 2, 2, 128 * CB + 16, 128), BF16),
        vm((CC, 4, 2, 32 * CB + 16, 128), BF16),
        vm((512, 256), F32),
        vm((512, 256), F32),
        vm((512, 256), F32),
        vm((512, 256), F32),
        pltpu.SemaphoreType.DMA((len(SEMAPHORES),)),
        pltpu.SemaphoreType.DMA((count,)),
        pltpu.SemaphoreType.DMA((4 + CC,)),
    ]
    whole = pl.BlockSpec(memory_space=pltpu.VMEM)
    there = pl.BlockSpec(memory_space=pl.ANY)
    square = jax.ShapeDtypeStruct((512, 256), F32)
    coded, new_first, new_second = pl.pallas_call(
        kernel,
        out_shape=(jax.ShapeDtypeStruct((CC, 8, 32 * CB + 16, 128), BF16), square, square),
        in_specs=[whole, whole, whole, there, there],
        out_specs=(there,) * 3,
        scratch_shapes=scratch,
        compiler_params=pltpu.CompilerParams(
            collective_id=0, has_side_effects=True, vmem_limit_bytes=56 * 2**20
        ),
    )(grad, left_basis, right_basis, first_moment, second_moment)
    return pl.pallas_call(
        finish,
        out_shape=(jax.ShapeDtypeStruct((32, 4096), F32), square, square),
        in_specs=[whole] * 3,
        out_specs=(whole,) * 3,
    )(coded, new_first, new_second)


def solution(mesh):
    placed = (
        P(("dp", "tensor"), None),
        P("dp", "tensor"),
        P("dp", "tensor"),
        P("dp", "tensor"),
        P("dp", "tensor"),
    )
    return jax.shard_map(
        body,
        mesh=mesh,
        in_specs=placed,
        out_specs=(P(("dp", "tensor"), None), P("dp", "tensor"), P("dp", "tensor")),
        check_vma=False,
    )
```

```python
import functools

import jax
import jax.numpy as jnp
from jax import lax
from jax.experimental import pallas as pl
from jax.experimental.pallas import tpu as pltpu
from jax.sharding import PartitionSpec as P

STEP = 10
F32 = jnp.float32
BF16 = jnp.bfloat16
MESH = pl.DeviceIdType.MESH

SPAN = 250.0
BASE = 124.0
BOUND = 0.09375


def encode(x, inverse):
    t = jnp.maximum(jnp.abs(x) * inverse, 1e-30)
    y = jnp.exp2((t * lax.rsqrt(t)) * SPAN - BASE)
    return jnp.where(x < 0, -y, y).astype(BF16)


def decode(code, scale):
    y = code.astype(F32)
    t = (jnp.log2(jnp.abs(y)) + BASE) * (1.0 / SPAN)
    v = t * t * scale
    return jnp.where(y < 0, -v, v)


def pack(get, message, rows, blocks):
    most = None
    for b in range(blocks):
        a = jnp.max(jnp.abs(get(b)).reshape(rows // 16, 16, 128), axis=0)
        most = a if most is None else jnp.maximum(most, a)
    scale = (most * 1.01 + 1e-30).astype(BF16)
    message[pl.ds(blocks * rows, 16), :] = scale
    inverse = (1.0 / scale.astype(F32))[None]
    for b in range(blocks):
        code = encode(get(b).reshape(rows // 16, 16, 128), inverse)
        message[pl.ds(b * rows, rows), :] = code.reshape(rows, 128)


def unpack_rows(message, start, rows, end):
    scale = message[pl.ds(end, 16), :].astype(F32)[None]
    code = message[pl.ds(start, rows), :].reshape(rows // 16, 16, 128)
    return decode(code, scale).reshape(rows, 128)


def unpack(message, b, rows, blocks):
    return unpack_rows(message, b * rows, rows, blocks * rows)


def halves(x):
    hi = x.astype(BF16)
    return hi, (x - hi.astype(F32)).astype(BF16)


def dot(a, b):
    return lax.dot_general(a, b, (((1,), (0,)), ((), ())), preferred_element_type=F32)


def dot_t(a, b):
    return lax.dot_general(a, b, (((1,), (1,)), ((), ())), preferred_element_type=F32)


NC = 4
RC = 128 // NC
RIGHT_LATE = True
GRAD_FIRST = False
ORDER = (
    "turned0", "take1", "turned1", "pass0", "forward2", "take2", "turned_sum0", "forward3", "take3", "turned_sum1",
    "turned2", "basis0", "basis1", "rotate0", "turned3", "rotate1", "turned_sum2", "flip0", "moments0",
    "turned_sum3", "flip1", "moments1", "rotate2", "back0", "rotate3", "back1", "moments2", "flip2", "back_sum0",
    "flip3", "moments3", "back_sum1", "back2", "back3", "raise0", "back_sum2", "raise1", "back_sum3", "raise2",
)
CC = 2
CB = 4 // CC


def kernel(
    grad, left, right, first_hbm, second_hbm, u_last_in, first_out, second_out,
    left_out, left_mid, left_in, lt, lf, grad_out, grad_in, right_out, right_in, right_hi, right_lo,
    h_out, h_in, h_gather, h_part, h_block, h_parts, rot_block, rot_out, rot_in, d_block, d_out, d_in, d_parts,
    y_block, y_sum, y_out, y_in, y_gather_out, y_gather, y_hi, y_lo, u_acc, u_sum, u_far_out, u_far_in, u_out, u_in, u_last_out,
    first, second, new_first, new_second, ss, rs, ls,
):
    dp = lax.axis_index("dp")
    tensor = lax.axis_index("tensor")
    y, xh = dp // 2, dp % 2
    z, xl, core = tensor // 4, (tensor // 2) % 2, tensor % 2
    x = xh * 2 + xl
    other = 1 - core

    def device(px, py, pz, pc):
        return (py * 2 + px // 2, pz * 4 + (px % 2) * 2 + pc)

    def turn(a, o):
        return (a + o) % 4

    first_sem, send_sem = {}, {}
    total = 0
    for i, (name, count) in enumerate(SEMAPHORES):
        first_sem[name], send_sem[name] = total, i
        total += count

    def remote(name, j, src, dst, target):
        return pltpu.make_async_remote_copy(
            src_ref=src, dst_ref=dst, send_sem=ss.at[send_sem[name]], recv_sem=rs.at[first_sem[name] + j],
            device_id=device(*target), device_id_type=MESH,
        )

    def send(name, j, src, dst, target):
        remote(name, j, src, dst, target).start()

    def send_unless(own, name, j, src, dst, target):
        pl.when(own)(pltpu.make_async_copy(src, dst, rs.at[first_sem[name] + j]).start)
        pl.when(jnp.logical_not(own))(remote(name, j, src, dst, target).start)

    def arrive(name, j, like):
        pltpu.make_async_copy(like, like, rs.at[first_sem[name] + j]).wait()

    def sent(name, like):
        pltpu.make_async_copy(like, like, ss.at[send_sem[name]]).wait()

    def both_cores(o):
        return [(oc, pc) for oc, pc in ((1, other), (0, core)) if o or oc]

    pending = []
    loads = [pltpu.make_async_copy(first_hbm, first, ls.at[0]), pltpu.make_async_copy(second_hbm, second, ls.at[1])]
    for load in loads:
        load.start()

    barrier = pltpu.get_barrier_semaphore()
    peers = [(turn(x, o), y, z, pc) for o in range(4) for _, pc in both_cores(o)]
    peers += [(x, y, turn(z, o), pc) for o in (1, 2, 3) for _, pc in both_cores(o)]
    peers += [(x, turn(y, o), z, core) for o in (1, 2, 3)]
    for peer in peers:
        pl.semaphore_signal(barrier, inc=1, device_id=device(*peer), device_id_type=MESH)

    for b in range(4):
        code = encode(left[pl.ds(b * 128, 128), :].T, 1.0 / BOUND)
        for a in range(NC):
            for h in range(2):
                left_out[a, b, pl.ds(h * RC, RC), :] = code[h * 128 + a * RC : h * 128 + (a + 1) * RC]
    for px in range(4):
        for pc in range(2):
            for b in range(4):
                grad_out[px, pc, :, pl.ds(b * 128, 128)] = grad[:, pl.ds(pc * 2048 + b * 512 + px * 128, 128)]

    pl.semaphore_wait(barrier, len(peers))

    for a in range(NC):
        for o in (2, 1, 3):
            send("lz", a, left_out.at[a, turn(z, o)], left_mid.at[a, z], (x, y, turn(z, o), core))
        left_mid[a, z] = left_out[a, z]
    own_rows = pl.ds(pl.multiple_of(y * 256 + x * 64 + core * 32, 32), 32)
    for o in (2, 1, 3, 0):
        for oc, pc in both_cores(o):
            px = turn(x, o)
            send("g1", 0, grad_out.at[px, pc], grad_in.at[own_rows], (px, y, z, pc))
    grad_in[own_rows] = grad_out[x, core]
    def ring_start(name, half):
        for up, h, part in ((1, 0, 0), (3, 1, 1), (1, 1, 2), (3, 0, 2)):
            send(name, part, half(y, h), half(y, h), (x, turn(y, up), z, core))

    def ring_pass(name, half):
        for from_, h, to in ((3, 0, 1), (1, 1, 3)):
            piece = half(turn(y, from_), h)
            arrive(name, h, piece)
            send(name, 2, piece, piece, (x, turn(y, to), z, core))

    def grad_half(py, h):
        return grad_in.at[pl.ds(pl.multiple_of(py * 256 + h * 128, 128), 128)]

    def right_half(py, h):
        return right_in.at[py, core, pl.ds(h * 2, 2)]

    def left_turn(a):
        arrive("lz", a, left_mid.at[a, pl.ds(0, 3)])
        for o in (2, 1, 3):
            to = turn(y, o)
            send("ly", a, left_mid.at[a, to], left_in.at[a, x, core, y], (x, to, z, core))
        left_in[a, x, core, y] = left_mid[a, y]

    def left_spread(a):
        piece = left_in.at[a, x, core]
        arrive("ly", a, piece.at[pl.ds(0, 3)])
        for o in (2, 1, 3):
            send("lg", a, piece, piece, (turn(x, o), y, z, core))
        send("lc", a, piece, piece, (x, y, z, other))

    def left_forward(a):
        arrive("lg", a, left_in.at[a, pl.ds(0, 3), core])
        for o in (1, 3, 2):
            piece = left_in.at[a, turn(x, 4 - o), core]
            send("lc", a, piece, piece, (x, y, z, other))

    def left_take(a):
        def one(px, carry, pc):
            for ry in range(4):
                hi, lo = halves(decode(left_in[a, px, pc, ry], BOUND))
                at = pl.ds(pl.multiple_of(ry * 256 + (px // 2) * 128, 128), 128)
                for h in range(2):
                    rows = (pc * 2 + h) * RC
                    lt[a, px % 2, pl.ds(pl.multiple_of(rows, RC), RC), at] = hi[h * RC : (h + 1) * RC]
                    lt[a, px % 2, pl.ds(pl.multiple_of(4 * RC + rows, RC), RC), at] = lo[h * RC : (h + 1) * RC]
            return carry

        lax.fori_loop(0, 4, functools.partial(one, pc=core), 0)
        arrive("lc", a, left_in.at[a, :, other])
        lax.fori_loop(0, 4, functools.partial(one, pc=other), 0)

    def flip(a):
        def one(s, carry):
            at = pl.ds(pl.multiple_of(s * 128, 128), 128)
            for pc in range(2):
                for part in range(2):
                    for sub in range(4 * RC // 128):
                        v = lt[a, pc, pl.ds(part * 4 * RC + sub * 128, 128), at].T
                        to = pl.ds(pl.multiple_of(part * 256 + (s % 2) * 128, 128), 128)
                        lf[a, s // 2, to, pl.ds(pc * 4 * RC + sub * 128, 128)] = v
            return carry

        lax.fori_loop(0, 8, one, 0)

    left_turn(0)
    for q in range(4):
        for b in range(2):
            right_out[q, pl.ds(b * 128, 128), :] = encode(
                right[pl.ds(q * 128, 128), pl.ds(b * 128, 128)], 1.0 / BOUND
            )
    right_in[y, core, x] = right_out[x]
    if GRAD_FIRST:
        arrive("g1", 0, grad_in.at[pl.ds(0, 224)])
        ring_start("g2", grad_half)
    for a in range(1, NC):
        left_turn(a)
    if not GRAD_FIRST:
        arrive("g1", 0, grad_in.at[pl.ds(0, 224)])
        ring_start("g2", grad_half)
    for o in (2, 1, 3):
        px = turn(x, o)
        send("r1", 0, right_out.at[px], right_in.at[y, core, x], (px, y, z, core))
    left_spread(0)
    left_spread(1)
    ring_pass("g2", grad_half)
    arrive("r1", 0, right_in.at[0, 0, pl.ds(0, 3)])
    if not RIGHT_LATE:
        ring_start("rg", right_half)
    send("rc", 0, right_in.at[y, core], right_in.at[y, core], (x, y, z, other))
    left_forward(0)
    left_spread(2)
    left_take(0)
    if RIGHT_LATE:
        ring_start("rg", right_half)
    left_forward(1)
    left_spread(3)
    arrive("g2", 2, grad_in.at[pl.ds(0, 512)])

    def turned(a):
        for oc, pc in ((1, other), (0, core)):
            both = dot(lt[a, pc], grad_in[...])
            h_block[...] = both[0 : 4 * RC] + both[4 * RC : 8 * RC]
            for o in (2, 1, 3, 0):
                pz = turn(z, o)
                rows = pl.ds(pl.multiple_of(pz * RC, RC), RC)
                here = h_in.at[a, z * 2 + core]
                message = h_out.at[a, o, oc] if o or oc else here
                pack(lambda b, rows=rows: h_block[rows, pl.ds(b * 128, 128)], message, RC, 4)
                if o or oc:
                    send("h1", a, message, here, (x, y, pz, pc))

    def turned_sum(a):
        arrive("h1", a, h_in.at[a, pl.ds(0, 7)])

        def one(b, carry):
            for pc in range(2):
                v = None
                for pz in range(4):
                    start = pl.multiple_of(b * RC, RC)
                    term = unpack_rows(h_in.at[a, pz * 2 + pc], start, RC, 4 * RC)
                    v = term if v is None else v + term
                h_part[:, pl.ds(pl.multiple_of(pc * 512 + b * 128, 128), 128)] = v
            return carry

        lax.fori_loop(0, 4, one, 0)
        message = h_gather.at[a, z]
        pack(lambda b: h_part[:, pl.ds(b * 128, 128)], message, RC, 8)
        for o in (2, 1, 3):
            send("h2", a, message, message, (x, y, turn(z, o), core))

    def rotate(a):
        arrive("h2", a, h_gather.at[a, pl.ds(0, 3)])

        def one(pz, carry):
            for b in range(8):
                hi, lo = halves(unpack(h_gather.at[a, pz], b, RC, 8))
                h_parts[pl.ds(pl.multiple_of(pz * RC, RC), RC), pl.ds(b * 128, 128)] = hi
                h_parts[pl.ds(pl.multiple_of((4 + pz) * RC, RC), RC), pl.ds(b * 128, 128)] = lo
            return carry

        lax.fori_loop(0, 4, one, 0)
        for i in range(2):
            at = pl.ds(i * 512, 512)
            both = dot(h_parts[...], right_hi[:, at])
            low = dot(h_parts[pl.ds(0, 4 * RC), :], right_lo[:, at])
            rot_block[:, at] = both[0 : 4 * RC] + both[4 * RC : 8 * RC] + low
        for i in (1, 2, 3, 0):
            jd = turn(xl * 2 + core, i)
            pack(
                lambda b, jd=jd: rot_block[:, pl.ds(pl.multiple_of(jd * 256 + b * 128, 128), 128)],
                rot_out.at[a, i], 4 * RC, 2,
            )
            target = (core * 2 + jd // 2, y, z, jd % 2)
            args = ("p", a, rot_out.at[a, i], rot_in.at[a, x], target)
            if i:
                send(*args)
            else:
                send_unless(xh == core, *args)

    def moments(a):
        if a == 0:
            for load in loads:
                load.wait()
        arrive("p", a, rot_in.at[a])

        def one(pz, carry):
            rows = pl.ds(pl.multiple_of(pz * 128 + a * RC, RC), RC)
            part = pl.ds(pl.multiple_of(pz * RC, RC), RC)
            for b in range(2):
                rot = None
                for px in range(4):
                    start = pl.multiple_of((b * 4 + pz) * RC, RC)
                    term = unpack_rows(rot_in.at[a, px], start, RC, 8 * RC)
                    rot = term if rot is None else rot + term
                at = pl.ds(b * 128, 128)
                moved_first = 0.9 * first[rows, at] + 0.1 * rot
                moved_second = 0.95 * second[rows, at] + 0.05 * rot * rot
                new_first[rows, at] = moved_first
                new_second[rows, at] = moved_second
                d_block[part, at] = (
                    moved_first / (1.0 - 0.9**STEP) / (jnp.sqrt(moved_second / (1.0 - 0.95**STEP)) + 1e-08)
                )
            return carry

        lax.fori_loop(0, 4, one, 0)
        pack(lambda b: d_block[:, pl.ds(b * 128, 128)], d_out.at[a], 4 * RC, 2)
        if a == NC - 1:
            for i, (src, dst) in enumerate(((new_first, first_out), (new_second, second_out))):
                store = pltpu.make_async_copy(src, dst, ls.at[2 + i])
                store.start()
                pending.append(store.wait)
        slot = xl * 2 + core
        for i in (2, 1, 3, 0):
            args = ("d", a, d_out.at[a], d_in.at[a, slot], (turn(x, i), y, z, xh))
            if i:
                send(*args)
            else:
                send_unless(xh == core, *args)

    def back(a):
        arrive("d", a, d_in.at[a])
        for j in range(4):
            for b in range(2):
                hi, lo = halves(unpack(d_in.at[a, j], b, 4 * RC, 2))
                at = pl.ds(j * 256 + b * 128, 128)
                d_parts[pl.ds(0, 4 * RC), at] = hi
                d_parts[pl.ds(4 * RC, 4 * RC), at] = lo

        both = dot_t(d_parts[...], right_hi[...])
        low = dot_t(d_parts[pl.ds(0, 4 * RC), :], right_lo[...])
        y_block[...] = both[0 : 4 * RC] + both[4 * RC : 8 * RC] + low
        for o in (2, 1, 3, 0):
            pz = turn(z, o)
            rows = pl.ds(pl.multiple_of(pz * RC, RC), RC)
            message = y_out.at[a, o] if o else y_in.at[a, z]
            pack(lambda b, rows=rows: y_block[rows, pl.ds(b * 128, 128)], message, RC, 8)
            if o:
                send("y1", a, message, y_in.at[a, z], (x, y, pz, core))

    def back_sum(a):
        arrive("y1", a, y_in.at[a, pl.ds(0, 3)])

        def one(b, carry):
            v = None
            for pz in range(4):
                term = unpack_rows(y_in.at[a, pz], pl.multiple_of(b * RC, RC), RC, 8 * RC)
                v = term if v is None else v + term
            y_sum[:, pl.ds(pl.multiple_of(b * 128, 128), 128)] = v
            return carry

        lax.fori_loop(0, 8, one, 0)
        for oc, pc in ((1, other), (0, core)):
            here = y_gather.at[a, core * 4 + z]
            message = y_gather_out.at[a] if oc else here
            pack(
                lambda b, pc=pc: y_sum[:, pl.ds(pl.multiple_of(pc * 512 + b * 128, 128), 128)], message, RC, 4
            )
            for o in (2, 1, 3, 0):
                if o or oc:
                    send("y2", a, message, here, (x, y, turn(z, o), pc))

    def raised_take(a):
        arrive("y2", a, y_gather.at[a, pl.ds(0, 7)])

        def one(i, carry):
            rows = pl.ds(pl.multiple_of(i * RC, RC), RC)
            for b in range(4):
                hi, lo = halves(unpack(y_gather.at[a, i], b, RC, 4))
                y_hi[rows, pl.ds(b * 128, 128)] = hi
                y_lo[rows, pl.ds(b * 128, 128)] = lo
            return carry

        lax.fori_loop(0, 8, one, 0)

    def raised(a, py):
        both = dot(lf[a, py], y_hi[...])
        v = both[0:256] + both[256:512] + dot(lf[a, py, pl.ds(0, 256), :], y_lo[...])
        u_acc[py] = u_acc[py] + v if a else v

    def right_piece(py, pc):
        def one(px, carry):
            for b in range(2):
                hi, lo = halves(decode(right_in[py, pc, px, pl.ds(b * 128, 128), :], BOUND))
                rows = pl.ds(pl.multiple_of(py * 256 + (px // 2) * 128, 128), 128)
                at = pl.ds(pl.multiple_of((px % 2) * 512 + pc * 256 + b * 128, 128), 128)
                right_hi[rows, at] = hi
                right_lo[rows, at] = lo
            return carry

        lax.fori_loop(0, 4, one, 0)

    def basis_take(part):
        if part == 0:
            arrive("rg", 2, right_in.at[pl.ds(0, 2), core])
            for o in (1, 3, 2):
                piece = right_in.at[turn(y, 4 - o), core]
                send("rc", 0, piece, piece, (x, y, z, other))
            for o in (0, 1, 3, 2):
                right_piece(turn(y, 4 - o), core)
        else:
            arrive("rc", 0, right_in.at[:, other])
            for o in (0, 1, 3, 2):
                right_piece(turn(y, 4 - o), other)

    def raise_all(a):
        raised_take(a)

        def one(py, carry):
            raised(a, py)
            return carry

        lax.fori_loop(0, 4, one, 0)

    steps = {
        "turned": turned, "pass": lambda a: ring_pass("rg", right_half), "forward": left_forward, "take": left_take,
        "turned_sum": turned_sum, "basis": basis_take, "rotate": rotate, "moments": moments, "flip": flip,
        "back": back, "back_sum": back_sum, "raise": raise_all,
    }
    for name in ORDER:
        steps[name[:-1]](int(name[-1]))

    raised_take(NC - 1)
    def rows_of(py, h, c, b):
        return u_acc[py, pl.ds(h * 128, 128), pl.ds((c * CB + b) * 128, 128)]

    def to_neighbour(name, c, h, up, py, message, dst):
        pack(lambda b: rows_of(py, h, c, b), message, 128, CB)
        send(name, c, message, dst, (x, turn(y, up), z, core))

    raised(NC - 1, turn(y, 2))
    for c in range(CC):
        for h, up in ((0, 1), (1, 3)):
            to_neighbour("uf", c, h, up, turn(y, 2), u_far_out.at[c, h], u_far_in.at[c, h])
    raised(NC - 1, turn(y, 1))
    raised(NC - 1, turn(y, 3))
    for c in range(CC):
        for h, up, slot in ((1, 1, 0), (0, 3, 1)):
            to_neighbour("u1", c, h, up, turn(y, up), u_out.at[c, slot, h], u_in.at[c, slot, h])
    for c in range(CC):
        arrive("uf", c, u_far_in.at[c])
        for h, up, slot in ((0, 1, 0), (1, 3, 1)):
            py = turn(y, up)
            for b in range(CB):
                at = pl.ds((c * CB + b) * 128, 128)
                u_acc[py, pl.ds(h * 128, 128), at] += unpack(u_far_in.at[c, h], b, 128, CB)
            to_neighbour("u1", c, h, up, py, u_out.at[c, slot, h], u_in.at[c, slot, h])
    raised(NC - 1, y)
    for c in range(CC):
        arrive("u1", c, u_in.at[c])
        for b in range(CB):
            for h in range(2):
                v = rows_of(y, h, c, b)
                for slot in range(2):
                    v = v + unpack(u_in.at[c, slot, h], b, 128, CB)
                u_sum[pl.ds(h * 128, 128), pl.ds(b * 128, 128)] = v
        here = u_last_in.at[c, x * 2 + core]
        for px in range(4):
            for pc in range(2):
                rows = pl.ds(px * 64 + pc * 32, 32)
                pack(lambda b, rows=rows: u_sum[rows, pl.ds(b * 128, 128)], u_last_out.at[c, px, pc], 32, CB)
        for o in (2, 1, 3, 0):
            for oc, pc in both_cores(o):
                px = turn(x, o)
                send("u2", c, u_last_out.at[c, px, pc], here, (px, y, z, pc))
        own = pltpu.make_async_copy(u_last_out.at[c, x, core], here, ls.at[4 + c])
        own.start()
        pending.append(own.wait)

    sent("lz", left_mid.at[:, pl.ds(0, 3)])
    sent("ly", left_in.at[:, 0, 0, pl.ds(0, 3)])
    sent("lg", left_in.at[:, pl.ds(0, 3), 0])
    sent("lc", left_in.at[:, :, 0])
    sent("g1", grad_in.at[pl.ds(0, 224)])
    sent("g2", grad_in.at[pl.ds(0, 768)])
    sent("r1", right_in.at[0, 0, pl.ds(0, 3)])
    sent("rg", right_in.at[pl.ds(0, 3), 0])
    sent("rc", right_in.at[:, 0])
    sent("h1", h_in.at[:, pl.ds(0, 7)])
    sent("h2", h_gather.at[:, pl.ds(0, 3)])
    for name, like in (("p", rot_in), ("d", d_in)):
        pl.when(xh == core)(lambda name=name, like=like: sent(name, like.at[:, pl.ds(0, 3)]))
        pl.when(xh != core)(lambda name=name, like=like: sent(name, like))
    sent("y1", y_in.at[:, pl.ds(0, 3)])
    sent("y2", y_gather.at[:, pl.ds(0, 7)])
    sent("uf", u_far_in)
    sent("u1", u_in)
    for c in range(CC):
        arrive("u2", c, u_last_in.at[c, pl.ds(0, 7)])
    sent("u2", u_last_in.at[:, pl.ds(0, 7)])
    for wait in pending:
        wait()


def finish(coded, first, second, update, new_first, new_second):
    new_first[...] = first[...]
    new_second[...] = second[...]
    for c in range(CC):
        for px in range(4):
            for pc in range(2):
                for b in range(CB):
                    at = pl.ds(pc * 2048 + (c * CB + b) * 512 + px * 128, 128)
                    update[:, at] = unpack(coded.at[c, px * 2 + pc], b, 32, CB)


SEMAPHORES = (
    ("lz", NC), ("ly", NC), ("lg", NC), ("lc", NC), ("g1", 1), ("g2", 3), ("r1", 1), ("rg", 3), ("rc", 1),
    ("h1", NC), ("h2", NC), ("p", NC), ("d", NC), ("y1", NC), ("y2", NC), ("uf", CC), ("u1", CC), ("u2", CC),
)


def body(grad, left_basis, right_basis, first_moment, second_moment):
    vm = pltpu.VMEM
    count = sum(n for _, n in SEMAPHORES)
    scratch = [
        vm((NC, 4, 2 * RC, 128), BF16),
        vm((NC, 4, 2 * RC, 128), BF16),
        vm((NC, 4, 2, 4, 2 * RC, 128), BF16),
        vm((NC, 2, 8 * RC, 1024), BF16),
        vm((NC, 4, 512, 8 * RC), BF16),
        vm((4, 2, 32, 512), BF16),
        vm((1024, 512), BF16),
        vm((4, 256, 128), BF16),
        vm((4, 2, 4, 256, 128), BF16),
        vm((1024, 1024), BF16),
        vm((1024, 1024), BF16),
        vm((NC, 4, 2, 4 * RC + 16, 128), BF16),
        vm((NC, 8, 4 * RC + 16, 128), BF16),
        vm((NC, 4, 8 * RC + 16, 128), BF16),
        vm((RC, 1024), F32),
        vm((4 * RC, 512), F32),
        vm((8 * RC, 1024), BF16),
        vm((4 * RC, 1024), F32),
        vm((NC, 4, 8 * RC + 16, 128), BF16),
        vm((NC, 4, 8 * RC + 16, 128), BF16),
        vm((4 * RC, 256), F32),
        vm((NC, 8 * RC + 16, 128), BF16),
        vm((NC, 4, 8 * RC + 16, 128), BF16),
        vm((8 * RC, 1024), BF16),
        vm((4 * RC, 1024), F32),
        vm((RC, 1024), F32),
        vm((NC, 4, 8 * RC + 16, 128), BF16),
        vm((NC, 4, 8 * RC + 16, 128), BF16),
        vm((NC, 4 * RC + 16, 128), BF16),
        vm((NC, 8, 4 * RC + 16, 128), BF16),
        vm((8 * RC, 512), BF16),
        vm((8 * RC, 512), BF16),
        vm((4, 256, 512), F32),
        vm((256, 128 * CB), F32),
        vm((CC, 2, 128 * CB + 16, 128), BF16),
        vm((CC, 2, 128 * CB + 16, 128), BF16),
        vm((CC, 2, 2, 128 * CB + 16, 128), BF16),
        vm((CC, 2, 2, 128 * CB + 16, 128), BF16),
        vm((CC, 4, 2, 32 * CB + 16, 128), BF16),
        vm((512, 256), F32),
        vm((512, 256), F32),
        vm((512, 256), F32),
        vm((512, 256), F32),
        pltpu.SemaphoreType.DMA((len(SEMAPHORES),)),
        pltpu.SemaphoreType.DMA((count,)),
        pltpu.SemaphoreType.DMA((4 + CC,)),
    ]
    whole = pl.BlockSpec(memory_space=pltpu.VMEM)
    there = pl.BlockSpec(memory_space=pl.ANY)
    square = jax.ShapeDtypeStruct((512, 256), F32)
    coded, new_first, new_second = pl.pallas_call(
        kernel,
        out_shape=(jax.ShapeDtypeStruct((CC, 8, 32 * CB + 16, 128), BF16), square, square),
        in_specs=[whole, whole, whole, there, there],
        out_specs=(there,) * 3,
        scratch_shapes=scratch,
        compiler_params=pltpu.CompilerParams(
            collective_id=0, has_side_effects=True, vmem_limit_bytes=56 * 2**20
        ),
    )(grad, left_basis, right_basis, first_moment, second_moment)
    return pl.pallas_call(
        finish,
        out_shape=(jax.ShapeDtypeStruct((32, 4096), F32), square, square),
        in_specs=[whole] * 3,
        out_specs=(whole,) * 3,
    )(coded, new_first, new_second)


def solution(mesh):
    placed = (
        P(("dp", "tensor"), None),
        P("dp", "tensor"),
        P("dp", "tensor"),
        P("dp", "tensor"),
        P("dp", "tensor"),
    )
    return jax.shard_map(
        body,
        mesh=mesh,
        in_specs=placed,
        out_specs=(P(("dp", "tensor"), None), P("dp", "tensor"), P("dp", "tensor")),
        check_vma=False,
    )
```

```python
import functools

import jax
import jax.numpy as jnp
from jax import lax
from jax.experimental import pallas as pl
from jax.experimental.pallas import tpu as pltpu
from jax.sharding import PartitionSpec as P

STEP = 10
F32 = jnp.float32
BF16 = jnp.bfloat16
MESH = pl.DeviceIdType.MESH

SPAN = 250.0
BASE = 124.0
BOUND = 0.09375


def encode(x, inverse):
    t = jnp.maximum(jnp.abs(x) * inverse, 1e-30)
    y = jnp.exp2((t * lax.rsqrt(t)) * SPAN - BASE)
    return jnp.where(x < 0, -y, y).astype(BF16)


def decode(code, scale):
    y = code.astype(F32)
    t = (jnp.log2(jnp.abs(y)) + BASE) * (1.0 / SPAN)
    v = t * t * scale
    return jnp.where(y < 0, -v, v)


def pack(get, message, rows, blocks):
    most = None
    for b in range(blocks):
        a = jnp.max(jnp.abs(get(b)).reshape(rows // 16, 16, 128), axis=0)
        most = a if most is None else jnp.maximum(most, a)
    scale = (most * 1.01 + 1e-30).astype(BF16)
    message[pl.ds(blocks * rows, 16), :] = scale
    inverse = (1.0 / scale.astype(F32))[None]
    for b in range(blocks):
        code = encode(get(b).reshape(rows // 16, 16, 128), inverse)
        message[pl.ds(b * rows, rows), :] = code.reshape(rows, 128)


def unpack_rows(message, start, rows, end):
    scale = message[pl.ds(end, 16), :].astype(F32)[None]
    code = message[pl.ds(start, rows), :].reshape(rows // 16, 16, 128)
    return decode(code, scale).reshape(rows, 128)


def unpack(message, b, rows, blocks):
    return unpack_rows(message, b * rows, rows, blocks * rows)


def halves(x):
    hi = x.astype(BF16)
    return hi, (x - hi.astype(F32)).astype(BF16)


def dot(a, b):
    return lax.dot_general(a, b, (((1,), (0,)), ((), ())), preferred_element_type=F32)


def dot_t(a, b):
    return lax.dot_general(a, b, (((1,), (1,)), ((), ())), preferred_element_type=F32)


NC = 4
RC = 128 // NC
RIGHT_LATE = True
GRAD_FIRST = False
ORDER = (
    "turned0", "take1", "turned1", "pass0", "forward2", "take2", "turned_sum0", "forward3", "take3", "turned_sum1",
    "turned2", "basis0", "basis1", "rotate0", "turned3", "rotate1", "turned_sum2", "flip0", "moments0",
    "turned_sum3", "flip1", "moments1", "rotate2", "rotate3", "back0", "back1", "moments2", "flip2", "back_sum0",
    "flip3", "moments3", "back_sum1", "back2", "back3", "raise0", "back_sum2", "raise1", "back_sum3", "raise2",
)
CC = 2
CB = 4 // CC


def kernel(
    grad, left, right, first_hbm, second_hbm, u_last_in, first_out, second_out,
    left_out, left_mid, left_in, lt, lf, grad_out, grad_in, right_out, right_in, right_hi, right_lo,
    h_out, h_in, h_gather, h_part, h_block, h_parts, rot_block, rot_out, rot_in, d_block, d_out, d_in, d_parts,
    y_block, y_sum, y_out, y_in, y_gather_out, y_gather, y_hi, y_lo, u_acc, u_sum, u_far_out, u_far_in, u_out, u_in, u_last_out,
    first, second, new_first, new_second, ss, rs, ls,
):
    dp = lax.axis_index("dp")
    tensor = lax.axis_index("tensor")
    y, xh = dp // 2, dp % 2
    z, xl, core = tensor // 4, (tensor // 2) % 2, tensor % 2
    x = xh * 2 + xl
    other = 1 - core

    def device(px, py, pz, pc):
        return (py * 2 + px // 2, pz * 4 + (px % 2) * 2 + pc)

    def turn(a, o):
        return (a + o) % 4

    first_sem, send_sem = {}, {}
    total = 0
    for i, (name, count) in enumerate(SEMAPHORES):
        first_sem[name], send_sem[name] = total, i
        total += count

    def remote(name, j, src, dst, target):
        return pltpu.make_async_remote_copy(
            src_ref=src, dst_ref=dst, send_sem=ss.at[send_sem[name]], recv_sem=rs.at[first_sem[name] + j],
            device_id=device(*target), device_id_type=MESH,
        )

    def send(name, j, src, dst, target):
        remote(name, j, src, dst, target).start()

    def send_unless(own, name, j, src, dst, target):
        pl.when(own)(pltpu.make_async_copy(src, dst, rs.at[first_sem[name] + j]).start)
        pl.when(jnp.logical_not(own))(remote(name, j, src, dst, target).start)

    def arrive(name, j, like):
        pltpu.make_async_copy(like, like, rs.at[first_sem[name] + j]).wait()

    def sent(name, like):
        pltpu.make_async_copy(like, like, ss.at[send_sem[name]]).wait()

    def both_cores(o):
        return [(oc, pc) for oc, pc in ((1, other), (0, core)) if o or oc]

    pending = []
    loads = [pltpu.make_async_copy(first_hbm, first, ls.at[0]), pltpu.make_async_copy(second_hbm, second, ls.at[1])]
    for load in loads:
        load.start()

    barrier = pltpu.get_barrier_semaphore()
    peers = [(turn(x, o), y, z, pc) for o in range(4) for _, pc in both_cores(o)]
    peers += [(x, y, turn(z, o), pc) for o in (1, 2, 3) for _, pc in both_cores(o)]
    peers += [(x, turn(y, o), z, core) for o in (1, 2, 3)]
    for peer in peers:
        pl.semaphore_signal(barrier, inc=1, device_id=device(*peer), device_id_type=MESH)

    for b in range(4):
        code = encode(left[pl.ds(b * 128, 128), :].T, 1.0 / BOUND)
        for a in range(NC):
            for h in range(2):
                left_out[a, b, pl.ds(h * RC, RC), :] = code[h * 128 + a * RC : h * 128 + (a + 1) * RC]
    for px in range(4):
        for pc in range(2):
            for b in range(4):
                grad_out[px, pc, :, pl.ds(b * 128, 128)] = grad[:, pl.ds(pc * 2048 + b * 512 + px * 128, 128)]

    pl.semaphore_wait(barrier, len(peers))

    for a in range(NC):
        for o in (2, 1, 3):
            send("lz", a, left_out.at[a, turn(z, o)], left_mid.at[a, z], (x, y, turn(z, o), core))
        left_mid[a, z] = left_out[a, z]
    own_rows = pl.ds(pl.multiple_of(y * 256 + x * 64 + core * 32, 32), 32)
    for o in (2, 1, 3, 0):
        for oc, pc in both_cores(o):
            px = turn(x, o)
            send("g1", 0, grad_out.at[px, pc], grad_in.at[own_rows], (px, y, z, pc))
    grad_in[own_rows] = grad_out[x, core]
    def ring_start(name, half):
        for up, h, part in ((1, 0, 0), (3, 1, 1), (1, 1, 2), (3, 0, 2)):
            send(name, part, half(y, h), half(y, h), (x, turn(y, up), z, core))

    def ring_pass(name, half):
        for from_, h, to in ((3, 0, 1), (1, 1, 3)):
            piece = half(turn(y, from_), h)
            arrive(name, h, piece)
            send(name, 2, piece, piece, (x, turn(y, to), z, core))

    def grad_half(py, h):
        return grad_in.at[pl.ds(pl.multiple_of(py * 256 + h * 128, 128), 128)]

    def right_half(py, h):
        return right_in.at[py, core, pl.ds(h * 2, 2)]

    def left_turn(a):
        arrive("lz", a, left_mid.at[a, pl.ds(0, 3)])
        for o in (2, 1, 3):
            to = turn(y, o)
            send("ly", a, left_mid.at[a, to], left_in.at[a, x, core, y], (x, to, z, core))
        left_in[a, x, core, y] = left_mid[a, y]

    def left_spread(a):
        piece = left_in.at[a, x, core]
        arrive("ly", a, piece.at[pl.ds(0, 3)])
        for o in (2, 1, 3):
            send("lg", a, piece, piece, (turn(x, o), y, z, core))
        send("lc", a, piece, piece, (x, y, z, other))

    def left_forward(a):
        arrive("lg", a, left_in.at[a, pl.ds(0, 3), core])
        for o in (1, 3, 2):
            piece = left_in.at[a, turn(x, 4 - o), core]
            send("lc", a, piece, piece, (x, y, z, other))

    def left_take(a):
        def one(px, carry, pc):
            for ry in range(4):
                hi, lo = halves(decode(left_in[a, px, pc, ry], BOUND))
                at = pl.ds(pl.multiple_of(ry * 256 + (px // 2) * 128, 128), 128)
                for h in range(2):
                    rows = (pc * 2 + h) * RC
                    lt[a, px % 2, pl.ds(pl.multiple_of(rows, RC), RC), at] = hi[h * RC : (h + 1) * RC]
                    lt[a, px % 2, pl.ds(pl.multiple_of(4 * RC + rows, RC), RC), at] = lo[h * RC : (h + 1) * RC]
            return carry

        lax.fori_loop(0, 4, functools.partial(one, pc=core), 0)
        arrive("lc", a, left_in.at[a, :, other])
        lax.fori_loop(0, 4, functools.partial(one, pc=other), 0)

    def flip(a):
        def one(s, carry):
            at = pl.ds(pl.multiple_of(s * 128, 128), 128)
            for pc in range(2):
                for part in range(2):
                    for sub in range(4 * RC // 128):
                        v = lt[a, pc, pl.ds(part * 4 * RC + sub * 128, 128), at].T
                        to = pl.ds(pl.multiple_of(part * 256 + (s % 2) * 128, 128), 128)
                        lf[a, s // 2, to, pl.ds(pc * 4 * RC + sub * 128, 128)] = v
            return carry

        lax.fori_loop(0, 8, one, 0)

    left_turn(0)
    for q in range(4):
        for b in range(2):
            right_out[q, pl.ds(b * 128, 128), :] = encode(
                right[pl.ds(q * 128, 128), pl.ds(b * 128, 128)], 1.0 / BOUND
            )
    right_in[y, core, x] = right_out[x]
    if GRAD_FIRST:
        arrive("g1", 0, grad_in.at[pl.ds(0, 224)])
        ring_start("g2", grad_half)
    for a in range(1, NC):
        left_turn(a)
    if not GRAD_FIRST:
        arrive("g1", 0, grad_in.at[pl.ds(0, 224)])
        ring_start("g2", grad_half)
    for o in (2, 1, 3):
        px = turn(x, o)
        send("r1", 0, right_out.at[px], right_in.at[y, core, x], (px, y, z, core))
    left_spread(0)
    left_spread(1)
    ring_pass("g2", grad_half)
    arrive("r1", 0, right_in.at[0, 0, pl.ds(0, 3)])
    if not RIGHT_LATE:
        ring_start("rg", right_half)
    send("rc", 0, right_in.at[y, core], right_in.at[y, core], (x, y, z, other))
    left_forward(0)
    left_spread(2)
    left_take(0)
    if RIGHT_LATE:
        ring_start("rg", right_half)
    left_forward(1)
    left_spread(3)
    arrive("g2", 2, grad_in.at[pl.ds(0, 512)])

    def turned(a):
        for oc, pc in ((1, other), (0, core)):
            both = dot(lt[a, pc], grad_in[...])
            h_block[...] = both[0 : 4 * RC] + both[4 * RC : 8 * RC]
            for o in (2, 1, 3, 0):
                pz = turn(z, o)
                rows = pl.ds(pl.multiple_of(pz * RC, RC), RC)
                here = h_in.at[a, z * 2 + core]
                message = h_out.at[a, o, oc] if o or oc else here
                pack(lambda b, rows=rows: h_block[rows, pl.ds(b * 128, 128)], message, RC, 4)
                if o or oc:
                    send("h1", a, message, here, (x, y, pz, pc))

    def turned_sum(a):
        arrive("h1", a, h_in.at[a, pl.ds(0, 7)])

        def one(b, carry):
            for pc in range(2):
                v = None
                for pz in range(4):
                    start = pl.multiple_of(b * RC, RC)
                    term = unpack_rows(h_in.at[a, pz * 2 + pc], start, RC, 4 * RC)
                    v = term if v is None else v + term
                h_part[:, pl.ds(pl.multiple_of(pc * 512 + b * 128, 128), 128)] = v
            return carry

        lax.fori_loop(0, 4, one, 0)
        message = h_gather.at[a, z]
        pack(lambda b: h_part[:, pl.ds(b * 128, 128)], message, RC, 8)
        for o in (2, 1, 3):
            send("h2", a, message, message, (x, y, turn(z, o), core))

    def rotate(a):
        arrive("h2", a, h_gather.at[a, pl.ds(0, 3)])

        def one(pz, carry):
            for b in range(8):
                hi, lo = halves(unpack(h_gather.at[a, pz], b, RC, 8))
                h_parts[pl.ds(pl.multiple_of(pz * RC, RC), RC), pl.ds(b * 128, 128)] = hi
                h_parts[pl.ds(pl.multiple_of((4 + pz) * RC, RC), RC), pl.ds(b * 128, 128)] = lo
            return carry

        lax.fori_loop(0, 4, one, 0)
        for i in range(2):
            at = pl.ds(i * 512, 512)
            both = dot(h_parts[...], right_hi[:, at])
            low = dot(h_parts[pl.ds(0, 4 * RC), :], right_lo[:, at])
            rot_block[:, at] = both[0 : 4 * RC] + both[4 * RC : 8 * RC] + low
        for i in (1, 2, 3, 0):
            jd = turn(xl * 2 + core, i)
            pack(
                lambda b, jd=jd: rot_block[:, pl.ds(pl.multiple_of(jd * 256 + b * 128, 128), 128)],
                rot_out.at[a, i], 4 * RC, 2,
            )
            target = (core * 2 + jd // 2, y, z, jd % 2)
            args = ("p", a, rot_out.at[a, i], rot_in.at[a, x], target)
            if i:
                send(*args)
            else:
                send_unless(xh == core, *args)

    def moments(a):
        if a == 0:
            for load in loads:
                load.wait()
        arrive("p", a, rot_in.at[a])

        def one(pz, carry):
            rows = pl.ds(pl.multiple_of(pz * 128 + a * RC, RC), RC)
            part = pl.ds(pl.multiple_of(pz * RC, RC), RC)
            for b in range(2):
                rot = None
                for px in range(4):
                    start = pl.multiple_of((b * 4 + pz) * RC, RC)
                    term = unpack_rows(rot_in.at[a, px], start, RC, 8 * RC)
                    rot = term if rot is None else rot + term
                at = pl.ds(b * 128, 128)
                moved_first = 0.9 * first[rows, at] + 0.1 * rot
                moved_second = 0.95 * second[rows, at] + 0.05 * rot * rot
                new_first[rows, at] = moved_first
                new_second[rows, at] = moved_second
                d_block[part, at] = (
                    moved_first / (1.0 - 0.9**STEP) / (jnp.sqrt(moved_second / (1.0 - 0.95**STEP)) + 1e-08)
                )
            return carry

        lax.fori_loop(0, 4, one, 0)
        pack(lambda b: d_block[:, pl.ds(b * 128, 128)], d_out.at[a], 4 * RC, 2)
        if a == NC - 1:
            for i, (src, dst) in enumerate(((new_first, first_out), (new_second, second_out))):
                store = pltpu.make_async_copy(src, dst, ls.at[2 + i])
                store.start()
                pending.append(store.wait)
        slot = xl * 2 + core
        for i in (2, 1, 3, 0):
            args = ("d", a, d_out.at[a], d_in.at[a, slot], (turn(x, i), y, z, xh))
            if i:
                send(*args)
            else:
                send_unless(xh == core, *args)

    def back(a):
        arrive("d", a, d_in.at[a])
        for j in range(4):
            for b in range(2):
                hi, lo = halves(unpack(d_in.at[a, j], b, 4 * RC, 2))
                at = pl.ds(j * 256 + b * 128, 128)
                d_parts[pl.ds(0, 4 * RC), at] = hi
                d_parts[pl.ds(4 * RC, 4 * RC), at] = lo

        both = dot_t(d_parts[...], right_hi[...])
        low = dot_t(d_parts[pl.ds(0, 4 * RC), :], right_lo[...])
        y_block[...] = both[0 : 4 * RC] + both[4 * RC : 8 * RC] + low
        for o in (2, 1, 3, 0):
            pz = turn(z, o)
            rows = pl.ds(pl.multiple_of(pz * RC, RC), RC)
            message = y_out.at[a, o] if o else y_in.at[a, z]
            pack(lambda b, rows=rows: y_block[rows, pl.ds(b * 128, 128)], message, RC, 8)
            if o:
                send("y1", a, message, y_in.at[a, z], (x, y, pz, core))

    def back_sum(a):
        arrive("y1", a, y_in.at[a, pl.ds(0, 3)])

        def one(b, carry):
            v = None
            for pz in range(4):
                term = unpack_rows(y_in.at[a, pz], pl.multiple_of(b * RC, RC), RC, 8 * RC)
                v = term if v is None else v + term
            y_sum[:, pl.ds(pl.multiple_of(b * 128, 128), 128)] = v
            return carry

        lax.fori_loop(0, 8, one, 0)
        for oc, pc in ((1, other), (0, core)):
            here = y_gather.at[a, core * 4 + z]
            message = y_gather_out.at[a] if oc else here
            pack(
                lambda b, pc=pc: y_sum[:, pl.ds(pl.multiple_of(pc * 512 + b * 128, 128), 128)], message, RC, 4
            )
            for o in (2, 1, 3, 0):
                if o or oc:
                    send("y2", a, message, here, (x, y, turn(z, o), pc))

    def raised_take(a):
        arrive("y2", a, y_gather.at[a, pl.ds(0, 7)])

        def one(i, carry):
            rows = pl.ds(pl.multiple_of(i * RC, RC), RC)
            for b in range(4):
                hi, lo = halves(unpack(y_gather.at[a, i], b, RC, 4))
                y_hi[rows, pl.ds(b * 128, 128)] = hi
                y_lo[rows, pl.ds(b * 128, 128)] = lo
            return carry

        lax.fori_loop(0, 8, one, 0)

    def raised(a, py):
        both = dot(lf[a, py], y_hi[...])
        v = both[0:256] + both[256:512] + dot(lf[a, py, pl.ds(0, 256), :], y_lo[...])
        u_acc[py] = u_acc[py] + v if a else v

    def right_piece(py, pc):
        def one(px, carry):
            for b in range(2):
                hi, lo = halves(decode(right_in[py, pc, px, pl.ds(b * 128, 128), :], BOUND))
                rows = pl.ds(pl.multiple_of(py * 256 + (px // 2) * 128, 128), 128)
                at = pl.ds(pl.multiple_of((px % 2) * 512 + pc * 256 + b * 128, 128), 128)
                right_hi[rows, at] = hi
                right_lo[rows, at] = lo
            return carry

        lax.fori_loop(0, 4, one, 0)

    def basis_take(part):
        if part == 0:
            arrive("rg", 2, right_in.at[pl.ds(0, 2), core])
            for o in (1, 3, 2):
                piece = right_in.at[turn(y, 4 - o), core]
                send("rc", 0, piece, piece, (x, y, z, other))
            for o in (0, 1, 3, 2):
                right_piece(turn(y, 4 - o), core)
        else:
            arrive("rc", 0, right_in.at[:, other])
            for o in (0, 1, 3, 2):
                right_piece(turn(y, 4 - o), other)

    def raise_all(a):
        raised_take(a)

        def one(py, carry):
            raised(a, py)
            return carry

        lax.fori_loop(0, 4, one, 0)

    steps = {
        "turned": turned, "pass": lambda a: ring_pass("rg", right_half), "forward": left_forward, "take": left_take,
        "turned_sum": turned_sum, "basis": basis_take, "rotate": rotate, "moments": moments, "flip": flip,
        "back": back, "back_sum": back_sum, "raise": raise_all,
    }
    for name in ORDER:
        steps[name[:-1]](int(name[-1]))

    raised_take(NC - 1)
    def rows_of(py, h, c, b):
        return u_acc[py, pl.ds(h * 128, 128), pl.ds((c * CB + b) * 128, 128)]

    def to_neighbour(name, c, h, up, py, message, dst):
        pack(lambda b: rows_of(py, h, c, b), message, 128, CB)
        send(name, c, message, dst, (x, turn(y, up), z, core))

    raised(NC - 1, turn(y, 2))
    for c in range(CC):
        for h, up in ((0, 1), (1, 3)):
            to_neighbour("uf", c, h, up, turn(y, 2), u_far_out.at[c, h], u_far_in.at[c, h])
    raised(NC - 1, turn(y, 1))
    raised(NC - 1, turn(y, 3))
    for c in range(CC):
        for h, up, slot in ((1, 1, 0), (0, 3, 1)):
            to_neighbour("u1", c, h, up, turn(y, up), u_out.at[c, slot, h], u_in.at[c, slot, h])
    for c in range(CC):
        arrive("uf", c, u_far_in.at[c])
        for h, up, slot in ((0, 1, 0), (1, 3, 1)):
            py = turn(y, up)
            for b in range(CB):
                at = pl.ds((c * CB + b) * 128, 128)
                u_acc[py, pl.ds(h * 128, 128), at] += unpack(u_far_in.at[c, h], b, 128, CB)
            to_neighbour("u1", c, h, up, py, u_out.at[c, slot, h], u_in.at[c, slot, h])
    raised(NC - 1, y)
    for c in range(CC):
        arrive("u1", c, u_in.at[c])
        for b in range(CB):
            for h in range(2):
                v = rows_of(y, h, c, b)
                for slot in range(2):
                    v = v + unpack(u_in.at[c, slot, h], b, 128, CB)
                u_sum[pl.ds(h * 128, 128), pl.ds(b * 128, 128)] = v
        here = u_last_in.at[c, x * 2 + core]
        for px in range(4):
            for pc in range(2):
                rows = pl.ds(px * 64 + pc * 32, 32)
                pack(lambda b, rows=rows: u_sum[rows, pl.ds(b * 128, 128)], u_last_out.at[c, px, pc], 32, CB)
        for o in (2, 1, 3, 0):
            for oc, pc in both_cores(o):
                px = turn(x, o)
                send("u2", c, u_last_out.at[c, px, pc], here, (px, y, z, pc))
        own = pltpu.make_async_copy(u_last_out.at[c, x, core], here, ls.at[4 + c])
        own.start()
        pending.append(own.wait)

    sent("lz", left_mid.at[:, pl.ds(0, 3)])
    sent("ly", left_in.at[:, 0, 0, pl.ds(0, 3)])
    sent("lg", left_in.at[:, pl.ds(0, 3), 0])
    sent("lc", left_in.at[:, :, 0])
    sent("g1", grad_in.at[pl.ds(0, 224)])
    sent("g2", grad_in.at[pl.ds(0, 768)])
    sent("r1", right_in.at[0, 0, pl.ds(0, 3)])
    sent("rg", right_in.at[pl.ds(0, 3), 0])
    sent("rc", right_in.at[:, 0])
    sent("h1", h_in.at[:, pl.ds(0, 7)])
    sent("h2", h_gather.at[:, pl.ds(0, 3)])
    for name, like in (("p", rot_in), ("d", d_in)):
        pl.when(xh == core)(lambda name=name, like=like: sent(name, like.at[:, pl.ds(0, 3)]))
        pl.when(xh != core)(lambda name=name, like=like: sent(name, like))
    sent("y1", y_in.at[:, pl.ds(0, 3)])
    sent("y2", y_gather.at[:, pl.ds(0, 7)])
    sent("uf", u_far_in)
    sent("u1", u_in)
    for c in range(CC):
        arrive("u2", c, u_last_in.at[c, pl.ds(0, 7)])
    sent("u2", u_last_in.at[:, pl.ds(0, 7)])
    for wait in pending:
        wait()


def finish(coded, first, second, update, new_first, new_second):
    new_first[...] = first[...]
    new_second[...] = second[...]
    for c in range(CC):
        for px in range(4):
            for pc in range(2):
                for b in range(CB):
                    at = pl.ds(pc * 2048 + (c * CB + b) * 512 + px * 128, 128)
                    update[:, at] = unpack(coded.at[c, px * 2 + pc], b, 32, CB)


SEMAPHORES = (
    ("lz", NC), ("ly", NC), ("lg", NC), ("lc", NC), ("g1", 1), ("g2", 3), ("r1", 1), ("rg", 3), ("rc", 1),
    ("h1", NC), ("h2", NC), ("p", NC), ("d", NC), ("y1", NC), ("y2", NC), ("uf", CC), ("u1", CC), ("u2", CC),
)


def body(grad, left_basis, right_basis, first_moment, second_moment):
    vm = pltpu.VMEM
    count = sum(n for _, n in SEMAPHORES)
    scratch = [
        vm((NC, 4, 2 * RC, 128), BF16),
        vm((NC, 4, 2 * RC, 128), BF16),
        vm((NC, 4, 2, 4, 2 * RC, 128), BF16),
        vm((NC, 2, 8 * RC, 1024), BF16),
        vm((NC, 4, 512, 8 * RC), BF16),
        vm((4, 2, 32, 512), BF16),
        vm((1024, 512), BF16),
        vm((4, 256, 128), BF16),
        vm((4, 2, 4, 256, 128), BF16),
        vm((1024, 1024), BF16),
        vm((1024, 1024), BF16),
        vm((NC, 4, 2, 4 * RC + 16, 128), BF16),
        vm((NC, 8, 4 * RC + 16, 128), BF16),
        vm((NC, 4, 8 * RC + 16, 128), BF16),
        vm((RC, 1024), F32),
        vm((4 * RC, 512), F32),
        vm((8 * RC, 1024), BF16),
        vm((4 * RC, 1024), F32),
        vm((NC, 4, 8 * RC + 16, 128), BF16),
        vm((NC, 4, 8 * RC + 16, 128), BF16),
        vm((4 * RC, 256), F32),
        vm((NC, 8 * RC + 16, 128), BF16),
        vm((NC, 4, 8 * RC + 16, 128), BF16),
        vm((8 * RC, 1024), BF16),
        vm((4 * RC, 1024), F32),
        vm((RC, 1024), F32),
        vm((NC, 4, 8 * RC + 16, 128), BF16),
        vm((NC, 4, 8 * RC + 16, 128), BF16),
        vm((NC, 4 * RC + 16, 128), BF16),
        vm((NC, 8, 4 * RC + 16, 128), BF16),
        vm((8 * RC, 512), BF16),
        vm((8 * RC, 512), BF16),
        vm((4, 256, 512), F32),
        vm((256, 128 * CB), F32),
        vm((CC, 2, 128 * CB + 16, 128), BF16),
        vm((CC, 2, 128 * CB + 16, 128), BF16),
        vm((CC, 2, 2, 128 * CB + 16, 128), BF16),
        vm((CC, 2, 2, 128 * CB + 16, 128), BF16),
        vm((CC, 4, 2, 32 * CB + 16, 128), BF16),
        vm((512, 256), F32),
        vm((512, 256), F32),
        vm((512, 256), F32),
        vm((512, 256), F32),
        pltpu.SemaphoreType.DMA((len(SEMAPHORES),)),
        pltpu.SemaphoreType.DMA((count,)),
        pltpu.SemaphoreType.DMA((4 + CC,)),
    ]
    whole = pl.BlockSpec(memory_space=pltpu.VMEM)
    there = pl.BlockSpec(memory_space=pl.ANY)
    square = jax.ShapeDtypeStruct((512, 256), F32)
    coded, new_first, new_second = pl.pallas_call(
        kernel,
        out_shape=(jax.ShapeDtypeStruct((CC, 8, 32 * CB + 16, 128), BF16), square, square),
        in_specs=[whole, whole, whole, there, there],
        out_specs=(there,) * 3,
        scratch_shapes=scratch,
        compiler_params=pltpu.CompilerParams(
            collective_id=0, has_side_effects=True, vmem_limit_bytes=56 * 2**20
        ),
    )(grad, left_basis, right_basis, first_moment, second_moment)
    return pl.pallas_call(
        finish,
        out_shape=(jax.ShapeDtypeStruct((32, 4096), F32), square, square),
        in_specs=[whole] * 3,
        out_specs=(whole,) * 3,
    )(coded, new_first, new_second)


def solution(mesh):
    placed = (
        P(("dp", "tensor"), None),
        P("dp", "tensor"),
        P("dp", "tensor"),
        P("dp", "tensor"),
        P("dp", "tensor"),
    )
    return jax.shard_map(
        body,
        mesh=mesh,
        in_specs=placed,
        out_specs=(P(("dp", "tensor"), None), P("dp", "tensor"), P("dp", "tensor")),
        check_vma=False,
    )
```
